256 devices in a mesh: dp: 4 (over x), ctx: 16 (over z, core), exp: 4 (over y).
Axes of the slice: x: 4, y: 4, z: 8, core: 2. Of those that a mesh axis runs over, the one named last changes fastest.
Arguments:
- queries: bfloat16 [4, 8192, 1024], P('dp', 'ctx', 'exp'), may hold values from -6 to 6
- key_rows: bfloat16 [4, 8192, 1024], P('dp', 'ctx', 'exp'), may hold values from -6 to 6
- value_rows: bfloat16 [4, 8192, 1024], P('dp', 'ctx', 'exp'), may hold values from -6 to 6
- segments: int32 [4, 8192], P('dp', 'ctx'), may hold values from 0 to 7, never falling along the last dimension, each value on 1 to 2048 neighbouring positions
- left_blocks: int32 [4, 128, 3], P('dp', 'ctx'), may hold values from -1 to 126, as said below
- moe_input: bfloat16 [4, 8192, 1024], P('dp', ('ctx', 'exp')), may hold values from -6 to 6
- out_grad: bfloat16 [4, 8192, 1024], P('dp', ('ctx', 'exp')), may hold values from -6 to 6
- expert_ids: int32 [4, 8192, 2], P('dp', ('ctx', 'exp')), may hold values from 0 to 63, all different within a row; in each aligned block of 128 rows (0 to 127, 128 to 255, ..., all dimensions but the last counted through in order) at most 8 rows name the same one
- gate_weights: bfloat16 [4, 8192, 2], P('dp', ('ctx', 'exp')), may hold values from 0.19921875 to 1
- expert_in: bfloat16 [64, 1024, 1024], P(('ctx', 'exp')), may hold values from -0.1875 to 0.1875
- expert_out: bfloat16 [64, 1024, 1024], P(('ctx', 'exp')), may hold values from -0.1875 to 0.1875
Outputs:
- d_queries: bfloat16 [4, 8192, 1024], P('dp', 'ctx', 'exp')
- d_keys: bfloat16 [4, 8192, 1024], P('dp', 'ctx', 'exp')
- d_values: bfloat16 [4, 8192, 1024], P('dp', 'ctx', 'exp')
- d_residual: bfloat16 [4, 8192, 1024], P('dp', ('ctx', 'exp'))
- d_gates: bfloat16 [4, 8192, 2], P('dp', ('ctx', 'exp'))
- d_expert_in: bfloat16 [64, 1024, 1024], P(('ctx', 'exp'))
- d_expert_out: bfloat16 [64, 1024, 1024], P(('ctx', 'exp'))
The draws below stay inside these ranges and needn't reach their ends.
Inputs may be any that keep to these rules, and one draw needn't show every extreme that they name: `left_blocks`: entries of group c (counted from 0 in its batch) are -1 or distinct groups from c - 8 to c - 1; every odd group c of 8 or more lists group c - 8. `expert_ids`: in the 128 rows of one device no expert is named by more than 8 rows, and in some aligned block one expert is named by exactly 8.
All inputs are finite; a program needn't handle non-finite values.
Results may differ from the reference program's by a relative error of at most 0.013.
Values may be sent and summed in bfloat16 or wider, within the bound.
A program may use at most 128 MiB of HBM per device.

```python
import math
import jax
import jax.numpy as jnp
import numpy as np
from jax import lax

D = 1024
H = 16
DH = 64
F = 1024
CH = 64
LB = 3
NB = 4
S = 8192
NCHUNK = 128
CPD = 8
ROWS = 128
EXPERTS = 64
CAP = 8
SEQS = 8
SEQ_MOST = 2048


def draw_queries(key, part):
    key = jax.random.fold_in(key, 3)
    drawn = jnp.clip(jax.random.normal(key, (NB, S, D), jnp.float32), -4.0, 4.0)
    return drawn.astype(jnp.bfloat16)


def draw_key_rows(key, part):
    key = jax.random.fold_in(key, 5)
    drawn = jnp.clip(jax.random.normal(key, (NB, S, D), jnp.float32), -4.0, 4.0)
    return drawn.astype(jnp.bfloat16)


def draw_left_blocks(key, part):
    key = jax.random.fold_in(key, 7)
    offsets = jnp.arange(CPD, dtype=jnp.int32)
    group_ids = jnp.arange(NCHUNK, dtype=jnp.int32)[None, :, None]
    ranking = jax.random.randint(key, (NB, NCHUNK, CPD), 0, 1 << 20) * CPD + offsets
    farthest = (group_ids % 2 == 1) & (offsets == CPD - 1)
    ranking = jnp.where(farthest, 1 << 30, ranking)
    order = jnp.argsort(-ranking, axis=-1)[..., :LB].astype(jnp.int32)
    target = group_ids - (order + 1)
    dropped = (jax.random.randint(jax.random.fold_in(key, 1), (NB, NCHUNK, LB), 0, 4) == 0) & (order + 1 < CPD)
    return jnp.where((target >= 0) & jnp.logical_not(dropped), target, -1).astype(jnp.int32)


def levels(stream_key, shape, pieces, low, high):
    gain, own = 1.0, jax.random.fold_in(stream_key, 6)
    for dim, parts in pieces:
        draws = jnp.exp(jax.random.uniform(jax.random.fold_in(own, dim), (parts,), jnp.float32, low / len(pieces), high / len(pieces)))
        gain = gain * jnp.repeat(draws, shape[dim] // parts).reshape([-1 if axis == dim else 1 for axis in range(len(shape))])
    return gain


def length_profile(amount, total, bound, skew):
    weights = [(1 << 20) // math.isqrt(standing ** skew) + 1 for standing in range(2, amount + 1)]
    surplus, counts = total - bound - (amount - 1), [1] * (amount - 1)
    while surplus > 0:
        free = [i for i in range(amount - 1) if counts[i] < bound]
        pool, remaining = sum([weights[i] for i in free]), surplus
        for i in free:
            more = min(bound - counts[i], max(1, remaining * weights[i] // pool), surplus)
            counts[i] = counts[i] + more
            surplus = surplus - more
    return np.array([bound] + counts)


def ragged(key, amount, total, most, lean):
    if amount == 2:
        one = jax.random.randint(key, (), max(1, total - most), min(most, total - 1) + 1)
        return jnp.stack([one, total - one])
    sizes = jnp.asarray(length_profile(amount, total, most, lean), jnp.int32)
    pairs = (amount - 1) // 2
    giver, receiver = sizes[1:1 + 2 * pairs:2], sizes[2:2 + 2 * pairs:2]
    slack = jnp.minimum(giver - 1, most - receiver)
    moved = jax.random.randint(jax.random.fold_in(key, 1), (pairs,), 0, 1 << 20) % (slack + 1)
    sizes = sizes.at[1:1 + 2 * pairs:2].set(giver - moved).at[2:2 + 2 * pairs:2].set(receiver + moved)
    return sizes[jax.random.permutation(jax.random.fold_in(key, 2), amount)]


def assign_block(rng, own, number, rows, count, top, reach, skew):
    order = jax.random.permutation(rng, count)
    heavy_load, common = portions_of(count, rows * top, reach, skew, True), portions_of(count, rows * top, reach, skew, False)
    places = jnp.arange(count)

    def named(sizes, turn):
        used = int((sizes > 0).sum())
        fixed = max(1, used // 4)
        passed = fixed + (places - fixed + turn * (used - fixed)) % max(1, count - fixed)
        return jnp.zeros((count,), jnp.int32).at[order[jnp.where(places < fixed, places, passed)]].set(jnp.asarray(sizes, jnp.int32))

    sizes = jnp.where(number % 4 == 0, named(heavy_load, number // 4), named(common, number - number // 4 - 1))
    mixed = jax.random.permutation(jax.random.fold_in(own, 3), count)
    giver, receiver = mixed[0:count // 2 * 2:2], mixed[1:count // 2 * 2:2]
    slack = jnp.minimum(sizes[giver] - 1, reach - sizes[receiver]) // 2
    slack = jnp.where((giver == order[0]) | (receiver == order[0]) | (sizes[receiver] == 0), 0, jnp.maximum(slack, 0))
    passed = jax.random.randint(jax.random.fold_in(own, 4), (count // 2,), 0, 1 << 20) % (slack + 1)
    sizes = sizes.at[giver].add(-passed).at[receiver].add(passed)
    labels = jnp.searchsorted(jnp.cumsum(sizes), jnp.arange(rows * top), side="right").astype(jnp.int32)
    grid = labels.reshape(top, rows).T
    grid = grid[jax.random.permutation(jax.random.fold_in(own, 1), rows)]
    turn = jax.random.randint(jax.random.fold_in(own, 2), (rows, 1), 0, top)
    return jnp.take_along_axis(grid, (jnp.arange(top)[None, :] + turn) % top, axis=1)


def portions_of(amount, total, reach, slope, full):
    loads = [(1 << 20) // math.isqrt(rank ** slope) + 1 for rank in range(1, amount + 1)]
    largest = reach if full else min(reach, max(-(-total // amount), total * loads[0] // sum(loads)))
    least = 1 if total - largest >= amount - 1 else 0
    given, spare = [largest] + [least] * (amount - 1), total - largest - least * (amount - 1)
    while spare > 0:
        movable = [i for i in range(1, amount) if given[i] < largest] or [i for i in range(1, amount) if given[i] < reach]
        mass, left = sum([loads[i] for i in movable]), spare
        for i in movable:
            extra = min(reach - given[i], max(1, left * loads[i] // mass), spare)
            given[i] = given[i] + extra
            spare = spare - extra
    return np.array(given)


def scatter_about(rng, shape, scale, most, shards=(), kind=jnp.bfloat16):
    result = jax.random.normal(rng, shape, jnp.float32) * scale
    if len(shards) > 0:
        result = levels(rng, shape, shards, -0.22, 0.18) * result
    return jnp.clip(result, min=-most, max=most).astype(kind)


def setup_inputs(seed: int = 0) -> dict:
    streams_of = jax.random.split(jax.random.key(seed), 12)
    queries = draw_queries(jax.random.fold_in(streams_of[11], 71), 0)
    key_rows = draw_key_rows(jax.random.fold_in(streams_of[11], 71), 0)
    value_rows = scatter_about(streams_of[2], (NB, S, D), 1.0, 6.0, ((0, 4), (1, 16), (2, 4)))
    segments = jax.vmap(lambda own: jnp.searchsorted(jnp.cumsum(ragged(own, SEQS, S, SEQ_MOST, 1)), jnp.arange(S), side="right"))(jax.random.split(streams_of[3], NB)).reshape((NB, S)).astype(jnp.int32)
    left_blocks = draw_left_blocks(jax.random.fold_in(streams_of[11], 71), 0)
    moe_input = scatter_about(streams_of[5], (NB, S, D), 1.0, 6.0, ((0, 4), (1, 64)))
    out_grad = scatter_about(streams_of[6], (NB, S, D), 1.0, 6.0, ((0, 4), (1, 64)))
    expert_ids_keys = jax.random.split(jax.random.fold_in(streams_of[7], 1), NB * S // ROWS)
    expert_ids_turns = jax.random.permutation(jax.random.fold_in(streams_of[7], 3), NB * S // ROWS)
    expert_ids = jax.vmap(lambda own, number: assign_block(jax.random.fold_in(streams_of[7], 2), own, number, ROWS, EXPERTS, 2, CAP, 2))(expert_ids_keys, expert_ids_turns).reshape((NB, S, 2))
    gate_weights = jnp.clip(0.19921875 + 0.80078125 * jax.random.uniform(streams_of[8], (NB, S, 2), jnp.float32) ** levels(streams_of[8], (NB, S, 2), ((0, 4), (1, 64)), -0.2, 0.2), 0.19921875, 1.0).astype(jnp.bfloat16)
    expert_in = scatter_about(streams_of[9], (EXPERTS, D, F), D ** -0.5, 0.1875, ((0, 64),))
    expert_out = scatter_about(streams_of[10], (EXPERTS, F, D), F ** -0.5, 0.1875, ((0, 64),))
    return dict(queries=queries, key_rows=key_rows, value_rows=value_rows, segments=segments, left_blocks=left_blocks, moe_input=moe_input, out_grad=out_grad, expert_ids=expert_ids, gate_weights=gate_weights, expert_in=expert_in, expert_out=expert_out)


masked_score = -1.0e30


def expert_backward(inputs):
    weight_in, weight_out, rows_in, rows_grad, gate_rows = inputs
    pre = jnp.dot(rows_in, weight_in, preferred_element_type=jnp.float32)
    sigma = jax.nn.sigmoid(pre)
    active = (pre * sigma).astype(jnp.bfloat16)
    produced = jnp.dot(active, weight_out, preferred_element_type=jnp.float32)
    gate_grad = jnp.sum(produced * rows_grad.astype(jnp.float32), axis=1).astype(jnp.bfloat16)
    scaled = (gate_rows.astype(jnp.float32)[:, None] * rows_grad.astype(jnp.float32)).astype(jnp.bfloat16)
    grad_out = lax.dot_general(active, scaled, (((0,), (0,)), ((), ())), preferred_element_type=jnp.float32)
    grad_active = lax.dot_general(scaled, weight_out, (((1,), (1,)), ((), ())), preferred_element_type=jnp.float32)
    grad_pre = (grad_active * sigma * (1.0 + pre * (1.0 - sigma))).astype(jnp.bfloat16)
    grad_in = lax.dot_general(rows_in, grad_pre, (((0,), (0,)), ((), ())), preferred_element_type=jnp.float32)
    back = lax.dot_general(grad_pre, weight_in, (((1,), (1,)), ((), ())), preferred_element_type=jnp.float32).astype(jnp.bfloat16)
    return grad_in, grad_out, back, gate_grad


def positions(expert_ids):
    flat_routes = expert_ids.reshape(EXPERTS, 2 * ROWS).astype(jnp.int32)
    onehot = (flat_routes[:, :, None] == jnp.arange(EXPERTS, dtype=jnp.int32)).astype(jnp.int32)
    earlier = jnp.cumsum(onehot, axis=1) - onehot
    slot_index = jnp.sum(earlier * onehot, axis=2)
    block_index = jnp.arange(EXPERTS, dtype=jnp.int32)[:, None]
    return (flat_routes * (EXPERTS * CAP) + block_index * CAP + slot_index).reshape(-1).astype(jnp.int32)


def moe_backward(moe_input, out_grad, expert_ids, gate_weights, expert_in, expert_out):
    position = positions(expert_ids)
    source = jnp.full((EXPERTS * EXPERTS * CAP,), -1, jnp.int32).at[position].set(jnp.arange(2 * S, dtype=jnp.int32))
    filled = source >= 0
    chosen = jnp.where(filled, source, 0).astype(jnp.int32)
    zero_half = jnp.zeros((), jnp.bfloat16)
    rows_in = jnp.where(filled[:, None], moe_input[chosen // 2], zero_half).reshape(EXPERTS, EXPERTS * CAP, D)
    rows_grad = jnp.where(filled[:, None], out_grad[chosen // 2], zero_half).reshape(EXPERTS, EXPERTS * CAP, D)
    gate_rows = jnp.where(filled, gate_weights.reshape(-1)[chosen], zero_half).reshape(EXPERTS, EXPERTS * CAP)
    grad_in, grad_out, back, gate_grad = lax.map(expert_backward, (expert_in, expert_out, rows_in, rows_grad, gate_rows))
    back_rows = back.reshape(-1, D)[position].reshape(S, 2, D)
    d_residual = (out_grad.astype(jnp.float32) + jnp.sum(back_rows.astype(jnp.float32), axis=1)).astype(jnp.bfloat16)
    d_gates = gate_grad.reshape(-1)[position].reshape(S, 2)
    return d_residual, d_gates, grad_in.astype(jnp.bfloat16), grad_out.astype(jnp.bfloat16)


def attention_backward(queries, key_rows, value_rows, grad_rows, segments, blocks):
    score_scale = DH ** -0.5
    width = (1 + LB) * CH
    group_ids = jnp.arange(NCHUNK, dtype=jnp.int32)
    lists = jnp.concatenate([group_ids[:, None], blocks.astype(jnp.int32)], axis=1)
    present = lists >= 0
    safe_index = jnp.where(present, lists, 0).astype(jnp.int32)
    query_c = queries.reshape(NCHUNK, CH, H, DH)
    key_c = key_rows.reshape(NCHUNK, CH, H, DH)
    value_c = value_rows.reshape(NCHUNK, CH, H, DH)
    grad_c = grad_rows.reshape(NCHUNK, CH, H, DH)
    seg_c = segments.reshape(NCHUNK, CH)

    def one_group(totals, group):
        key_total, value_total = totals
        chosen = safe_index[group]
        key_blocks = key_c[chosen].reshape(width, H, DH).astype(jnp.float32)
        value_blocks = value_c[chosen].reshape(width, H, DH).astype(jnp.float32)
        query = query_c[group].astype(jnp.float32)
        grad_here = grad_c[group].astype(jnp.float32)
        seg_keys = seg_c[chosen].reshape(width)
        allowed = jnp.repeat(present[group], CH)[None, :] & (seg_c[group][:, None] == seg_keys[None, :])
        scores = jnp.einsum("qhd,khd->hqk", query, key_blocks) * score_scale
        scores = jnp.where(allowed[None], scores, masked_score)
        row_max = jnp.max(scores, axis=2, keepdims=True)
        log_total = row_max + jnp.log(jnp.sum(jnp.exp(scores - row_max), axis=2, keepdims=True))
        weights = jnp.exp(scores - log_total)
        probs = weights.astype(jnp.bfloat16).astype(jnp.float32)
        attended = jnp.einsum("hqk,khd->qhd", probs, value_blocks)
        delta = jnp.transpose(jnp.sum(grad_here * attended, axis=2), (1, 0))[:, :, None]
        grad_probs = jnp.einsum("qhd,khd->hqk", grad_here, value_blocks)
        dscore = (weights * (grad_probs - delta)).astype(jnp.bfloat16).astype(jnp.float32)
        grad_query = jnp.einsum("hqk,khd->qhd", dscore, key_blocks) * score_scale
        key_terms = jnp.einsum("hqk,qhd->khd", dscore, query) * score_scale
        value_terms = jnp.einsum("hqk,qhd->khd", probs, grad_here)
        key_total = key_total.at[chosen].add(key_terms.reshape(1 + LB, CH, H, DH))
        value_total = value_total.at[chosen].add(value_terms.reshape(1 + LB, CH, H, DH))
        return (key_total, value_total), grad_query.astype(jnp.bfloat16)

    zero_grid = jnp.zeros((NCHUNK, CH, H, DH), jnp.float32)
    (key_total, value_total), grad_query = lax.scan(one_group, (zero_grid, zero_grid), group_ids)
    return (grad_query.reshape(S, D), key_total.reshape(S, D).astype(jnp.bfloat16),
            value_total.reshape(S, D).astype(jnp.bfloat16))


def reference(queries, key_rows, value_rows, segments, left_blocks, moe_input, out_grad, expert_ids, gate_weights, expert_in, expert_out):
    def one_batch(inputs):
        query_b, key_b, value_b, segment_b, block_b, input_b, grad_b, route_b, gate_b = inputs
        d_residual, d_gates, grad_in, grad_out = moe_backward(input_b, grad_b, route_b, gate_b, expert_in, expert_out)
        d_queries, d_keys, d_values = attention_backward(query_b, key_b, value_b, d_residual, segment_b, block_b)
        return d_queries, d_keys, d_values, d_residual, d_gates, grad_in, grad_out

    results = lax.map(one_batch, (queries, key_rows, value_rows, segments, left_blocks, moe_input, out_grad, expert_ids, gate_weights))
    d_expert_in = jnp.sum(results[5].astype(jnp.float32), axis=0).astype(jnp.bfloat16)
    d_expert_out = jnp.sum(results[6].astype(jnp.float32), axis=0).astype(jnp.bfloat16)
    return (results[0], results[1], results[2], results[3], results[4], d_expert_in, d_expert_out)
```

```python
import functools

import jax
import jax.numpy as jnp
from jax import lax
from jax.experimental import pallas as pl
from jax.experimental.pallas import tpu as pltpu
from jax.sharding import PartitionSpec as P

MESH = pl.DeviceIdType.MESH
BF = jnp.bfloat16
F32 = jnp.float32
I32 = jnp.int32

DP, CTX, EXP = 4, 16, 4
PEERS = CTX * EXP
HALF = CTX // 2
CAP = 8
BLOCK = 2 * CAP
TOKENS = 128
WIDTH = 1024
PART = WIDTH // DP
CHUNKS = 4
PER_CHUNK = PEERS // CHUNKS
CHUNK_ROWS = PER_CHUNK * CAP
GROUP = 64
GROUPS = 8
FRAMES = 512
LOCAL = 256
QROWS = 128
WINDOW = FRAMES + QROWS
FAR = 32768.0
VMEM_BYTES = 50 * 1024 * 1024


def dot(a, b, ca, cb, precision=None):
    return lax.dot_general(
        a, b, (((ca,), (cb,)), ((), ())), preferred_element_type=F32, precision=precision
    )


def wait_bytes(ref, sem):
    pltpu.make_async_copy(ref, ref, sem).wait()


def hop(j):
    s = j // EXP
    return HALF + (2 * (s % 2) - 1) * (s // 2), j % EXP


def moe_kernel(
    x_ref,
    z_ref,
    ids_ref,
    gate_ref,
    win_hbm,
    wout_hbm,
    dres_ref,
    dgate_ref,
    quarter_ref,
    win,
    wout,
    send,
    recv,
    pick_lo,
    pick_hi,
    u_all,
    s_all,
    gp_all,
    act_all,
    bsend,
    brecv,
    hsend,
    hrecv,
    part,
    first,
    second,
    load_sem,
    send_sem,
    recv_sem,
    bsend_sem,
    brecv_sem,
    hsend_sem,
    hrecv_sem,
    dp_send,
    dp_recv,
):
    me_d, me_c, me_x = lax.axis_index("dp"), lax.axis_index("ctx"), lax.axis_index("exp")
    right, left = lax.rem(me_d + 1, DP), lax.rem(me_d + DP - 1, DP)
    load_in = pltpu.make_async_copy(win_hbm, win, load_sem.at[0])
    load_out = pltpu.make_async_copy(wout_hbm, wout, load_sem.at[1])
    load_in.start()
    load_out.start()

    def ahead(k, xo):
        return {"ctx": lax.rem(me_c + k, CTX), "exp": lax.rem(me_x + xo, EXP)}

    def behind(k, xo):
        return {"ctx": lax.rem(me_c - k + CTX, CTX), "exp": lax.rem(me_x - xo + EXP, EXP)}

    barrier = pltpu.get_barrier_semaphore()
    for j in range(1, EXP):
        pl.semaphore_signal(barrier, inc=1, device_id=ahead(0, j), device_id_type=MESH)

    @pl.loop(EXP, PEERS)
    def _(j):
        k, xo = hop(j)
        pl.semaphore_signal(barrier, inc=1, device_id=ahead(k, xo), device_id_type=MESH)

    for other in (left, right):
        pl.semaphore_signal(barrier, inc=1, device_id={"dp": other}, device_id_type=MESH)

    lane64 = lax.broadcasted_iota(I32, (TOKENS, PEERS), 1)
    lane_q = lax.broadcasted_iota(I32, (TOKENS, PEERS * BLOCK), 1)
    ids = ids_ref[...]

    def relative(column):
        k = (column // EXP - me_c + CTX) % CTX
        xo = (column % EXP - me_x + EXP) % EXP
        s = jnp.where(k == 0, 0, jnp.where(k < HALF, CTX - 2 * k, 2 * k - CTX + 1))
        return s * EXP + xo

    peer = [relative(ids[:, t : t + 1]) for t in range(2)]
    named = [(peer[t] == lane64).astype(F32) for t in range(2)]
    before = (
        lax.broadcasted_iota(I32, (TOKENS, TOKENS), 1)
        < lax.broadcasted_iota(I32, (TOKENS, TOKENS), 0)
    ).astype(BF)
    earlier = dot(before, (named[0] + named[1]).astype(BF), 1, 0)
    slot = [
        jnp.sum(named[t] * earlier, axis=1, keepdims=True).astype(I32) for t in range(2)
    ]
    row = [peer[t] * BLOCK + slot[t] for t in range(2)]
    hit_lo = [row[t] == lane_q for t in range(2)]
    hit_hi = [row[t] + CAP == lane_q for t in range(2)]
    pick_lo[...] = (hit_lo[0] | hit_lo[1]).astype(F32).astype(BF)
    pick_hi[...] = (hit_hi[0] | hit_hi[1]).astype(F32).astype(BF)
    gates = gate_ref[...].astype(F32)
    gated = (
        jnp.where(hit_hi[0], gates[:, 0:1], 0.0) + jnp.where(hit_hi[1], gates[:, 1:2], 0.0)
    ).astype(BF)
    second_part = part.at[0, 0]
    second_part[0:TOKENS, :] = gated

    @pl.loop(0, 4)
    def _(t):
        cols = pl.ds(pl.multiple_of(t * 256, 256), 256)
        rows = dot(pick_lo[:, cols], x_ref[...], 0, 0) + dot(
            second_part[0:TOKENS, cols], z_ref[...], 0, 0
        )
        send[pl.ds(t * 16, 16)] = rows.astype(BF).reshape(16, BLOCK, WIDTH)

    pl.semaphore_wait(barrier, PEERS - 1 + 2)

    def dispatch(j, k, xo):
        pltpu.make_async_remote_copy(
            src_ref=send.at[j],
            dst_ref=recv.at[j],
            send_sem=send_sem,
            recv_sem=recv_sem.at[j // EXP],
            device_id=ahead(k, xo),
            device_id_type=MESH,
        ).start()

    @pl.loop(EXP, PEERS)
    def _(j):
        dispatch(j, *hop(j))

    for j in range(1, EXP):
        dispatch(j, 0, j)
    recv[0] = send[0]

    load_in.wait()
    load_out.wait()
    wait_bytes(recv.at[pl.ds(1, EXP - 1)], recv_sem.at[0])
    for s in range(1, PER_CHUNK // EXP):
        wait_bytes(recv.at[pl.ds(s * EXP, EXP)], recv_sem.at[s])

    lane128 = lax.broadcasted_iota(I32, (CHUNK_ROWS, 128), 1)
    slot128 = lax.broadcasted_iota(I32, (CHUNK_ROWS, 128), 0) % CAP

    def give_back(j, k, xo):
        pltpu.make_async_remote_copy(
            src_ref=bsend.at[j],
            dst_ref=brecv.at[j],
            send_sem=bsend_sem,
            recv_sem=brecv_sem,
            device_id=behind(k, xo),
            device_id_type=MESH,
        ).start()
        pltpu.make_async_remote_copy(
            src_ref=hsend.at[j],
            dst_ref=hrecv.at[j],
            send_sem=hsend_sem,
            recv_sem=hrecv_sem,
            device_id=behind(k, xo),
            device_id_type=MESH,
        ).start()

    @pl.loop(0, CHUNKS)
    def _(ch):
        base = ch * PER_CHUNK

        @pl.when(ch > 0)
        def _():
            for i in range(PER_CHUNK // EXP):
                wait_bytes(
                    recv.at[pl.ds(base + i * EXP, EXP)], recv_sem.at[ch * (PER_CHUNK // EXP) + i]
                )

        rows = pl.ds(pl.multiple_of(ch * CHUNK_ROWS, CHUNK_ROWS), CHUNK_ROWS)
        peers = pl.ds(base, PER_CHUNK)
        came = recv[peers].astype(F32)
        u_all[rows] = came[:, :CAP].reshape(CHUNK_ROWS, WIDTH).astype(BF)
        s_all[rows] = came[:, CAP:].reshape(CHUNK_ROWS, WIDTH).astype(BF)

        def hidden(t, total):
            cols = pl.ds(pl.multiple_of(t * 256, 256), 256)
            pre = dot(u_all[rows], win[:, cols], 1, 0)
            grad = dot(s_all[rows], wout[cols, :], 1, 1)
            sigma = jax.nn.sigmoid(pre)
            act = pre * sigma
            act_all[rows, cols] = act.astype(BF)
            gp_all[rows, cols] = (grad * sigma * (1.0 + pre * (1.0 - sigma))).astype(BF)
            return total + jnp.sum(act * grad, axis=1, keepdims=True)

        total = lax.fori_loop(0, WIDTH // 256, hidden, jnp.zeros((CHUNK_ROWS, 1), F32))
        spread = jnp.where(lane128 == slot128, total, 0.0)
        hsend[peers] = jnp.sum(spread.reshape(PER_CHUNK, CAP, 128), axis=1, keepdims=True)

        @pl.loop(0, 2)
        def _(t):
            lo = pl.ds(pl.multiple_of(t * 256, 256), 256)
            hi = pl.ds(pl.multiple_of(t * 256 + 512, 256), 256)
            low = dot(gp_all[rows], win[lo, :], 1, 1).reshape(PER_CHUNK, CAP, 256)
            high = dot(gp_all[rows], win[hi, :], 1, 1).reshape(PER_CHUNK, CAP, 256)
            bsend[peers, :, lo] = jnp.concatenate([low, high], axis=1).astype(BF)

        @pl.when(ch == 0)
        def _():
            brecv[0] = bsend[0]
            hrecv[0] = hsend[0]
            for j in range(1, EXP):
                give_back(j, 0, j)

        @pl.when(ch > 0)
        def _():
            for i in range(EXP):
                give_back(base + i, *hop(base + i))

        @pl.loop(EXP, PER_CHUNK)
        def _(i):
            give_back(base + i, *hop(base + i))

    def make_part(o):
        cols = pl.ds(pl.multiple_of(lax.rem(me_d + o, DP) * PART, PART), PART)

        @pl.loop(0, 2)
        def _(t):
            half = pl.ds(pl.multiple_of(t * 512, 512), 512)
            part[o, 0, :, half] = dot(u_all[:, cols], gp_all[:, half], 0, 0).astype(BF)
            part[o, 1, :, half] = dot(act_all[:, cols], s_all[:, half], 0, 0).astype(BF)

    def to_dp(n, src, dst, other):
        copy = pltpu.make_async_remote_copy(
            src_ref=src,
            dst_ref=dst,
            send_sem=dp_send.at[n],
            recv_sem=dp_recv.at[n],
            device_id={"dp": other},
            device_id_type=MESH,
        )
        copy.start()
        return copy

    make_part(2)
    c0 = to_dp(0, part.at[2, 0], first.at[0], right)
    c1 = to_dp(1, part.at[2, 1], first.at[1], left)
    make_part(1)
    c2 = to_dp(2, part.at[1, 1], second.at[0, 1], right)
    make_part(3)
    c3 = to_dp(3, part.at[3, 0], second.at[1, 0], left)
    make_part(0)
    c0.wait_recv()
    part[1, 0] = (part[1, 0].astype(F32) + first[0].astype(F32)).astype(BF)
    c4 = to_dp(4, part.at[1, 0], second.at[0, 0], right)
    c1.wait_recv()
    part[3, 1] = (part[3, 1].astype(F32) + first[1].astype(F32)).astype(BF)
    c5 = to_dp(5, part.at[3, 1], second.at[1, 1], left)

    others = pl.ds(1, PEERS - 1)
    wait_bytes(brecv.at[others], brecv_sem)
    wait_bytes(hrecv.at[others], hrecv_sem)
    back = brecv[...].reshape(PEERS * BLOCK, WIDTH // 2)
    dres_ref[:, : WIDTH // 2] = (
        z_ref[:, : WIDTH // 2].astype(F32) + dot(pick_lo[...], back, 1, 0)
    ).astype(BF)
    dres_ref[:, WIDTH // 2 :] = (
        z_ref[:, WIDTH // 2 :].astype(F32) + dot(pick_hi[...], back, 1, 0)
    ).astype(BF)
    sums = jnp.sum(hrecv[...], axis=1)
    lane_s = lax.broadcasted_iota(I32, (TOKENS, 128), 1)
    parts = []
    for t in range(2):
        chosen = dot(named[t], sums, 1, 0, lax.Precision.HIGHEST)
        value = jnp.sum(jnp.where(lane_s == slot[t], chosen, 0.0), axis=1, keepdims=True)
        parts.append(value / gates[:, t : t + 1])
    lane2 = lax.broadcasted_iota(I32, (TOKENS, 2), 1)
    dgate_ref[...] = jnp.where(lane2 == 0, parts[0], parts[1]).astype(BF)

    for c in (c2, c3, c4, c5):
        c.wait_recv()
    for i in range(2):
        quarter_ref[i] = (
            part[0, i].astype(F32) + second[0, i].astype(F32) + second[1, i].astype(F32)
        ).astype(BF)
    for c in (c0, c1, c2, c3, c4, c5):
        c.wait_send()
    wait_bytes(send.at[others], send_sem)
    wait_bytes(bsend.at[others], bsend_sem)
    wait_bytes(hsend.at[others], hsend_sem)


def expert_layer(x, z, ids, gates, win, wout):
    vmem = pl.BlockSpec(memory_space=pltpu.VMEM)
    anywhere = pl.BlockSpec(memory_space=pl.ANY)
    rows = PEERS * CAP
    return pl.pallas_call(
        moe_kernel,
        out_shape=(
            jax.ShapeDtypeStruct((TOKENS, WIDTH), BF),
            jax.ShapeDtypeStruct((TOKENS, 2), BF),
            jax.ShapeDtypeStruct((2, PART, WIDTH), BF),
        ),
        in_specs=[vmem] * 4 + [anywhere] * 2,
        out_specs=(vmem,) * 3,
        scratch_shapes=[
            pltpu.VMEM((WIDTH, WIDTH), BF),
            pltpu.VMEM((WIDTH, WIDTH), BF),
            pltpu.VMEM((PEERS, BLOCK, WIDTH), BF),
            pltpu.VMEM((PEERS, BLOCK, WIDTH), BF),
            pltpu.VMEM((TOKENS, PEERS * BLOCK), BF),
            pltpu.VMEM((TOKENS, PEERS * BLOCK), BF),
            pltpu.VMEM((rows, WIDTH), BF),
            pltpu.VMEM((rows, WIDTH), BF),
            pltpu.VMEM((rows, WIDTH), BF),
            pltpu.VMEM((rows, WIDTH), BF),
            pltpu.VMEM((PEERS, BLOCK, WIDTH // 2), BF),
            pltpu.VMEM((PEERS, BLOCK, WIDTH // 2), BF),
            pltpu.VMEM((PEERS, 1, 128), F32),
            pltpu.VMEM((PEERS, 1, 128), F32),
            pltpu.VMEM((DP, 2, PART, WIDTH), BF),
            pltpu.VMEM((2, PART, WIDTH), BF),
            pltpu.VMEM((2, 2, PART, WIDTH), BF),
            pltpu.SemaphoreType.DMA((2,)),
            pltpu.SemaphoreType.DMA,
            pltpu.SemaphoreType.DMA((CTX,)),
            pltpu.SemaphoreType.DMA,
            pltpu.SemaphoreType.DMA,
            pltpu.SemaphoreType.DMA,
            pltpu.SemaphoreType.DMA,
            pltpu.SemaphoreType.DMA((6,)),
            pltpu.SemaphoreType.DMA((6,)),
        ],
        compiler_params=pltpu.CompilerParams(
            collective_id=0, has_side_effects=True, vmem_limit_bytes=VMEM_BYTES
        ),
        name="experts",
    )(x, z, ids, gates, win, wout)


def attention_kernel(
    q_ref,
    k_ref,
    v_ref,
    seg_ref,
    list_ref,
    dres_ref,
    quarter_ref,
    dq_ref,
    dk_ref,
    dv_ref,
    gin_ref,
    gout_ref,
    k_all,
    v_all,
    seg_prev,
    do_all,
    k_aug,
    q_aug,
    acc_k,
    acc_v,
    over,
    came,
    kv_send,
    kv_recv,
    do_send,
    do_recv,
    ag_send,
    ag_recv,
    own_sem,
    ret_send,
    ret_recv,
):
    me_d, me_c, me_x = lax.axis_index("dp"), lax.axis_index("ctx"), lax.axis_index("exp")
    right, left = lax.rem(me_d + 1, DP), lax.rem(me_d + DP - 1, DP)
    after, prior = lax.rem(me_c + 1, CTX), lax.rem(me_c + CTX - 1, CTX)

    barrier = pltpu.get_barrier_semaphore()
    for target in (
        [{"dp": left}, {"dp": right}, {"ctx": after}, {"ctx": prior}]
        + [{"exp": lax.rem(me_x + o, EXP)} for o in range(1, EXP)]
    ):
        pl.semaphore_signal(barrier, inc=1, device_id=target, device_id_type=MESH)
    pl.semaphore_wait(barrier, 4 + EXP - 1)

    def remote(src, dst, ssem, rsem, target):
        copy = pltpu.make_async_remote_copy(
            src_ref=src, dst_ref=dst, send_sem=ssem, recv_sem=rsem,
            device_id=target, device_id_type=MESH,
        )
        copy.start()
        return copy

    mine = pl.ds(pl.multiple_of(me_d * PART, PART), PART)
    lefts = pl.ds(pl.multiple_of(left * PART, PART), PART)
    rights = pl.ds(pl.multiple_of(right * PART, PART), PART)
    sends = []
    my_rows = pl.ds(pl.multiple_of(me_x * TOKENS, TOKENS), TOKENS)
    do_copies = []
    for o in range(1, EXP):
        px = lax.rem(me_x + o, EXP)
        do_copies.append(
            remote(
                dres_ref.at[:, pl.ds(pl.multiple_of(px * LOCAL, LOCAL), LOCAL)],
                do_all.at[my_rows],
                do_send.at[o - 1],
                do_recv.at[o - 1],
                {"exp": px},
            )
        )
    kv_copies = [
        remote(seg_ref, seg_prev, kv_send.at[2], kv_recv.at[2], {"ctx": after}),
        remote(k_ref, k_all.at[pl.ds(0, FRAMES)], kv_send.at[0], kv_recv.at[0], {"ctx": after}),
        remote(v_ref, v_all.at[pl.ds(0, FRAMES)], kv_send.at[1], kv_recv.at[1], {"ctx": after}),
    ]
    in_right = remote(
        quarter_ref.at[0], gin_ref.at[mine], ag_send.at[0], ag_recv.at[0], {"dp": right}
    )
    out_left = remote(
        quarter_ref.at[1], gout_ref.at[mine], ag_send.at[1], ag_recv.at[1], {"dp": left}
    )
    out_right = remote(
        quarter_ref.at[1], gout_ref.at[mine], ag_send.at[2], ag_recv.at[2], {"dp": right}
    )
    in_left = remote(
        quarter_ref.at[0], gin_ref.at[mine], ag_send.at[3], ag_recv.at[3], {"dp": left}
    )
    own = [
        pltpu.make_async_copy(quarter_ref.at[0], gin_ref.at[mine], own_sem.at[0]),
        pltpu.make_async_copy(quarter_ref.at[1], gout_ref.at[mine], own_sem.at[1]),
    ]
    for c in own:
        c.start()

    k_all[FRAMES:] = k_ref[...]
    v_all[FRAMES:] = v_ref[...]
    do_all[my_rows] = dres_ref[:, pl.ds(pl.multiple_of(me_x * LOCAL, LOCAL), LOCAL)]
    acc_k[...] = jnp.zeros_like(acc_k)
    acc_v[...] = jnp.zeros_like(acc_v)

    kinds = 2 * GROUPS
    lane_f = lax.broadcasted_iota(I32, (kinds, 128), 1)
    row_f = lax.broadcasted_iota(I32, (kinds, 128), 0)
    place = ((lane_f == row_f) | (lane_f == row_f + 64)).astype(F32).astype(BF)
    row8 = lax.broadcasted_iota(I32, (8, FRAMES), 0)
    group_of = lax.broadcasted_iota(I32, (8, FRAMES), 1) // GROUP
    seg_own = seg_ref[...] == row8
    kv_copies[0].wait_recv()
    seg_past = seg_prev[...] == row8
    lists = list_ref[...]
    moved = jnp.where(lists >= 0, lists - (me_c - 1) * GROUPS, -1)

    def listed(groups):
        return (
            (moved[:, 0:1] == groups) | (moved[:, 1:2] == groups) | (moved[:, 2:3] == groups)
        )

    list_past = listed(group_of)
    list_own = listed(group_of + GROUPS) | (group_of == row8)

    def features(segment, group, miss, match):
        both = jnp.concatenate(
            [jnp.where(segment, match, miss), jnp.where(group, match, miss)], axis=0
        ).astype(BF)
        return dot(both, place, 0, 0).astype(BF)

    feat_q = features(seg_own, group_of == row8, 0.0, 1.0)
    feat_past = features(seg_past, list_past, -FAR, 0.0)
    feat_own = features(seg_own, list_own, -FAR, 0.0)
    low = lax.broadcasted_iota(I32, (FRAMES, 128), 1) < 64
    for hp in range(2):
        tile = slice(hp * 128, hp * 128 + 128)
        q_t = (q_ref[:, tile].astype(F32) * 0.125).astype(BF)
        k_t = k_ref[:, tile]
        q_aug[2 * hp] = jnp.where(low, q_t, feat_q)
        q_aug[2 * hp + 1] = jnp.where(low, feat_q, q_t)
        k_aug[2 * hp, FRAMES:] = jnp.where(low, k_t, feat_own)
        k_aug[2 * hp + 1, FRAMES:] = jnp.where(low, feat_own, k_t)
    kv_copies[1].wait_recv()
    for hp in range(2):
        tile = slice(hp * 128, hp * 128 + 128)
        k_t = k_all[:FRAMES, tile]
        k_aug[2 * hp, :FRAMES] = jnp.where(low, k_t, feat_past)
        k_aug[2 * hp + 1, :FRAMES] = jnp.where(low, feat_past, k_t)
    kv_copies[2].wait_recv()
    for c in do_copies:
        c.wait_recv()

    low_q = lax.broadcasted_iota(I32, (QROWS, 128), 1) < 64
    none = jnp.zeros((QROWS, 128), BF)

    def block(b, carry):
        rows = pl.ds(pl.multiple_of(b * QROWS, QROWS), QROWS)
        window = pl.ds(pl.multiple_of(b * QROWS, QROWS), WINDOW)
        for hp in range(2):
            tile = slice(hp * 128, hp * 128 + 128)
            do_t = do_all[rows, tile]
            v_t = v_all[window, tile]
            k_t = k_all[window, tile]
            halves_p, halves_s, halves_d, halves_q, outs = [], [], [], [], []
            for e in range(2):
                q_a = q_aug[2 * hp + e, rows]
                score = dot(q_a, k_aug[2 * hp + e, window], 1, 1)
                high = jnp.max(score, axis=1, keepdims=True)
                weight = jnp.exp(score - high)
                weight = weight * (1.0 / jnp.sum(weight, axis=1, keepdims=True))
                probs = weight.astype(BF)
                keep = low_q if e == 0 else jnp.logical_not(low_q)
                do_e = jnp.where(keep, do_t, none)
                grad = dot(do_e, v_t, 1, 1)
                delta = jnp.sum(probs.astype(F32) * grad, axis=1, keepdims=True)
                dscore = (weight * (grad - delta)).astype(BF)
                outs.append(dot(dscore, k_t, 1, 0))
                halves_p.append(probs)
                halves_s.append(dscore)
                halves_d.append(do_e)
                halves_q.append(jnp.where(keep, q_a, none))
            dq_ref[rows, tile] = (jnp.where(low_q, outs[0], outs[1]) * 0.125).astype(BF)
            acc_k[window, tile] += dot(
                jnp.concatenate(halves_s, axis=0), jnp.concatenate(halves_q, axis=0), 0, 0
            )
            acc_v[window, tile] += dot(
                jnp.concatenate(halves_p, axis=0), jnp.concatenate(halves_d, axis=0), 0, 0
            )
        return carry

    blocks = FRAMES // QROWS
    lax.fori_loop(0, blocks // 2, block, 0)
    in_right.wait_recv()
    on_right = remote(
        gin_ref.at[lefts], gin_ref.at[lefts], ag_send.at[4], ag_recv.at[4], {"dp": right}
    )
    out_left.wait_recv()
    on_left = remote(
        gout_ref.at[rights], gout_ref.at[rights], ag_send.at[5], ag_recv.at[5], {"dp": left}
    )
    lax.fori_loop(blocks // 2, blocks, block, 0)

    over[0] = acc_k[:FRAMES].astype(BF)
    over[1] = acc_v[:FRAMES].astype(BF)
    returned = [
        remote(over.at[i], came.at[i], ret_send.at[i], ret_recv.at[i], {"ctx": prior})
        for i in range(2)
    ]
    returned[0].wait_recv()
    dk_ref[...] = (acc_k[FRAMES:] + came[0].astype(F32)).astype(BF)
    returned[1].wait_recv()
    dv_ref[...] = (acc_v[FRAMES:] + came[1].astype(F32)).astype(BF)
    for c in (out_right, in_left, on_right, on_left):
        c.wait_recv()
    for c in own:
        c.wait()
    for c in do_copies + kv_copies + returned:
        c.wait_send()
    for c in (in_right, out_left, out_right, in_left, on_right, on_left):
        c.wait_send()


def attention(q, k, v, seg, lists, dres, quarter):
    vmem = pl.BlockSpec(memory_space=pltpu.VMEM)
    anywhere = pl.BlockSpec(memory_space=pl.ANY)
    frames = jax.ShapeDtypeStruct((FRAMES, LOCAL), BF)
    weight = jax.ShapeDtypeStruct((WIDTH, WIDTH), BF)
    dma = pltpu.SemaphoreType.DMA
    return pl.pallas_call(
        attention_kernel,
        out_shape=(frames, frames, frames, weight, weight),
        in_specs=[vmem] * 7,
        out_specs=(vmem, vmem, vmem, anywhere, anywhere),
        scratch_shapes=[
            pltpu.VMEM((2 * FRAMES, LOCAL), BF),
            pltpu.VMEM((2 * FRAMES, LOCAL), BF),
            pltpu.VMEM((1, FRAMES), I32),
            pltpu.VMEM((FRAMES, LOCAL), BF),
            pltpu.VMEM((4, 2 * FRAMES, 128), BF),
            pltpu.VMEM((4, FRAMES, 128), BF),
            pltpu.VMEM((2 * FRAMES, LOCAL), F32),
            pltpu.VMEM((2 * FRAMES, LOCAL), F32),
            pltpu.VMEM((2, FRAMES, LOCAL), BF),
            pltpu.VMEM((2, FRAMES, LOCAL), BF),
            dma((3,)),
            dma((3,)),
            dma((3,)),
            dma((3,)),
            dma((6,)),
            dma((6,)),
            dma((2,)),
            dma((2,)),
            dma((2,)),
        ],
        compiler_params=pltpu.CompilerParams(
            collective_id=1, has_side_effects=True, vmem_limit_bytes=VMEM_BYTES
        ),
        name="attention",
    )(q, k, v, seg, lists, dres, quarter)


def local(
    queries,
    key_rows,
    value_rows,
    segments,
    left_blocks,
    moe_input,
    out_grad,
    expert_ids,
    gate_weights,
    expert_in,
    expert_out,
):
    d_residual, d_gates, quarter = expert_layer(
        moe_input[0], out_grad[0], expert_ids[0], gate_weights[0], expert_in[0], expert_out[0]
    )
    dq, dk, dv, grad_in, grad_out = attention(
        queries[0], key_rows[0], value_rows[0], segments, left_blocks[0], d_residual, quarter
    )
    return (
        dq[None],
        dk[None],
        dv[None],
        d_residual[None],
        d_gates[None],
        grad_in[None],
        grad_out[None],
    )


def solution(mesh):
    assert dict(mesh.shape) == {"dp": DP, "ctx": CTX, "exp": EXP}
    return jax.shard_map(
        local,
        mesh=mesh,
        in_specs=(
            P("dp", "ctx", "exp"),
            P("dp", "ctx", "exp"),
            P("dp", "ctx", "exp"),
            P("dp", "ctx"),
            P("dp", "ctx", None),
            P("dp", ("ctx", "exp"), None),
            P("dp", ("ctx", "exp"), None),
            P("dp", ("ctx", "exp"), None),
            P("dp", ("ctx", "exp"), None),
            P(("ctx", "exp"), None, None),
            P(("ctx", "exp"), None, None),
        ),
        out_specs=(
            P("dp", "ctx", "exp"),
            P("dp", "ctx", "exp"),
            P("dp", "ctx", "exp"),
            P("dp", ("ctx", "exp"), None),
            P("dp", ("ctx", "exp"), None),
            P(("ctx", "exp"), None, None),
            P(("ctx", "exp"), None, None),
        ),
        check_vma=False,
    )
```

```python
import types

import jax
import jax.numpy as jnp
from jax import lax
from jax.experimental import pallas as pl
from jax.experimental.pallas import tpu as pltpu
from jax.sharding import PartitionSpec as P

MESH = pl.DeviceIdType.MESH
BF = jnp.bfloat16
F32 = jnp.float32
I32 = jnp.int32

DP, CTX, EXP = 4, 16, 4
PEERS = CTX * EXP
HALF = CTX // 2
CAP = 8
BLOCK = 2 * CAP
TOKENS = 128
WIDTH = 1024
PART = WIDTH // DP
CHUNKS = 4
PER_CHUNK = PEERS // CHUNKS
CHUNK_ROWS = PER_CHUNK * CAP
ROWS = PEERS * CAP
ORDER = (2, 1, 3, 0)
GROUP = 64
GROUPS = 8
FRAMES = 512
LOCAL = 256
QROWS = 128
BLOCKS = FRAMES // QROWS
WINDOW = FRAMES + QROWS
FAR = 32768.0
VMEM_BYTES = 56 * 1024 * 1024


def dot(a, b, ca, cb, precision=None):
    return lax.dot_general(
        a, b, (((ca,), (cb,)), ((), ())), preferred_element_type=F32, precision=precision
    )


def wait_bytes(ref, sem):
    pltpu.make_async_copy(ref, ref, sem).wait()


def span(index, size):
    return pl.ds(pl.multiple_of(index * size, size), size)


def hop(j):
    s = j // EXP
    return HALF + (2 * (s % 2) - 1) * (s // 2), j % EXP


def iota(shape, dim):
    return lax.broadcasted_iota(I32, shape, dim)


def column(row):
    n = row.shape[1]
    same = iota((n, n), 0) == iota((n, n), 1)
    return jnp.sum(jnp.where(same, row, jnp.zeros_like(row)), axis=1, keepdims=True)


def as_row(col):
    n = col.shape[0]
    same = iota((n, n), 0) == iota((n, n), 1)
    return jnp.sum(jnp.where(same, col, jnp.zeros_like(col)), axis=0, keepdims=True)


INPUTS = ("q", "k", "v", "seg", "lists", "x", "z", "ids", "gate", "win", "wout")
OUTPUTS = ("dq", "dk", "dv", "dres", "dgate", "gout", "gin")
DMA = pltpu.SemaphoreType.DMA
LOADS = ("ids", "gate", "x", "z", "win", "wout", "q", "seg", "lists", "k", "v")
SCRATCH = dict(
    q_own=pltpu.VMEM((FRAMES, LOCAL), BF),
    seg_own=pltpu.VMEM((1, FRAMES), I32),
    lists_own=pltpu.VMEM((3, 1, GROUPS), I32),
    x_own=pltpu.VMEM((TOKENS, WIDTH), BF),
    z_own=pltpu.VMEM((TOKENS, WIDTH), BF),
    ids_own=pltpu.VMEM((2, TOKENS), I32),
    gate_own=pltpu.VMEM((2, TOKENS), BF),
    w_in=pltpu.VMEM((WIDTH, WIDTH), BF),
    w_out=pltpu.VMEM((WIDTH, WIDTH), BF),
    pick=pltpu.VMEM((2 * TOKENS, PEERS * BLOCK), BF),
    gated=pltpu.VMEM((2 * TOKENS, PEERS * BLOCK), BF),
    xx=pltpu.VMEM((2 * TOKENS, WIDTH // 2), BF),
    zz=pltpu.VMEM((2 * TOKENS, WIDTH // 2), BF),
    send_u=pltpu.VMEM((PEERS, BLOCK, WIDTH // 2), BF),
    recv_u=pltpu.VMEM((PEERS, BLOCK, WIDTH // 2), BF),
    send_s=pltpu.VMEM((DP, PEERS, BLOCK, PART // 2), BF),
    recv_s=pltpu.VMEM((DP, PEERS, BLOCK, PART // 2), BF),
    u_chunk=pltpu.VMEM((CHUNK_ROWS, WIDTH), BF),
    u_t=pltpu.VMEM((WIDTH, ROWS), BF),
    act_t=pltpu.VMEM((WIDTH, ROWS), BF),
    pre_all=pltpu.VMEM((ROWS, WIDTH), F32),
    s_all=pltpu.VMEM((ROWS, WIDTH), BF),
    gp_all=pltpu.VMEM((ROWS, WIDTH), BF),
    bsend=pltpu.VMEM((PEERS, BLOCK, WIDTH // 2), BF),
    brecv=pltpu.VMEM((PEERS, BLOCK, WIDTH // 2), BF),
    hsend=pltpu.VMEM((PEERS, 1, 128), F32),
    hrecv=pltpu.VMEM((PEERS, 1, 128), F32),
    part=pltpu.VMEM((2, DP, WIDTH, PART), BF),
    first=pltpu.VMEM((2, 2, WIDTH // 2, PART), BF),
    second=pltpu.VMEM((2, 2, WIDTH, PART), BF),
    fin=pltpu.VMEM((2, WIDTH, PART), BF),
    k_all=pltpu.VMEM((2 * FRAMES, LOCAL), BF),
    v_all=pltpu.VMEM((2 * FRAMES, LOCAL), BF),
    seg_prev=pltpu.VMEM((1, FRAMES), I32),
    do_all=pltpu.VMEM((FRAMES, LOCAL), BF),
    k_aug=pltpu.VMEM((4, 2 * FRAMES, 128), BF),
    q_aug=pltpu.VMEM((4, FRAMES, 128), BF),
    probs=pltpu.VMEM((4, FRAMES, WINDOW), BF),
    acc_k=pltpu.VMEM((2 * FRAMES, LOCAL), F32),
    acc_v=pltpu.VMEM((2 * FRAMES, LOCAL), F32),
    over=pltpu.VMEM((2, FRAMES, LOCAL), BF),
    came=pltpu.VMEM((2, FRAMES, LOCAL), BF),
    load_sem=DMA((len(LOADS),)),
    u_send=DMA,
    u_recv=DMA((CTX,)),
    s_send=DMA((DP,)),
    s_recv=DMA((DP,)),
    b_send=DMA,
    b_recv=DMA,
    h_send=DMA,
    h_recv=DMA,
    rs_send=DMA((2, 6)),
    rs_recv=DMA((2, 6)),
    ag_send=DMA((2, 6)),
    ag_recv=DMA((2, 6)),
    own_sem=DMA((2,)),
    kv_send=DMA((3,)),
    kv_recv=DMA((3,)),
    do_send=DMA((EXP - 1,)),
    do_recv=DMA((EXP - 1,)),
    ret_send=DMA((2,)),
    ret_recv=DMA((2,)),
)


def layer_kernel(*refs):
    r = types.SimpleNamespace(**dict(zip(INPUTS + OUTPUTS + tuple(SCRATCH), refs)))
    me_d, me_c, me_x = lax.axis_index("dp"), lax.axis_index("ctx"), lax.axis_index("exp")
    right, left = lax.rem(me_d + 1, DP), lax.rem(me_d + DP - 1, DP)
    after, prior = lax.rem(me_c + 1, CTX), lax.rem(me_c + CTX - 1, CTX)
    outs = (r.gout, r.gin)

    targets = dict(
        ids=r.ids_own,
        gate=r.gate_own,
        x=r.x_own,
        z=r.z_own,
        win=r.w_in,
        wout=r.w_out,
        q=r.q_own,
        seg=r.seg_own,
        lists=r.lists_own,
        k=r.k_all.at[pl.ds(FRAMES, FRAMES)],
        v=r.v_all.at[pl.ds(FRAMES, FRAMES)],
    )
    loads = {
        name: pltpu.make_async_copy(getattr(r, name), targets[name], r.load_sem.at[i])
        for i, name in enumerate(LOADS)
    }
    for name in LOADS:
        loads[name].start()

    def ahead(k, xo):
        return {"ctx": lax.rem(me_c + k, CTX), "exp": lax.rem(me_x + xo, EXP)}

    def behind(k, xo):
        return {"ctx": lax.rem(me_c - k + CTX, CTX), "exp": lax.rem(me_x - xo + EXP, EXP)}

    def remote(src, dst, ssem, rsem, target):
        copy = pltpu.make_async_remote_copy(
            src_ref=src,
            dst_ref=dst,
            send_sem=ssem,
            recv_sem=rsem,
            device_id=target,
            device_id_type=MESH,
        )
        copy.start()
        return copy

    barrier = pltpu.get_barrier_semaphore()
    for other in (left, right):
        pl.semaphore_signal(barrier, inc=1, device_id={"dp": other}, device_id_type=MESH)
    for j in range(1, EXP):
        pl.semaphore_signal(barrier, inc=1, device_id=ahead(0, j), device_id_type=MESH)

    @pl.loop(EXP, PEERS)
    def _(j):
        k, xo = hop(j)
        pl.semaphore_signal(barrier, inc=1, device_id=ahead(k, xo), device_id_type=MESH)

    lane64 = iota((TOKENS, PEERS), 1)
    lane_q = iota((TOKENS, PEERS * BLOCK), 1)

    def relative(ids):
        k = (ids // EXP - me_c + CTX) % CTX
        xo = (ids % EXP - me_x + EXP) % EXP
        s = jnp.where(k == 0, 0, jnp.where(k < HALF, CTX - 2 * k, 2 * k - CTX + 1))
        return s * EXP + xo

    loads["ids"].wait()
    peer = [column(relative(r.ids_own[t : t + 1, :])) for t in range(2)]
    named = [(peer[t] == lane64).astype(F32) for t in range(2)]
    before = (iota((TOKENS, TOKENS), 1) < iota((TOKENS, TOKENS), 0)).astype(F32).astype(BF)
    earlier = dot(before, (named[0] + named[1]).astype(BF), 1, 0)
    slot = [jnp.sum(named[t] * earlier, axis=1, keepdims=True).astype(I32) for t in range(2)]
    row = [peer[t] * BLOCK + slot[t] for t in range(2)]
    loads["gate"].wait()
    gates = [column(r.gate_own[t : t + 1, :].astype(F32)) for t in range(2)]
    for half in range(2):
        hit = [row[t] + half * CAP == lane_q for t in range(2)]
        rows = pl.ds(half * TOKENS, TOKENS)
        r.pick[rows] = (hit[0] | hit[1]).astype(F32).astype(BF)
        r.gated[rows] = (
            jnp.where(hit[0], gates[0], 0.0) + jnp.where(hit[1], gates[1], 0.0)
        ).astype(BF)
    loads["x"].wait()
    r.xx[:TOKENS] = r.x_own[:, : WIDTH // 2]
    r.xx[TOKENS:] = r.x_own[:, WIDTH // 2 :]

    @pl.loop(0, CHUNKS)
    def _(t):
        rows = dot(r.pick[:, span(t, 256)], r.xx[...], 0, 0)
        r.send_u[pl.ds(t * 16, 16)] = rows.astype(BF).reshape(16, BLOCK, WIDTH // 2)

    pl.semaphore_wait(barrier, PEERS - 1 + 2)

    def send_rows(j, k, xo):
        remote(r.send_u.at[j], r.recv_u.at[j], r.u_send, r.u_recv.at[j // EXP], ahead(k, xo))

    @pl.loop(EXP, PEERS)
    def _(j):
        send_rows(j, *hop(j))

    for j in range(1, EXP):
        send_rows(j, 0, j)
    r.recv_u[0] = r.send_u[0]

    loads["z"].wait()
    for n, o in enumerate(ORDER):
        member = lax.rem(me_d + o, DP)
        tile = slice(n * 128, n * 128 + 128)
        r.zz[:TOKENS, tile] = r.z_own[:, span(2 * member, 128)]
        r.zz[TOKENS:, tile] = r.z_own[:, span(2 * member + 1, 128)]

    @pl.loop(0, CHUNKS)
    def _(t):
        rows = dot(r.gated[:, span(t, 256)], r.zz[...], 0, 0).astype(BF)
        for n in range(DP):
            r.send_s[n, pl.ds(t * 16, 16)] = rows[:, n * 128 : n * 128 + 128].reshape(
                16, BLOCK, 128
            )

    for n in range(DP):

        def send_grads(j, k, xo):
            remote(
                r.send_s.at[n, j], r.recv_s.at[n, j], r.s_send.at[n], r.s_recv.at[n], ahead(k, xo)
            )

        @pl.loop(EXP, PEERS)
        def _(j):
            send_grads(j, *hop(j))

        for j in range(1, EXP):
            send_grads(j, 0, j)
        r.recv_s[n, 0] = r.send_s[n, 0]

    past = pl.ds(0, FRAMES)
    kv_copies = [
        remote(r.seg, r.seg_prev, r.kv_send.at[0], r.kv_recv.at[0], {"ctx": after}),
        remote(r.k, r.k_all.at[past], r.kv_send.at[1], r.kv_recv.at[1], {"ctx": after}),
        remote(r.v, r.v_all.at[past], r.kv_send.at[2], r.kv_recv.at[2], {"ctx": after}),
    ]

    for name in ("q", "seg", "lists", "k", "v"):
        loads[name].wait()
    kinds = 2 * GROUPS
    lane_f, row_f = iota((kinds, 128), 1), iota((kinds, 128), 0)
    place = ((lane_f == row_f) | (lane_f == row_f + 64)).astype(F32).astype(BF)
    row8 = iota((8, FRAMES), 0)
    group_of = iota((8, FRAMES), 1) // GROUP
    moved = []
    for j in range(3):
        lists = column(r.lists_own[j])
        moved.append(jnp.where(lists >= 0, lists - (me_c - 1) * GROUPS, -1))

    def listed(groups):
        return (moved[0] == groups) | (moved[1] == groups) | (moved[2] == groups)

    def features(segment, group, miss, match):
        both = jnp.concatenate(
            [jnp.where(segment, match, miss), jnp.where(group, match, miss)], axis=0
        ).astype(BF)
        return dot(both, place, 0, 0).astype(BF)

    low = iota((FRAMES, 128), 1) < 64
    low_q = iota((QROWS, 128), 1) < 64
    none = jnp.zeros((QROWS, 128), BF)

    def augment(part, feat):
        for hp in range(2):
            k_t = r.k_all[part, hp * 128 : hp * 128 + 128]
            r.k_aug[2 * hp, part] = jnp.where(low, k_t, feat)
            r.k_aug[2 * hp + 1, part] = jnp.where(low, feat, k_t)

    seg_own = r.seg_own[...] == row8
    feat_q = features(seg_own, group_of == row8, 0.0, 1.0)
    for hp in range(2):
        q_t = (r.q_own[:, hp * 128 : hp * 128 + 128].astype(F32) * 0.125).astype(BF)
        r.q_aug[2 * hp] = jnp.where(low, q_t, feat_q)
        r.q_aug[2 * hp + 1] = jnp.where(low, feat_q, q_t)
    list_own = listed(group_of + GROUPS) | (group_of == row8)
    augment(pl.ds(FRAMES, FRAMES), features(seg_own, list_own, -FAR, 0.0))
    r.acc_k[...] = jnp.zeros_like(r.acc_k)
    r.acc_v[...] = jnp.zeros_like(r.acc_v)

    loads["win"].wait()
    loads["wout"].wait()

    @pl.loop(0, CHUNKS)
    def _(ch):
        base = ch * PER_CHUNK

        @pl.when(ch == 0)
        def _():
            wait_bytes(r.recv_u.at[pl.ds(1, EXP - 1)], r.u_recv.at[0])

        @pl.when(ch > 0)
        def _():
            wait_bytes(r.recv_u.at[pl.ds(base, EXP)], r.u_recv.at[ch * (PER_CHUNK // EXP)])

        for i in range(1, PER_CHUNK // EXP):
            wait_bytes(
                r.recv_u.at[pl.ds(base + i * EXP, EXP)], r.u_recv.at[ch * (PER_CHUNK // EXP) + i]
            )
        rows = span(ch, CHUNK_ROWS)
        came = r.recv_u[pl.ds(base, PER_CHUNK)].astype(F32)
        for half in range(2):
            cols = slice(half * 512, half * 512 + 512)
            u = came[:, half * CAP : half * CAP + CAP].reshape(CHUNK_ROWS, WIDTH // 2)
            r.u_chunk[:, cols] = u.astype(BF)
            r.u_t[cols, rows] = u.T.astype(BF)

        @pl.loop(0, WIDTH // 256)
        def _(t):
            cols = span(t, 256)
            pre = dot(r.u_chunk[...], r.w_in[:, cols], 1, 0)
            r.pre_all[rows, cols] = pre
            r.act_t[cols, rows] = (pre * jax.nn.sigmoid(pre)).T.astype(BF)

    top, bottom = pl.ds(0, WIDTH // 2), pl.ds(WIDTH // 2, WIDTH // 2)
    halves = (top, bottom)

    def reduce_send(a, n, src, dst, other):
        return remote(src, dst, r.rs_send.at[a, n], r.rs_recv.at[a, n], {"dp": other})

    def make_part(a, o, lhs, rhs):
        @pl.loop(0, 2)
        def _(t):
            rows = span(t, 512)
            r.part[a, o, rows] = dot(lhs[rows, :], rhs, 1, 0).astype(BF)

    reduces = [{}, {}]

    def reduce_direct(a, o):
        c = reduces[a]
        if o == 2:
            c[0] = reduce_send(a, 0, r.part.at[a, 2, top], r.first.at[a, 0], right)
            c[1] = reduce_send(a, 1, r.part.at[a, 2, bottom], r.first.at[a, 1], left)
        if o == 1:
            c[2] = reduce_send(a, 2, r.part.at[a, 1, bottom], r.second.at[a, 0, bottom], right)
        if o == 3:
            c[3] = reduce_send(a, 3, r.part.at[a, 3, top], r.second.at[a, 1, top], left)

    def reduce_relay(a, o):
        c = reduces[a]
        side, half, other = (0, top, right) if o == 1 else (1, bottom, left)
        c[side].wait_recv()
        r.part[a, o, half] = (
            r.part[a, o, half].astype(F32) + r.first[a, side].astype(F32)
        ).astype(BF)
        c[4 + side] = reduce_send(
            a, 4 + side, r.part.at[a, o, half], r.second.at[a, side, half], other
        )

    mine, lefts, rights = span(me_d, PART), span(left, PART), span(right, PART)
    gathers = [{}, {}]
    own = []

    def gather_send(a, n, src, where, other):
        rows, cols = where
        return remote(
            src, outs[a].at[rows, cols], r.ag_send.at[a, n], r.ag_recv.at[a, n], {"dp": other}
        )

    def reduce_end(a):
        for n in (2, 3, 4, 5):
            reduces[a][n].wait_recv()
        r.fin[a] = (
            r.part[a, 0].astype(F32) + r.second[a, 0].astype(F32) + r.second[a, 1].astype(F32)
        ).astype(BF)
        g = gathers[a]
        g[0] = gather_send(a, 0, r.fin.at[a, top], (top, mine), right)
        g[1] = gather_send(a, 1, r.fin.at[a, bottom], (bottom, mine), left)
        g[2] = gather_send(a, 2, r.fin.at[a, bottom], (bottom, mine), right)
        g[3] = gather_send(a, 3, r.fin.at[a, top], (top, mine), left)
        copy = pltpu.make_async_copy(r.fin.at[a], outs[a].at[:, mine], r.own_sem.at[a])
        copy.start()
        own.append(copy)

    def gather_on(a):
        g = gathers[a]
        g[0].wait_recv()
        g[4] = gather_send(a, 4, outs[a].at[top, lefts], (top, lefts), right)
        g[1].wait_recv()
        g[5] = gather_send(a, 5, outs[a].at[bottom, rights], (bottom, rights), left)

    others = pl.ds(1, PEERS - 1)
    for n, o in enumerate(ORDER):
        member = lax.rem(me_d + o, DP)
        wait_bytes(r.recv_s.at[n, others], r.s_recv.at[n])
        came = r.recv_s[n].astype(F32)
        for half in range(2):
            r.s_all[:, span(2 * member + half, 128)] = (
                came[:, half * CAP : half * CAP + CAP].reshape(ROWS, 128).astype(BF)
            )
        make_part(0, o, r.act_t, r.s_all[:, span(member, PART)])
        reduce_direct(0, o)
        if o in (1, 3):
            reduce_relay(0, o)

    lane128 = iota((CHUNK_ROWS, 128), 1)
    slot128 = iota((CHUNK_ROWS, 128), 0) % CAP

    def give_back(j, k, xo):
        remote(r.bsend.at[j], r.brecv.at[j], r.b_send, r.b_recv, behind(k, xo))
        remote(r.hsend.at[j], r.hrecv.at[j], r.h_send, r.h_recv, behind(k, xo))

    @pl.loop(0, CHUNKS)
    def _(ch):
        base = ch * PER_CHUNK
        rows = span(ch, CHUNK_ROWS)
        peers = pl.ds(base, PER_CHUNK)

        def hidden(t, total):
            cols = span(t, 256)
            grad = dot(r.s_all[rows], r.w_out[cols, :], 1, 1)
            pre = r.pre_all[rows, cols]
            sigma = jax.nn.sigmoid(pre)
            r.gp_all[rows, cols] = (grad * sigma * (1.0 + pre * (1.0 - sigma))).astype(BF)
            return total + jnp.sum(pre * sigma * grad, axis=1, keepdims=True)

        total = lax.fori_loop(0, WIDTH // 256, hidden, jnp.zeros((CHUNK_ROWS, 1), F32))
        spread = jnp.where(lane128 == slot128, total, 0.0)
        r.hsend[peers] = jnp.sum(spread.reshape(PER_CHUNK, CAP, 128), axis=1, keepdims=True)

        @pl.loop(0, 2)
        def _(t):
            lo, hi = span(t, 256), span(t + 2, 256)
            first = dot(r.gp_all[rows], r.w_in[lo, :], 1, 1).reshape(PER_CHUNK, CAP, 256)
            last = dot(r.gp_all[rows], r.w_in[hi, :], 1, 1).reshape(PER_CHUNK, CAP, 256)
            r.bsend[peers, :, lo] = jnp.concatenate([first, last], axis=1).astype(BF)

        @pl.when(ch == 0)
        def _():
            r.brecv[0] = r.bsend[0]
            r.hrecv[0] = r.hsend[0]
            for j in range(1, EXP):
                give_back(j, 0, j)

        @pl.when(ch > 0)
        def _():
            for i in range(EXP):
                give_back(base + i, *hop(base + i))

        @pl.loop(EXP, PER_CHUNK)
        def _(i):
            give_back(base + i, *hop(base + i))

    for o in ORDER:
        make_part(1, o, r.u_t, r.gp_all[:, span(lax.rem(me_d + o, DP), PART)])
        reduce_direct(1, o)
    reduce_end(0)

    kv_copies[0].wait_recv()
    kv_copies[1].wait_recv()
    seg_past = r.seg_prev[...] == row8
    augment(past, features(seg_past, listed(group_of), -FAR, 0.0))

    def softmax(b, carry):
        rows = span(b, QROWS)
        window = pl.ds(pl.multiple_of(b * QROWS, QROWS), WINDOW)
        for h in range(4):
            score = dot(r.q_aug[h, rows], r.k_aug[h, window], 1, 1)
            weight = jnp.exp(score - jnp.max(score, axis=1, keepdims=True))
            r.probs[h, rows] = (
                weight * (1.0 / jnp.sum(weight, axis=1, keepdims=True))
            ).astype(BF)
        return carry

    lax.fori_loop(0, BLOCKS // 2, softmax, 0)
    reduce_relay(1, 1)
    reduce_relay(1, 3)
    lax.fori_loop(BLOCKS // 2, BLOCKS, softmax, 0)
    gather_on(0)

    wait_bytes(r.brecv.at[others], r.b_recv)
    back = r.brecv[...].reshape(PEERS * BLOCK, WIDTH // 2)
    for half in range(2):
        cols = slice(half * 512, half * 512 + 512)
        r.dres[:, cols] = (
            r.z_own[:, cols].astype(F32)
            + dot(r.pick[half * TOKENS : (half + 1) * TOKENS, :], back, 1, 0)
        ).astype(BF)
    my_rows = span(me_x, TOKENS)
    do_copies = []
    for o in range(1, EXP):
        px = lax.rem(me_x + o, EXP)
        do_copies.append(
            remote(
                r.dres.at[:, span(px, LOCAL)],
                r.do_all.at[my_rows],
                r.do_send.at[o - 1],
                r.do_recv.at[o - 1],
                {"exp": px},
            )
        )
    r.do_all[my_rows] = r.dres[:, span(me_x, LOCAL)]
    wait_bytes(r.hrecv.at[others], r.h_recv)
    sums = jnp.sum(r.hrecv[...], axis=1)
    lane_s = iota((TOKENS, 128), 1)
    for t in range(2):
        chosen = dot(named[t], sums, 1, 0, lax.Precision.HIGHEST)
        value = jnp.sum(jnp.where(lane_s == slot[t], chosen, 0.0), axis=1, keepdims=True)
        r.dgate[t : t + 1, :] = as_row(value / gates[t]).astype(BF)
    reduce_end(1)
    kv_copies[2].wait_recv()
    for c in do_copies:
        c.wait_recv()

    def backward(b, carry):
        rows = span(b, QROWS)
        window = pl.ds(pl.multiple_of(b * QROWS, QROWS), WINDOW)
        for hp in range(2):
            tile = slice(hp * 128, hp * 128 + 128)
            do_t = r.do_all[rows, tile]
            v_t = r.v_all[window, tile]
            k_t = r.k_all[window, tile]
            all_p, all_s, all_d, all_q, dq = [], [], [], [], []
            for e in range(2):
                keep = low_q if e == 0 else jnp.logical_not(low_q)
                do_e = jnp.where(keep, do_t, none)
                probs = r.probs[2 * hp + e, rows]
                weight = probs.astype(F32)
                grad = dot(do_e, v_t, 1, 1)
                delta = jnp.sum(weight * grad, axis=1, keepdims=True)
                dscore = (weight * (grad - delta)).astype(BF)
                dq.append(dot(dscore, k_t, 1, 0))
                all_p.append(probs)
                all_s.append(dscore)
                all_d.append(do_e)
                all_q.append(jnp.where(keep, r.q_aug[2 * hp + e, rows], none))
            r.dq[rows, tile] = (jnp.where(low_q, dq[0], dq[1]) * 0.125).astype(BF)
            r.acc_k[window, tile] += dot(
                jnp.concatenate(all_s, axis=0), jnp.concatenate(all_q, axis=0), 0, 0
            )
            r.acc_v[window, tile] += dot(
                jnp.concatenate(all_p, axis=0), jnp.concatenate(all_d, axis=0), 0, 0
            )
        return carry

    lax.fori_loop(0, BLOCKS, backward, 0)
    r.over[0] = r.acc_k[:FRAMES].astype(BF)
    r.over[1] = r.acc_v[:FRAMES].astype(BF)
    returned = [
        remote(r.over.at[i], r.came.at[i], r.ret_send.at[i], r.ret_recv.at[i], {"ctx": prior})
        for i in range(2)
    ]
    gather_on(1)
    returned[0].wait_recv()
    r.dk[...] = (r.acc_k[FRAMES:] + r.came[0].astype(F32)).astype(BF)
    returned[1].wait_recv()
    r.dv[...] = (r.acc_v[FRAMES:] + r.came[1].astype(F32)).astype(BF)
    for c in own:
        c.wait()
    for a in range(2):
        for n in (2, 3, 4, 5):
            gathers[a][n].wait_recv()
        for n in range(6):
            gathers[a][n].wait_send()
            reduces[a][n].wait_send()
    for c in do_copies + kv_copies + returned:
        c.wait_send()
    wait_bytes(r.send_u.at[others], r.u_send)
    for n in range(DP):
        wait_bytes(r.send_s.at[n, others], r.s_send.at[n])
    wait_bytes(r.bsend.at[others], r.b_send)
    wait_bytes(r.hsend.at[others], r.h_send)


PIECES = [(name, rows) for name in ("gout", "gin") for rows in range(0, WIDTH, 256)] + [
    (name, None) for name in ("dres", "dq", "dk", "dv", "dgate")
]


def deliver_kernel(*refs):
    n = len(OUTPUTS)
    sources, targets = dict(zip(OUTPUTS, refs)), dict(zip(OUTPUTS, refs[n:]))
    buffers = dict(zip(OUTPUTS, refs[2 * n :]))
    get_sem, put_sem = refs[3 * n :]

    def view(ref, rows):
        return ref if rows is None else ref.at[pl.ds(rows, 256)]

    gets, puts = [], []
    for i, (name, rows) in enumerate(PIECES):
        source, buffer, target = (
            view(group[name], rows) for group in (sources, buffers, targets)
        )
        gets.append(pltpu.make_async_copy(source, buffer, get_sem.at[i]))
        puts.append(pltpu.make_async_copy(buffer, target, put_sem.at[i]))
    for get in gets:
        get.start()
    for get, put in zip(gets, puts):
        get.wait()
        put.start()
    for put in puts:
        put.wait()


def layer(*args):
    vmem = pl.BlockSpec(memory_space=pltpu.VMEM)
    anywhere = pl.BlockSpec(memory_space=pl.ANY)
    frames = jax.ShapeDtypeStruct((FRAMES, LOCAL), BF)
    weight = jax.ShapeDtypeStruct((WIDTH, WIDTH), BF)
    shapes = (
        frames,
        frames,
        frames,
        jax.ShapeDtypeStruct((TOKENS, WIDTH), BF),
        jax.ShapeDtypeStruct((2, TOKENS), BF),
        weight,
        weight,
    )
    results = pl.pallas_call(
        layer_kernel,
        out_shape=shapes,
        in_specs=[anywhere] * len(INPUTS),
        out_specs=(vmem,) * 5 + (anywhere,) * 2,
        scratch_shapes=list(SCRATCH.values()),
        compiler_params=pltpu.CompilerParams(
            collective_id=0, has_side_effects=True, vmem_limit_bytes=VMEM_BYTES
        ),
        name="layer",
    )(*args)
    return pl.pallas_call(
        deliver_kernel,
        out_shape=shapes,
        in_specs=[anywhere] * len(OUTPUTS),
        out_specs=(anywhere,) * len(OUTPUTS),
        scratch_shapes=[pltpu.VMEM(s.shape, s.dtype) for s in shapes]
        + [DMA((len(PIECES),)), DMA((len(PIECES),))],
        compiler_params=pltpu.CompilerParams(vmem_limit_bytes=VMEM_BYTES),
        name="deliver",
    )(*results)


def local(
    queries,
    key_rows,
    value_rows,
    segments,
    left_blocks,
    moe_input,
    out_grad,
    expert_ids,
    gate_weights,
    expert_in,
    expert_out,
):
    dq, dk, dv, d_residual, d_gates, grad_out, grad_in = layer(
        queries[0],
        key_rows[0],
        value_rows[0],
        segments,
        jnp.transpose(left_blocks, (2, 0, 1)),
        moe_input[0],
        out_grad[0],
        expert_ids[0].T,
        gate_weights[0].T,
        expert_in[0],
        expert_out[0],
    )
    return (
        dq[None],
        dk[None],
        dv[None],
        d_residual[None],
        d_gates.T[None],
        grad_in[None],
        grad_out[None],
    )


def solution(mesh):
    assert dict(mesh.shape) == {"dp": DP, "ctx": CTX, "exp": EXP}
    return jax.shard_map(
        local,
        mesh=mesh,
        in_specs=(
            P("dp", "ctx", "exp"),
            P("dp", "ctx", "exp"),
            P("dp", "ctx", "exp"),
            P("dp", "ctx"),
            P("dp", "ctx", None),
            P("dp", ("ctx", "exp"), None),
            P("dp", ("ctx", "exp"), None),
            P("dp", ("ctx", "exp"), None),
            P("dp", ("ctx", "exp"), None),
            P(("ctx", "exp"), None, None),
            P(("ctx", "exp"), None, None),
        ),
        out_specs=(
            P("dp", "ctx", "exp"),
            P("dp", "ctx", "exp"),
            P("dp", "ctx", "exp"),
            P("dp", ("ctx", "exp"), None),
            P("dp", ("ctx", "exp"), None),
            P(("ctx", "exp"), None, None),
            P(("ctx", "exp"), None, None),
        ),
        check_vma=False,
    )
```

```python
import types

import jax
import jax.numpy as jnp
from jax import lax
from jax.experimental import pallas as pl
from jax.experimental.pallas import tpu as pltpu
from jax.sharding import PartitionSpec as P

MESH = pl.DeviceIdType.MESH
BF = jnp.bfloat16
F32 = jnp.float32
I32 = jnp.int32

DP, CTX, EXP = 4, 16, 4
PEERS = CTX * EXP
HALF = CTX // 2
CAP = 8
BLOCK = 2 * CAP
TOKENS = 128
WIDTH = 1024
CHUNKS = 4
PER_CHUNK = PEERS // CHUNKS
CHUNK_ROWS = PER_CHUNK * CAP
ROWS = PEERS * CAP
OTHERS = DP - 1
OTHER_ROWS = OTHERS * CHUNK_ROWS
STEPS = PER_CHUNK // EXP
GROUP = 64
GROUPS = 8
FRAMES = 512
LOCAL = 256
QROWS = 128
BLOCKS = FRAMES // QROWS
WINDOW = FRAMES + QROWS
FAR = 32768.0
VMEM_BYTES = 63 * 1024 * 1024


def dot(a, b, ca, cb, precision=None):
    return lax.dot_general(
        a, b, (((ca,), (cb,)), ((), ())), preferred_element_type=F32, precision=precision
    )


def wait_bytes(ref, sem):
    pltpu.make_async_copy(ref, ref, sem).wait()


def span(index, size):
    return pl.ds(pl.multiple_of(index * size, size), size)


def hop(j):
    s = j // EXP
    return HALF + (2 * (s % 2) - 1) * (s // 2), j % EXP


def iota(shape, dim):
    return lax.broadcasted_iota(I32, shape, dim)


def column(row):
    n = row.shape[1]
    same = iota((n, n), 0) == iota((n, n), 1)
    return jnp.sum(jnp.where(same, row, jnp.zeros_like(row)), axis=1, keepdims=True)


def as_row(col):
    n = col.shape[0]
    same = iota((n, n), 0) == iota((n, n), 1)
    return jnp.sum(jnp.where(same, col, jnp.zeros_like(col)), axis=0, keepdims=True)


INPUTS = ("q", "k", "v", "seg", "lists", "x", "z", "ids", "gate", "win", "wout")
OUTPUTS = ("dq", "dk", "dv", "dres", "dgate", "gout", "gin")
DMA = pltpu.SemaphoreType.DMA
LOADS = ("ids", "gate", "x", "z", "win", "wout", "q", "seg", "lists", "k", "v")
SCRATCH = dict(
    q_own=pltpu.VMEM((FRAMES, LOCAL), BF),
    seg_own=pltpu.VMEM((1, FRAMES), I32),
    lists_own=pltpu.VMEM((3, 1, GROUPS), I32),
    x_own=pltpu.VMEM((TOKENS, WIDTH), BF),
    z_own=pltpu.VMEM((TOKENS, WIDTH), BF),
    ids_own=pltpu.VMEM((2, TOKENS), I32),
    gate_own=pltpu.VMEM((2, TOKENS), BF),
    w_in=pltpu.VMEM((WIDTH, WIDTH), BF),
    w_out=pltpu.VMEM((WIDTH, WIDTH), BF),
    pick_t=pltpu.VMEM((PEERS * BLOCK, 2 * TOKENS), BF),
    gated_t=pltpu.VMEM((PEERS * BLOCK, 2 * TOKENS), BF),
    pick=pltpu.VMEM((2 * TOKENS, PEERS * BLOCK), BF),
    xx=pltpu.VMEM((2 * TOKENS, WIDTH // 2), BF),
    zz=pltpu.VMEM((2 * TOKENS, WIDTH // 2), BF),
    send_u=pltpu.VMEM((PEERS, BLOCK, WIDTH // 2), BF),
    recv_u=pltpu.VMEM((PEERS, BLOCK, WIDTH // 2), BF),
    send_s=pltpu.VMEM((PEERS, BLOCK, WIDTH // 2), BF),
    recv_s=pltpu.VMEM((PEERS, BLOCK, WIDTH // 2), BF),
    gath=pltpu.VMEM((2, OTHERS, PEERS, BLOCK, WIDTH // 2), BF),
    more=pltpu.VMEM((OTHER_ROWS, WIDTH), BF),
    more_gp=pltpu.VMEM((OTHER_ROWS, WIDTH), BF),
    more_u_t=pltpu.VMEM((CHUNKS, WIDTH, OTHER_ROWS), BF),
    more_act_t=pltpu.VMEM((CHUNKS, WIDTH, OTHER_ROWS), BF),
    more_pre=pltpu.VMEM((CHUNKS, OTHER_ROWS, WIDTH), BF),
    acc_in=pltpu.VMEM((WIDTH, WIDTH), F32),
    acc_out=pltpu.VMEM((WIDTH, WIDTH), F32),
    u_chunk=pltpu.VMEM((CHUNK_ROWS, WIDTH), BF),
    u_t=pltpu.VMEM((WIDTH, ROWS), BF),
    act_t=pltpu.VMEM((WIDTH, ROWS), BF),
    pre_all=pltpu.VMEM((ROWS, WIDTH), F32),
    s_all=pltpu.VMEM((ROWS, WIDTH), BF),
    gp_all=pltpu.VMEM((ROWS, WIDTH), BF),
    brecv=pltpu.VMEM((PEERS, BLOCK, WIDTH // 2), BF),
    hsend=pltpu.VMEM((PEERS, 1, 128), F32),
    hrecv=pltpu.VMEM((PEERS, 1, 128), F32),
    k_all=pltpu.VMEM((2 * FRAMES, LOCAL), BF),
    v_all=pltpu.VMEM((2 * FRAMES, LOCAL), BF),
    seg_prev=pltpu.VMEM((1, FRAMES), I32),
    do_all=pltpu.VMEM((FRAMES, LOCAL), BF),
    k_aug=pltpu.VMEM((4, 2 * FRAMES, 128), BF),
    q_aug=pltpu.VMEM((4, FRAMES, 128), BF),
    probs=pltpu.VMEM((4, FRAMES, WINDOW), BF),
    acc_k=pltpu.VMEM((2 * FRAMES, LOCAL), F32),
    acc_v=pltpu.VMEM((2 * FRAMES, LOCAL), F32),
    over=pltpu.VMEM((2, FRAMES, LOCAL), BF),
    came=pltpu.VMEM((2, FRAMES, LOCAL), BF),
    load_sem=DMA((len(LOADS),)),
    u_send=DMA,
    u_recv=DMA((CTX,)),
    s_send=DMA,
    s_recv=DMA((CTX,)),
    b_send=DMA,
    b_recv=DMA,
    h_send=DMA,
    h_recv=DMA,
    ag_send=DMA((2, CHUNKS, 4)),
    ag_recv=DMA((2, CHUNKS, 4)),
    kv_send=DMA((3,)),
    kv_recv=DMA((3,)),
    do_send=DMA((EXP - 1,)),
    do_recv=DMA((EXP - 1,)),
    ret_send=DMA((BLOCKS, 2)),
    ret_recv=DMA((BLOCKS, 2)),
)


def layer_kernel(*refs):
    r = types.SimpleNamespace(**dict(zip(INPUTS + OUTPUTS + tuple(SCRATCH), refs)))
    me_d, me_c, me_x = lax.axis_index("dp"), lax.axis_index("ctx"), lax.axis_index("exp")
    right, left = lax.rem(me_d + 1, DP), lax.rem(me_d + DP - 1, DP)
    after, prior = lax.rem(me_c + 1, CTX), lax.rem(me_c + CTX - 1, CTX)

    targets = dict(
        ids=r.ids_own,
        gate=r.gate_own,
        x=r.x_own,
        z=r.z_own,
        win=r.w_in,
        wout=r.w_out,
        q=r.q_own,
        seg=r.seg_own,
        lists=r.lists_own,
        k=r.k_all.at[pl.ds(FRAMES, FRAMES)],
        v=r.v_all.at[pl.ds(FRAMES, FRAMES)],
    )
    loads = {
        name: pltpu.make_async_copy(getattr(r, name), targets[name], r.load_sem.at[i])
        for i, name in enumerate(LOADS)
    }
    def ahead(k, xo):
        return {"ctx": lax.rem(me_c + k, CTX), "exp": lax.rem(me_x + xo, EXP)}

    def behind(k, xo):
        return {"ctx": lax.rem(me_c - k + CTX, CTX), "exp": lax.rem(me_x - xo + EXP, EXP)}

    def remote(src, dst, ssem, rsem, target):
        copy = pltpu.make_async_remote_copy(
            src_ref=src,
            dst_ref=dst,
            send_sem=ssem,
            recv_sem=rsem,
            device_id=target,
            device_id_type=MESH,
        )
        copy.start()
        return copy

    barrier = pltpu.get_barrier_semaphore()
    for name in LOADS[:4]:
        loads[name].start()
    columns_of = [lax.rem(me_c + k, CTX) for k in range(CTX)]
    rows_of = [lax.rem(me_x + xo, EXP) for xo in range(EXP)]
    for other in (left, right):
        pl.semaphore_signal(barrier, inc=1, device_id={"dp": other}, device_id_type=MESH)
    for k in range(CTX):
        for xo in range(EXP):
            if k or xo:
                pl.semaphore_signal(
                    barrier,
                    inc=1,
                    device_id={"ctx": columns_of[k], "exp": rows_of[xo]},
                    device_id_type=MESH,
                )
    for name in LOADS[4:]:
        loads[name].start()

    def relative(ids):
        k = (ids // EXP - me_c + CTX) % CTX
        xo = (ids % EXP - me_x + EXP) % EXP
        s = jnp.where(k == 0, 0, jnp.where(k < HALF, CTX - 2 * k, 2 * k - CTX + 1))
        return s * EXP + xo

    loads["ids"].wait()
    expert = iota((PEERS, TOKENS), 0)
    peer_row = [relative(r.ids_own[t : t + 1, :]) for t in range(2)]
    named_t = [(peer_row[t] == expert).astype(F32) for t in range(2)]
    before = (iota((TOKENS, TOKENS), 0) < iota((TOKENS, TOKENS), 1)).astype(F32).astype(BF)
    earlier = dot((named_t[0] + named_t[1]).astype(BF), before, 1, 0)
    slot_row = [
        jnp.sum(named_t[t] * earlier, axis=0, keepdims=True).astype(I32) for t in range(2)
    ]
    place_row = [peer_row[t] * BLOCK + slot_row[t] for t in range(2)]
    loads["gate"].wait()
    gate_row = [r.gate_own[t : t + 1, :].astype(F32) for t in range(2)]
    loads["x"].wait()
    r.xx[:TOKENS] = r.x_own[:, : WIDTH // 2]
    r.xx[TOKENS:] = r.x_own[:, WIDTH // 2 :]

    @pl.loop(0, CHUNKS)
    def _(t):
        place = iota((256, TOKENS), 0) + t * 256
        for half in range(2):
            hit = [place_row[i] + half * CAP == place for i in range(2)]
            cols = slice(half * TOKENS, half * TOKENS + TOKENS)
            r.pick_t[span(t, 256), cols] = (hit[0] | hit[1]).astype(F32).astype(BF)
            r.gated_t[span(t, 256), cols] = (
                jnp.where(hit[0], gate_row[0], 0.0) + jnp.where(hit[1], gate_row[1], 0.0)
            ).astype(BF)
        rows = dot(r.pick_t[span(t, 256)], r.xx[...], 1, 0)
        r.send_u[pl.ds(t * 16, 16)] = rows.astype(BF).reshape(16, BLOCK, WIDTH // 2)

    pl.semaphore_wait(barrier, PEERS - 1 + 2)

    past = pl.ds(0, FRAMES)
    kv_copies = [
        remote(r.seg, r.seg_prev, r.kv_send.at[0], r.kv_recv.at[0], {"ctx": after}),
        remote(r.k, r.k_all.at[past], r.kv_send.at[1], r.kv_recv.at[1], {"ctx": after}),
        remote(r.v, r.v_all.at[past], r.kv_send.at[2], r.kv_recv.at[2], {"ctx": after}),
    ]

    def send_rows(j, k, xo):
        remote(r.send_u.at[j], r.recv_u.at[j], r.u_send, r.u_recv.at[j // EXP], ahead(k, xo))

    @pl.loop(EXP, PEERS)
    def _(j):
        send_rows(j, *hop(j))

    for j in range(1, EXP):
        send_rows(j, 0, j)
    r.recv_u[0] = r.send_u[0]

    loads["z"].wait()
    r.zz[:TOKENS] = r.z_own[:, : WIDTH // 2]
    r.zz[TOKENS:] = r.z_own[:, WIDTH // 2 :]

    @pl.loop(0, CHUNKS)
    def _(t):
        rows = dot(r.gated_t[span(t, 256)], r.zz[...], 1, 0)
        r.send_s[pl.ds(t * 16, 16)] = rows.astype(BF).reshape(16, BLOCK, WIDTH // 2)

    def send_grads(j, k, xo):
        remote(r.send_s.at[j], r.recv_s.at[j], r.s_send, r.s_recv.at[j // EXP], ahead(k, xo))

    @pl.loop(EXP, PEERS)
    def _(j):
        send_grads(j, *hop(j))

    for j in range(1, EXP):
        send_grads(j, 0, j)
    r.recv_s[0] = r.send_s[0]

    peer = [column(peer_row[t]) for t in range(2)]
    slot = [column(slot_row[t]) for t in range(2)]
    gates = [column(gate_row[t]) for t in range(2)]
    named = [(peer[t] == iota((TOKENS, PEERS), 1)).astype(F32) for t in range(2)]
    lane_q = iota((TOKENS, PEERS * BLOCK), 1)
    for half in range(2):
        hit = [peer[t] * BLOCK + slot[t] + half * CAP == lane_q for t in range(2)]
        r.pick[pl.ds(half * TOKENS, TOKENS)] = (hit[0] | hit[1]).astype(F32).astype(BF)

    for name in ("q", "seg", "lists", "k", "v"):
        loads[name].wait()
    kinds = 2 * GROUPS
    lane_f, row_f = iota((kinds, 128), 1), iota((kinds, 128), 0)
    place = ((lane_f == row_f) | (lane_f == row_f + 64)).astype(F32).astype(BF)
    row8 = iota((8, FRAMES), 0)
    group_of = iota((8, FRAMES), 1) // GROUP
    moved = []
    for j in range(3):
        lists = column(r.lists_own[j])
        moved.append(jnp.where(lists >= 0, lists - (me_c - 1) * GROUPS, -1))

    def listed(groups):
        return (moved[0] == groups) | (moved[1] == groups) | (moved[2] == groups)

    def features(segment, group, miss, match):
        both = jnp.concatenate(
            [jnp.where(segment, match, miss), jnp.where(group, match, miss)], axis=0
        ).astype(BF)
        return dot(both, place, 0, 0).astype(BF)

    low = iota((FRAMES, 128), 1) < 64
    low_q = iota((QROWS, 128), 1) < 64
    none = jnp.zeros((QROWS, 128), BF)

    def augment(part, feat):
        for hp in range(2):
            k_t = r.k_all[part, hp * 128 : hp * 128 + 128]
            r.k_aug[2 * hp, part] = jnp.where(low, k_t, feat)
            r.k_aug[2 * hp + 1, part] = jnp.where(low, feat, k_t)

    seg_own = r.seg_own[...] == row8
    feat_q = features(seg_own, group_of == row8, 0.0, 1.0)
    for hp in range(2):
        q_t = (r.q_own[:, hp * 128 : hp * 128 + 128].astype(F32) * 0.125).astype(BF)
        r.q_aug[2 * hp] = jnp.where(low, q_t, feat_q)
        r.q_aug[2 * hp + 1] = jnp.where(low, feat_q, q_t)
    list_own = listed(group_of + GROUPS) | (group_of == row8)
    augment(pl.ds(FRAMES, FRAMES), features(seg_own, list_own, -FAR, 0.0))
    r.acc_k[...] = jnp.zeros_like(r.acc_k)
    r.acc_v[...] = jnp.zeros_like(r.acc_v)

    ours = (r.recv_u, r.recv_s)

    def gather(a, ch, n):
        chunk = pl.ds(ch * PER_CHUNK, PER_CHUNK)
        near = pl.ds(ch * PER_CHUNK, PER_CHUNK // 2)
        far = pl.ds(ch * PER_CHUNK + PER_CHUNK // 2, PER_CHUNK // 2)
        src, dst, other = (
            (ours[a].at[chunk], r.gath.at[a, 0, chunk], right),
            (ours[a].at[chunk], r.gath.at[a, 1, chunk], left),
            (r.gath.at[a, 0, near], r.gath.at[a, 2, near], right),
            (r.gath.at[a, 1, far], r.gath.at[a, 2, far], left),
        )[n]
        return pltpu.make_async_remote_copy(
            src_ref=src,
            dst_ref=dst,
            send_sem=r.ag_send.at[a, ch, n],
            recv_sem=r.ag_recv.at[a, ch, n],
            device_id={"dp": other},
            device_id_type=MESH,
        )

    def gather_own(a, ch):
        gather(a, ch, 0).start()
        gather(a, ch, 1).start()

    def gather_on(a, ch):
        gather(a, ch, 0).wait_recv()
        gather(a, ch, 2).start()
        gather(a, ch, 1).wait_recv()
        gather(a, ch, 3).start()

    def gather_wait(a, ch):
        gather(a, ch, 2).wait_recv()
        gather(a, ch, 3).wait_recv()

    def wait_chunk(buffer, sems, ch):
        @pl.when(ch == 0)
        def _():
            wait_bytes(buffer.at[pl.ds(1, EXP - 1)], sems.at[0])

        @pl.when(ch > 0)
        def _():
            wait_bytes(buffer.at[pl.ds(ch * PER_CHUNK, EXP)], sems.at[ch * STEPS])

        for i in range(1, STEPS):
            wait_bytes(buffer.at[pl.ds(ch * PER_CHUNK + i * EXP, EXP)], sems.at[ch * STEPS + i])

    def unpack(blocks):
        came = blocks.astype(F32)
        count = came.shape[0] * CAP
        return [
            came[:, half * CAP : half * CAP + CAP].reshape(count, WIDTH // 2) for half in range(2)
        ]

    def half_cols(half):
        return slice(half * 512, half * 512 + 512)

    def chunk_of_others(a, ch):
        blocks = r.gath[a, :, pl.ds(ch * PER_CHUNK, PER_CHUNK)]
        return blocks.reshape(OTHERS * PER_CHUNK, BLOCK, WIDTH // 2)

    def more_rows(ch):
        for half, u in enumerate(unpack(chunk_of_others(0, ch))):
            r.more[:, half_cols(half)] = u.astype(BF)
            r.more_u_t[ch, half_cols(half)] = u.T.astype(BF)

        @pl.loop(0, WIDTH // 256)
        def _(t):
            cols = span(t, 256)
            pre = dot(r.more[...], r.w_in[:, cols], 1, 0)
            r.more_pre[ch, :, cols] = pre.astype(BF)
            r.more_act_t[ch, cols] = (pre * jax.nn.sigmoid(pre)).T.astype(BF)

    def more_grads(ch):
        for half, s in enumerate(unpack(chunk_of_others(1, ch))):
            r.more[:, half_cols(half)] = s.astype(BF)

        @pl.loop(0, WIDTH // 256)
        def _(t):
            cols = span(t, 256)
            grad = dot(r.more[...], r.w_out[cols, :], 1, 1)
            pre = r.more_pre[ch, :, cols].astype(F32)
            sigma = jax.nn.sigmoid(pre)
            r.more_gp[:, cols] = (grad * sigma * (1.0 + pre * (1.0 - sigma))).astype(BF)

        @pl.loop(0, WIDTH // 256)
        def _(t):
            rows = span(t, 256)
            r.acc_in[rows] += dot(r.more_u_t[ch, rows], r.more_gp[...], 1, 0)
            r.acc_out[rows] += dot(r.more_act_t[ch, rows], r.more[...], 1, 0)

    def softmax(b):
        rows = span(b, QROWS)
        window = pl.ds(pl.multiple_of(b * QROWS, QROWS), WINDOW)
        for h in range(4):
            score = dot(r.q_aug[h, rows], r.k_aug[h, window], 1, 1)
            weight = jnp.exp(score - jnp.max(score, axis=1, keepdims=True))
            r.probs[h, rows] = (
                weight * (1.0 / jnp.sum(weight, axis=1, keepdims=True))
            ).astype(BF)

    loads["win"].wait()
    loads["wout"].wait()

    @pl.loop(0, CHUNKS)
    def _(ch):
        wait_chunk(r.recv_u, r.u_recv, ch)
        gather_own(0, ch)
        rows = span(ch, CHUNK_ROWS)
        for half, u in enumerate(unpack(r.recv_u[pl.ds(ch * PER_CHUNK, PER_CHUNK)])):
            r.u_chunk[:, half_cols(half)] = u.astype(BF)
            r.u_t[half_cols(half), rows] = u.T.astype(BF)

        @pl.loop(0, WIDTH // 256)
        def _(t):
            cols = span(t, 256)
            pre = dot(r.u_chunk[...], r.w_in[:, cols], 1, 0)
            r.pre_all[rows, cols] = pre
            r.act_t[cols, rows] = (pre * jax.nn.sigmoid(pre)).T.astype(BF)

        @pl.when(ch >= 2)
        def _():
            gather_on(0, ch - 2)

        @pl.when(ch == 1)
        def _():
            kv_copies[0].wait_recv()
            kv_copies[1].wait_recv()
            seg_past = r.seg_prev[...] == row8
            augment(past, features(seg_past, listed(group_of), -FAR, 0.0))

        @pl.when(ch >= 1)
        def _():
            softmax(ch - 1)

    softmax(BLOCKS - 1)

    others = pl.ds(1, PEERS - 1)
    wait_bytes(r.send_u.at[others], r.u_send)
    bsend = r.send_u
    lane128 = iota((CHUNK_ROWS, 128), 1)
    slot128 = iota((CHUNK_ROWS, 128), 0) % CAP

    def give_back(j, k, xo):
        remote(bsend.at[j], r.brecv.at[j], r.b_send, r.b_recv, behind(k, xo))
        remote(r.hsend.at[j], r.hrecv.at[j], r.h_send, r.h_recv, behind(k, xo))

    @pl.loop(0, CHUNKS)
    def _(ch):
        base = ch * PER_CHUNK
        rows = span(ch, CHUNK_ROWS)
        peers = pl.ds(base, PER_CHUNK)
        wait_chunk(r.recv_s, r.s_recv, ch)
        gather_own(1, ch)
        for half, s in enumerate(unpack(r.recv_s[peers])):
            r.s_all[rows, half_cols(half)] = s.astype(BF)

        def hidden(t, total):
            cols = span(t, 256)
            grad = dot(r.s_all[rows], r.w_out[cols, :], 1, 1)
            pre = r.pre_all[rows, cols]
            sigma = jax.nn.sigmoid(pre)
            r.gp_all[rows, cols] = (grad * sigma * (1.0 + pre * (1.0 - sigma))).astype(BF)
            return total + jnp.sum(pre * sigma * grad, axis=1, keepdims=True)

        total = lax.fori_loop(0, WIDTH // 256, hidden, jnp.zeros((CHUNK_ROWS, 1), F32))
        spread = jnp.where(lane128 == slot128, total, 0.0)
        r.hsend[peers] = jnp.sum(spread.reshape(PER_CHUNK, CAP, 128), axis=1, keepdims=True)

        @pl.loop(0, 2)
        def _(t):
            lo, hi = span(t, 256), span(t + 2, 256)
            first = dot(r.gp_all[rows], r.w_in[lo, :], 1, 1).reshape(PER_CHUNK, CAP, 256)
            last = dot(r.gp_all[rows], r.w_in[hi, :], 1, 1).reshape(PER_CHUNK, CAP, 256)
            bsend[peers, :, lo] = jnp.concatenate([first, last], axis=1).astype(BF)

        @pl.when(ch == 0)
        def _():
            r.brecv[0] = bsend[0]
            r.hrecv[0] = r.hsend[0]
            for j in range(1, EXP):
                give_back(j, 0, j)

        @pl.when(ch > 0)
        def _():
            for i in range(EXP):
                give_back(base + i, *hop(base + i))

        @pl.loop(EXP, PER_CHUNK)
        def _(i):
            give_back(base + i, *hop(base + i))

        @pl.when(ch < 2)
        def _():
            gather_on(0, ch + 2)

        @pl.when(ch >= 2)
        def _():
            gather_on(1, ch - 2)

        gather_wait(0, ch)
        more_rows(ch)

    @pl.loop(0, WIDTH // 256)
    def _(t):
        rows = span(t, 256)
        r.acc_in[rows] = dot(r.u_t[rows], r.gp_all[...], 1, 0)
        r.acc_out[rows] = dot(r.act_t[rows], r.s_all[...], 1, 0)

    def other_grads(ch, carry):
        gather_wait(1, ch)
        more_grads(ch)
        return carry

    gather_on(1, 2)
    lax.fori_loop(0, 2, other_grads, 0)
    gather_on(1, 3)
    lax.fori_loop(2, 3, other_grads, 0)

    wait_bytes(r.brecv.at[others], r.b_recv)
    back = r.brecv[...].reshape(PEERS * BLOCK, WIDTH // 2)
    for half in range(2):
        cols = slice(half * 512, half * 512 + 512)
        r.dres[:, cols] = (
            r.z_own[:, cols].astype(F32)
            + dot(r.pick[half * TOKENS : (half + 1) * TOKENS, :], back, 1, 0)
        ).astype(BF)
    my_rows = span(me_x, TOKENS)
    do_copies = []
    for o in range(1, EXP):
        px = lax.rem(me_x + o, EXP)
        do_copies.append(
            remote(
                r.dres.at[:, span(px, LOCAL)],
                r.do_all.at[my_rows],
                r.do_send.at[o - 1],
                r.do_recv.at[o - 1],
                {"exp": px},
            )
        )
    r.do_all[my_rows] = r.dres[:, span(me_x, LOCAL)]
    wait_bytes(r.hrecv.at[others], r.h_recv)
    sums = jnp.sum(r.hrecv[...], axis=1)
    lane_s = iota((TOKENS, 128), 1)
    for t in range(2):
        chosen = dot(named[t], sums, 1, 0, lax.Precision.HIGHEST)
        value = jnp.sum(jnp.where(lane_s == slot[t], chosen, 0.0), axis=1, keepdims=True)
        r.dgate[t : t + 1, :] = as_row(value / gates[t]).astype(BF)
    kv_copies[2].wait_recv()
    lax.fori_loop(3, 4, other_grads, 0)
    r.gin[...] = r.acc_in[...].astype(BF)
    r.gout[...] = r.acc_out[...].astype(BF)
    for c in do_copies:
        c.wait_recv()

    def backward(b, carry):
        rows = span(b, QROWS)
        window = pl.ds(pl.multiple_of(b * QROWS, QROWS), WINDOW)
        for hp in range(2):
            tile = slice(hp * 128, hp * 128 + 128)
            do_t = r.do_all[rows, tile]
            v_t = r.v_all[window, tile]
            k_t = r.k_all[window, tile]
            all_p, all_s, all_d, all_q, dq = [], [], [], [], []
            for e in range(2):
                keep = low_q if e == 0 else jnp.logical_not(low_q)
                do_e = jnp.where(keep, do_t, none)
                probs = r.probs[2 * hp + e, rows]
                weight = probs.astype(F32)
                grad = dot(do_e, v_t, 1, 1)
                delta = jnp.sum(weight * grad, axis=1, keepdims=True)
                dscore = (weight * (grad - delta)).astype(BF)
                dq.append(dot(dscore, k_t, 1, 0))
                all_p.append(probs)
                all_s.append(dscore)
                all_d.append(do_e)
                all_q.append(jnp.where(keep, r.q_aug[2 * hp + e, rows], none))
            r.dq[rows, tile] = (jnp.where(low_q, dq[0], dq[1]) * 0.125).astype(BF)
            r.acc_k[window, tile] += dot(
                jnp.concatenate(all_s, axis=0), jnp.concatenate(all_q, axis=0), 0, 0
            )
            r.acc_v[window, tile] += dot(
                jnp.concatenate(all_p, axis=0), jnp.concatenate(all_d, axis=0), 0, 0
            )
        r.over[0, rows] = r.acc_k[rows].astype(BF)
        r.over[1, rows] = r.acc_v[rows].astype(BF)
        for i in range(2):
            give_prior(b, i).start()
        return carry

    def give_prior(b, i):
        rows = span(b, QROWS)
        return pltpu.make_async_remote_copy(
            src_ref=r.over.at[i, rows],
            dst_ref=r.came.at[i, rows],
            send_sem=r.ret_send.at[b, i],
            recv_sem=r.ret_recv.at[b, i],
            device_id={"ctx": prior},
            device_id_type=MESH,
        )

    lax.fori_loop(0, BLOCKS, backward, 0)

    @pl.loop(0, BLOCKS)
    def _(b):
        rows = span(b, QROWS)
        late = pl.ds(pl.multiple_of(FRAMES + b * QROWS, QROWS), QROWS)
        for i, (out, acc) in enumerate(((r.dk, r.acc_k), (r.dv, r.acc_v))):
            give_prior(b, i).wait_recv()
            out[rows] = (acc[late] + r.came[i, rows].astype(F32)).astype(BF)
            give_prior(b, i).wait_send()

    for a in range(2):
        for ch in range(CHUNKS):
            for n in range(4):
                gather(a, ch, n).wait_send()
    for c in do_copies + kv_copies:
        c.wait_send()
    wait_bytes(r.send_s.at[others], r.s_send)
    wait_bytes(bsend.at[others], r.b_send)
    wait_bytes(r.hsend.at[others], r.h_send)


PIECES = [(name, rows) for name in ("gout", "gin") for rows in range(0, WIDTH, 256)] + [
    (name, None) for name in ("dres", "dq", "dk", "dv", "dgate")
]


def deliver_kernel(*refs):
    n = len(OUTPUTS)
    sources, targets = dict(zip(OUTPUTS, refs)), dict(zip(OUTPUTS, refs[n:]))
    buffers = dict(zip(OUTPUTS, refs[2 * n :]))
    get_sem, put_sem = refs[3 * n :]

    def view(ref, rows):
        return ref if rows is None else ref.at[pl.ds(rows, 256)]

    gets, puts = [], []
    for i, (name, rows) in enumerate(PIECES):
        source, buffer, target = (
            view(group[name], rows) for group in (sources, buffers, targets)
        )
        gets.append(pltpu.make_async_copy(source, buffer, get_sem.at[i]))
        puts.append(pltpu.make_async_copy(buffer, target, put_sem.at[i]))
    for get in gets:
        get.start()
    for get, put in zip(gets, puts):
        get.wait()
        put.start()
    for put in puts:
        put.wait()


def layer(*args):
    vmem = pl.BlockSpec(memory_space=pltpu.VMEM)
    anywhere = pl.BlockSpec(memory_space=pl.ANY)
    frames = jax.ShapeDtypeStruct((FRAMES, LOCAL), BF)
    weight = jax.ShapeDtypeStruct((WIDTH, WIDTH), BF)
    shapes = (
        frames,
        frames,
        frames,
        jax.ShapeDtypeStruct((TOKENS, WIDTH), BF),
        jax.ShapeDtypeStruct((2, TOKENS), BF),
        weight,
        weight,
    )
    results = pl.pallas_call(
        layer_kernel,
        out_shape=shapes,
        in_specs=[anywhere] * len(INPUTS),
        out_specs=(vmem,) * 7,
        scratch_shapes=list(SCRATCH.values()),
        compiler_params=pltpu.CompilerParams(
            collective_id=0, has_side_effects=True, vmem_limit_bytes=VMEM_BYTES
        ),
        name="layer",
    )(*args)
    return pl.pallas_call(
        deliver_kernel,
        out_shape=shapes,
        in_specs=[anywhere] * len(OUTPUTS),
        out_specs=(anywhere,) * len(OUTPUTS),
        scratch_shapes=[pltpu.VMEM(s.shape, s.dtype) for s in shapes]
        + [DMA((len(PIECES),)), DMA((len(PIECES),))],
        compiler_params=pltpu.CompilerParams(vmem_limit_bytes=VMEM_BYTES),
        name="deliver",
    )(*results)


def local(
    queries,
    key_rows,
    value_rows,
    segments,
    left_blocks,
    moe_input,
    out_grad,
    expert_ids,
    gate_weights,
    expert_in,
    expert_out,
):
    dq, dk, dv, d_residual, d_gates, grad_out, grad_in = layer(
        queries[0],
        key_rows[0],
        value_rows[0],
        segments,
        jnp.transpose(left_blocks, (2, 0, 1)),
        moe_input[0],
        out_grad[0],
        expert_ids[0].T,
        gate_weights[0].T,
        expert_in[0],
        expert_out[0],
    )
    return (
        dq[None],
        dk[None],
        dv[None],
        d_residual[None],
        d_gates.T[None],
        grad_in[None],
        grad_out[None],
    )


def solution(mesh):
    assert dict(mesh.shape) == {"dp": DP, "ctx": CTX, "exp": EXP}
    return jax.shard_map(
        local,
        mesh=mesh,
        in_specs=(
            P("dp", "ctx", "exp"),
            P("dp", "ctx", "exp"),
            P("dp", "ctx", "exp"),
            P("dp", "ctx"),
            P("dp", "ctx", None),
            P("dp", ("ctx", "exp"), None),
            P("dp", ("ctx", "exp"), None),
            P("dp", ("ctx", "exp"), None),
            P("dp", ("ctx", "exp"), None),
            P(("ctx", "exp"), None, None),
            P(("ctx", "exp"), None, None),
        ),
        out_specs=(
            P("dp", "ctx", "exp"),
            P("dp", "ctx", "exp"),
            P("dp", "ctx", "exp"),
            P("dp", ("ctx", "exp"), None),
            P("dp", ("ctx", "exp"), None),
            P(("ctx", "exp"), None, None),
            P(("ctx", "exp"), None, None),
        ),
        check_vma=False,
    )
```

```python
import types

import jax
import jax.numpy as jnp
from jax import lax
from jax.experimental import pallas as pl
from jax.experimental.pallas import tpu as pltpu
from jax.sharding import PartitionSpec as P

MESH = pl.DeviceIdType.MESH
BF = jnp.bfloat16
F32 = jnp.float32
I32 = jnp.int32

DP, CTX, EXP = 4, 16, 4
PEERS = CTX * EXP
HALF = CTX // 2
CAP = 8
BLOCK = 2 * CAP
TOKENS = 128
WIDTH = 1024
CHUNKS = 4
PER_CHUNK = PEERS // CHUNKS
CHUNK_ROWS = PER_CHUNK * CAP
ROWS = PEERS * CAP
OTHERS = DP - 1
OTHER_ROWS = OTHERS * CHUNK_ROWS
STEPS = PER_CHUNK // EXP
GROUP = 64
GROUPS = 8
FRAMES = 512
LOCAL = 256
QROWS = 128
BLOCKS = FRAMES // QROWS
WINDOW = FRAMES + QROWS
FAR = 32768.0
VMEM_BYTES = 63 * 1024 * 1024


def dot(a, b, ca, cb, precision=None):
    return lax.dot_general(
        a, b, (((ca,), (cb,)), ((), ())), preferred_element_type=F32, precision=precision
    )


def wait_bytes(ref, sem):
    pltpu.make_async_copy(ref, ref, sem).wait()


def span(index, size):
    return pl.ds(pl.multiple_of(index * size, size), size)


def hop(j):
    s = j // EXP
    return HALF + (2 * (s % 2) - 1) * (s // 2), j % EXP


def iota(shape, dim):
    return lax.broadcasted_iota(I32, shape, dim)


def column(row):
    n = row.shape[1]
    same = iota((n, n), 0) == iota((n, n), 1)
    return jnp.sum(jnp.where(same, row, jnp.zeros_like(row)), axis=1, keepdims=True)


def as_row(col):
    n = col.shape[0]
    same = iota((n, n), 0) == iota((n, n), 1)
    return jnp.sum(jnp.where(same, col, jnp.zeros_like(col)), axis=0, keepdims=True)


INPUTS = ("q", "k", "v", "seg", "lists", "x", "z", "ids", "gate", "win", "wout")
OUTPUTS = ("dq", "dk", "dv", "dres", "dgate", "gout", "gin")
DMA = pltpu.SemaphoreType.DMA
LOADS = ("ids", "gate", "x", "z", "win", "wout", "q", "seg", "lists", "k", "v")
SCRATCH = dict(
    q_own=pltpu.VMEM((FRAMES, LOCAL), BF),
    seg_own=pltpu.VMEM((1, FRAMES), I32),
    lists_own=pltpu.VMEM((3, 1, GROUPS), I32),
    x_own=pltpu.VMEM((TOKENS, WIDTH), BF),
    z_own=pltpu.VMEM((TOKENS, WIDTH), BF),
    ids_own=pltpu.VMEM((2, TOKENS), I32),
    gate_own=pltpu.VMEM((2, TOKENS), BF),
    w_in=pltpu.VMEM((WIDTH, WIDTH), BF),
    w_out=pltpu.VMEM((WIDTH, WIDTH), BF),
    pick_t=pltpu.VMEM((PEERS * BLOCK, 2 * TOKENS), BF),
    gated_t=pltpu.VMEM((PEERS * BLOCK, 2 * TOKENS), BF),
    pick=pltpu.VMEM((2 * TOKENS, PEERS * BLOCK), BF),
    xx=pltpu.VMEM((2 * TOKENS, WIDTH // 2), BF),
    zz=pltpu.VMEM((2 * TOKENS, WIDTH // 2), BF),
    send_u=pltpu.VMEM((PEERS, BLOCK, WIDTH // 2), BF),
    recv_u=pltpu.VMEM((PEERS, BLOCK, WIDTH // 2), BF),
    send_s=pltpu.VMEM((PEERS, BLOCK, WIDTH // 2), BF),
    recv_s=pltpu.VMEM((PEERS, BLOCK, WIDTH // 2), BF),
    gath=pltpu.VMEM((2, OTHERS, PEERS, BLOCK, WIDTH // 2), BF),
    more=pltpu.VMEM((OTHER_ROWS, WIDTH), BF),
    more_gp=pltpu.VMEM((OTHER_ROWS, WIDTH), BF),
    more_u_t=pltpu.VMEM((CHUNKS, WIDTH, OTHER_ROWS), BF),
    more_act_t=pltpu.VMEM((CHUNKS, WIDTH, OTHER_ROWS), BF),
    more_pre=pltpu.VMEM((CHUNKS, OTHER_ROWS, WIDTH), BF),
    acc_in=pltpu.VMEM((WIDTH, WIDTH), F32),
    acc_out=pltpu.VMEM((WIDTH, WIDTH), F32),
    u_chunk=pltpu.VMEM((CHUNK_ROWS, WIDTH), BF),
    u_t=pltpu.VMEM((WIDTH, ROWS), BF),
    act_t=pltpu.VMEM((WIDTH, ROWS), BF),
    pre_all=pltpu.VMEM((ROWS, WIDTH), F32),
    s_all=pltpu.VMEM((ROWS, WIDTH), BF),
    gp_all=pltpu.VMEM((ROWS, WIDTH), BF),
    brecv=pltpu.VMEM((PEERS, BLOCK, WIDTH // 2), BF),
    hsend=pltpu.VMEM((PEERS, 1, 128), F32),
    hrecv=pltpu.VMEM((PEERS, 1, 128), F32),
    k_all=pltpu.VMEM((2 * FRAMES, LOCAL), BF),
    v_all=pltpu.VMEM((2 * FRAMES, LOCAL), BF),
    seg_prev=pltpu.VMEM((1, FRAMES), I32),
    do_all=pltpu.VMEM((FRAMES, LOCAL), BF),
    k_aug=pltpu.VMEM((4, 2 * FRAMES, 128), BF),
    q_aug=pltpu.VMEM((4, FRAMES, 128), BF),
    probs=pltpu.VMEM((4, FRAMES, WINDOW), BF),
    acc_k=pltpu.VMEM((2 * FRAMES, LOCAL), F32),
    acc_v=pltpu.VMEM((2 * FRAMES, LOCAL), F32),
    over=pltpu.VMEM((2, FRAMES, LOCAL), BF),
    came=pltpu.VMEM((2, FRAMES, LOCAL), BF),
    load_sem=DMA((len(LOADS),)),
    u_send=DMA,
    u_recv=DMA((CTX,)),
    s_send=DMA,
    s_recv=DMA((CTX,)),
    b_send=DMA,
    b_recv=DMA,
    h_send=DMA,
    h_recv=DMA,
    ag_send=DMA((2, CHUNKS, 4)),
    ag_recv=DMA((2, CHUNKS, 4)),
    kv_send=DMA((3,)),
    kv_recv=DMA((3,)),
    do_send=DMA((EXP - 1,)),
    do_recv=DMA((EXP - 1,)),
    ret_send=DMA((BLOCKS, 2)),
    ret_recv=DMA((BLOCKS, 2)),
)


def layer_kernel(*refs):
    r = types.SimpleNamespace(**dict(zip(INPUTS + OUTPUTS + tuple(SCRATCH), refs)))
    me_d, me_c, me_x = lax.axis_index("dp"), lax.axis_index("ctx"), lax.axis_index("exp")
    right, left = lax.rem(me_d + 1, DP), lax.rem(me_d + DP - 1, DP)
    after, prior = lax.rem(me_c + 1, CTX), lax.rem(me_c + CTX - 1, CTX)

    targets = dict(
        ids=r.ids_own,
        gate=r.gate_own,
        x=r.x_own,
        z=r.z_own,
        win=r.w_in,
        wout=r.w_out,
        q=r.q_own,
        seg=r.seg_own,
        lists=r.lists_own,
        k=r.k_all.at[pl.ds(FRAMES, FRAMES)],
        v=r.v_all.at[pl.ds(FRAMES, FRAMES)],
    )
    loads = {
        name: pltpu.make_async_copy(getattr(r, name), targets[name], r.load_sem.at[i])
        for i, name in enumerate(LOADS)
    }
    def ahead(k, xo):
        return {"ctx": lax.rem(me_c + k, CTX), "exp": lax.rem(me_x + xo, EXP)}

    def behind(k, xo):
        return {"ctx": lax.rem(me_c - k + CTX, CTX), "exp": lax.rem(me_x - xo + EXP, EXP)}

    def remote(src, dst, ssem, rsem, target):
        copy = pltpu.make_async_remote_copy(
            src_ref=src,
            dst_ref=dst,
            send_sem=ssem,
            recv_sem=rsem,
            device_id=target,
            device_id_type=MESH,
        )
        copy.start()
        return copy

    barrier = pltpu.get_barrier_semaphore()
    for name in LOADS[:4]:
        loads[name].start()
    columns_of = [lax.rem(me_c + k, CTX) for k in range(CTX)]
    rows_of = [lax.rem(me_x + xo, EXP) for xo in range(EXP)]
    for other in (left, right):
        pl.semaphore_signal(barrier, inc=1, device_id={"dp": other}, device_id_type=MESH)
    for k in range(CTX):
        for xo in range(EXP):
            if k or xo:
                pl.semaphore_signal(
                    barrier,
                    inc=1,
                    device_id={"ctx": columns_of[k], "exp": rows_of[xo]},
                    device_id_type=MESH,
                )
    for name in LOADS[4:]:
        loads[name].start()

    def relative(ids):
        k = (ids // EXP - me_c + CTX) % CTX
        xo = (ids % EXP - me_x + EXP) % EXP
        s = jnp.where(k == 0, 0, jnp.where(k < HALF, CTX - 2 * k, 2 * k - CTX + 1))
        return s * EXP + xo

    loads["ids"].wait()
    expert = iota((PEERS, TOKENS), 0)
    peer_row = [relative(r.ids_own[t : t + 1, :]) for t in range(2)]
    named_t = [(peer_row[t] == expert).astype(F32) for t in range(2)]
    before = (iota((TOKENS, TOKENS), 0) < iota((TOKENS, TOKENS), 1)).astype(F32).astype(BF)
    earlier = dot((named_t[0] + named_t[1]).astype(BF), before, 1, 0)
    slot_row = [
        jnp.sum(named_t[t] * earlier, axis=0, keepdims=True).astype(I32) for t in range(2)
    ]
    place_row = [peer_row[t] * BLOCK + slot_row[t] for t in range(2)]
    loads["gate"].wait()
    gate_row = [r.gate_own[t : t + 1, :].astype(F32) for t in range(2)]
    loads["x"].wait()
    r.xx[:TOKENS] = r.x_own[:, : WIDTH // 2]
    r.xx[TOKENS:] = r.x_own[:, WIDTH // 2 :]

    @pl.loop(0, CHUNKS)
    def _(t):
        place = iota((256, TOKENS), 0) + t * 256
        for half in range(2):
            hit = [place_row[i] + half * CAP == place for i in range(2)]
            cols = slice(half * TOKENS, half * TOKENS + TOKENS)
            r.pick_t[span(t, 256), cols] = (hit[0] | hit[1]).astype(F32).astype(BF)
            r.gated_t[span(t, 256), cols] = (
                jnp.where(hit[0], gate_row[0], 0.0) + jnp.where(hit[1], gate_row[1], 0.0)
            ).astype(BF)
        rows = dot(r.pick_t[span(t, 256)], r.xx[...], 1, 0)
        r.send_u[pl.ds(t * 16, 16)] = rows.astype(BF).reshape(16, BLOCK, WIDTH // 2)

    pl.semaphore_wait(barrier, PEERS - 1 + 2)

    def send_rows(j, k, xo):
        remote(r.send_u.at[j], r.recv_u.at[j], r.u_send, r.u_recv.at[j // EXP], ahead(k, xo))

    @pl.loop(EXP, PEERS)
    def _(j):
        send_rows(j, *hop(j))

    for j in range(1, EXP):
        send_rows(j, 0, j)
    r.recv_u[0] = r.send_u[0]

    loads["z"].wait()
    r.zz[:TOKENS] = r.z_own[:, : WIDTH // 2]
    r.zz[TOKENS:] = r.z_own[:, WIDTH // 2 :]

    @pl.loop(0, CHUNKS)
    def _(t):
        rows = dot(r.gated_t[span(t, 256)], r.zz[...], 1, 0)
        r.send_s[pl.ds(t * 16, 16)] = rows.astype(BF).reshape(16, BLOCK, WIDTH // 2)

    def send_grads(j, k, xo):
        remote(r.send_s.at[j], r.recv_s.at[j], r.s_send, r.s_recv.at[j // EXP], ahead(k, xo))

    @pl.loop(EXP, PEERS)
    def _(j):
        send_grads(j, *hop(j))

    for j in range(1, EXP):
        send_grads(j, 0, j)
    r.recv_s[0] = r.send_s[0]

    past = pl.ds(0, FRAMES)
    for name in ("seg", "k", "v"):
        loads[name].wait()
    kv_copies = [
        remote(r.seg_own, r.seg_prev, r.kv_send.at[0], r.kv_recv.at[0], {"ctx": after}),
        remote(r.k_all.at[pl.ds(FRAMES, FRAMES)], r.k_all.at[past], r.kv_send.at[1], r.kv_recv.at[1], {"ctx": after}),
        remote(r.v_all.at[pl.ds(FRAMES, FRAMES)], r.v_all.at[past], r.kv_send.at[2], r.kv_recv.at[2], {"ctx": after}),
    ]

    peer = [column(peer_row[t]) for t in range(2)]
    slot = [column(slot_row[t]) for t in range(2)]
    gates = [column(gate_row[t]) for t in range(2)]
    named = [(peer[t] == iota((TOKENS, PEERS), 1)).astype(F32) for t in range(2)]
    lane_q = iota((TOKENS, PEERS * BLOCK), 1)
    for half in range(2):
        hit = [peer[t] * BLOCK + slot[t] + half * CAP == lane_q for t in range(2)]
        r.pick[pl.ds(half * TOKENS, TOKENS)] = (hit[0] | hit[1]).astype(F32).astype(BF)

    for name in ("q", "lists"):
        loads[name].wait()
    kinds = 2 * GROUPS
    lane_f, row_f = iota((kinds, 128), 1), iota((kinds, 128), 0)
    place = ((lane_f == row_f) | (lane_f == row_f + 64)).astype(F32).astype(BF)
    row8 = iota((8, FRAMES), 0)
    group_of = iota((8, FRAMES), 1) // GROUP
    moved = []
    for j in range(3):
        lists = column(r.lists_own[j])
        moved.append(jnp.where(lists >= 0, lists - (me_c - 1) * GROUPS, -1))

    def listed(groups):
        return (moved[0] == groups) | (moved[1] == groups) | (moved[2] == groups)

    def features(segment, group, miss, match):
        both = jnp.concatenate(
            [jnp.where(segment, match, miss), jnp.where(group, match, miss)], axis=0
        ).astype(BF)
        return dot(both, place, 0, 0).astype(BF)

    low = iota((FRAMES, 128), 1) < 64
    low_q = iota((QROWS, 128), 1) < 64
    none = jnp.zeros((QROWS, 128), BF)

    def augment(part, feat):
        for hp in range(2):
            k_t = r.k_all[part, hp * 128 : hp * 128 + 128]
            r.k_aug[2 * hp, part] = jnp.where(low, k_t, feat)
            r.k_aug[2 * hp + 1, part] = jnp.where(low, feat, k_t)

    seg_own = r.seg_own[...] == row8
    feat_q = features(seg_own, group_of == row8, 0.0, 1.0)
    for hp in range(2):
        q_t = (r.q_own[:, hp * 128 : hp * 128 + 128].astype(F32) * 0.125).astype(BF)
        r.q_aug[2 * hp] = jnp.where(low, q_t, feat_q)
        r.q_aug[2 * hp + 1] = jnp.where(low, feat_q, q_t)
    list_own = listed(group_of + GROUPS) | (group_of == row8)
    augment(pl.ds(FRAMES, FRAMES), features(seg_own, list_own, -FAR, 0.0))
    r.acc_k[...] = jnp.zeros_like(r.acc_k)
    r.acc_v[...] = jnp.zeros_like(r.acc_v)

    ours = (r.recv_u, r.recv_s)

    def gather(a, ch, n):
        chunk = pl.ds(ch * PER_CHUNK, PER_CHUNK)
        near = pl.ds(ch * PER_CHUNK, PER_CHUNK // 2)
        far = pl.ds(ch * PER_CHUNK + PER_CHUNK // 2, PER_CHUNK // 2)
        src, dst, other = (
            (ours[a].at[chunk], r.gath.at[a, 0, chunk], right),
            (ours[a].at[chunk], r.gath.at[a, 1, chunk], left),
            (r.gath.at[a, 0, near], r.gath.at[a, 2, near], right),
            (r.gath.at[a, 1, far], r.gath.at[a, 2, far], left),
        )[n]
        return pltpu.make_async_remote_copy(
            src_ref=src,
            dst_ref=dst,
            send_sem=r.ag_send.at[a, ch, n],
            recv_sem=r.ag_recv.at[a, ch, n],
            device_id={"dp": other},
            device_id_type=MESH,
        )

    def gather_own(a, ch):
        gather(a, ch, 0).start()
        gather(a, ch, 1).start()

    def gather_on(a, ch):
        gather(a, ch, 0).wait_recv()
        gather(a, ch, 2).start()
        gather(a, ch, 1).wait_recv()
        gather(a, ch, 3).start()

    def gather_wait(a, ch):
        gather(a, ch, 2).wait_recv()
        gather(a, ch, 3).wait_recv()

    def wait_chunk(buffer, sems, ch):
        @pl.when(ch == 0)
        def _():
            wait_bytes(buffer.at[pl.ds(1, EXP - 1)], sems.at[0])

        @pl.when(ch > 0)
        def _():
            wait_bytes(buffer.at[pl.ds(ch * PER_CHUNK, EXP)], sems.at[ch * STEPS])

        for i in range(1, STEPS):
            wait_bytes(buffer.at[pl.ds(ch * PER_CHUNK + i * EXP, EXP)], sems.at[ch * STEPS + i])

    def unpack(blocks):
        came = blocks.astype(F32)
        count = came.shape[0] * CAP
        return [
            came[:, half * CAP : half * CAP + CAP].reshape(count, WIDTH // 2) for half in range(2)
        ]

    def half_cols(half):
        return slice(half * 512, half * 512 + 512)

    def chunk_of_others(a, ch):
        blocks = r.gath[a, :, pl.ds(ch * PER_CHUNK, PER_CHUNK)]
        return blocks.reshape(OTHERS * PER_CHUNK, BLOCK, WIDTH // 2)

    def more_rows(ch):
        for half, u in enumerate(unpack(chunk_of_others(0, ch))):
            r.more[:, half_cols(half)] = u.astype(BF)
            r.more_u_t[ch, half_cols(half)] = u.T.astype(BF)

        @pl.loop(0, WIDTH // 256)
        def _(t):
            cols = span(t, 256)
            pre = dot(r.more[...], r.w_in[:, cols], 1, 0)
            r.more_pre[ch, :, cols] = pre.astype(BF)
            r.more_act_t[ch, cols] = (pre * jax.nn.sigmoid(pre)).T.astype(BF)

    def more_grads(ch):
        for half, s in enumerate(unpack(chunk_of_others(1, ch))):
            r.more[:, half_cols(half)] = s.astype(BF)

        @pl.loop(0, WIDTH // 256)
        def _(t):
            cols = span(t, 256)
            grad = dot(r.more[...], r.w_out[cols, :], 1, 1)
            pre = r.more_pre[ch, :, cols].astype(F32)
            sigma = jax.nn.sigmoid(pre)
            r.more_gp[:, cols] = (grad * sigma * (1.0 + pre * (1.0 - sigma))).astype(BF)

        @pl.loop(0, WIDTH // 256)
        def _(t):
            rows = span(t, 256)
            r.acc_in[rows] += dot(r.more_u_t[ch, rows], r.more_gp[...], 1, 0)
            r.acc_out[rows] += dot(r.more_act_t[ch, rows], r.more[...], 1, 0)

    def softmax(b):
        rows = span(b, QROWS)
        window = pl.ds(pl.multiple_of(b * QROWS, QROWS), WINDOW)
        for h in range(4):
            score = dot(r.q_aug[h, rows], r.k_aug[h, window], 1, 1)
            weight = jnp.exp(score - jnp.max(score, axis=1, keepdims=True))
            r.probs[h, rows] = (
                weight * (1.0 / jnp.sum(weight, axis=1, keepdims=True))
            ).astype(BF)

    loads["win"].wait()
    loads["wout"].wait()

    @pl.loop(0, CHUNKS)
    def _(ch):
        wait_chunk(r.recv_u, r.u_recv, ch)
        gather_own(0, ch)
        rows = span(ch, CHUNK_ROWS)
        for half, u in enumerate(unpack(r.recv_u[pl.ds(ch * PER_CHUNK, PER_CHUNK)])):
            r.u_chunk[:, half_cols(half)] = u.astype(BF)
            r.u_t[half_cols(half), rows] = u.T.astype(BF)

        @pl.loop(0, WIDTH // 256)
        def _(t):
            cols = span(t, 256)
            pre = dot(r.u_chunk[...], r.w_in[:, cols], 1, 0)
            r.pre_all[rows, cols] = pre
            r.act_t[cols, rows] = (pre * jax.nn.sigmoid(pre)).T.astype(BF)

        @pl.when(ch >= 2)
        def _():
            gather_on(0, ch - 2)


    others = pl.ds(1, PEERS - 1)
    wait_bytes(r.send_u.at[others], r.u_send)
    bsend = r.send_u
    lane128 = iota((CHUNK_ROWS, 128), 1)
    slot128 = iota((CHUNK_ROWS, 128), 0) % CAP

    def give_back(j, k, xo):
        remote(bsend.at[j], r.brecv.at[j], r.b_send, r.b_recv, behind(k, xo))
        remote(r.hsend.at[j], r.hrecv.at[j], r.h_send, r.h_recv, behind(k, xo))

    @pl.loop(0, CHUNKS)
    def _(ch):
        base = ch * PER_CHUNK
        rows = span(ch, CHUNK_ROWS)
        peers = pl.ds(base, PER_CHUNK)
        wait_chunk(r.recv_s, r.s_recv, ch)
        gather_own(1, ch)
        for half, s in enumerate(unpack(r.recv_s[peers])):
            r.s_all[rows, half_cols(half)] = s.astype(BF)

        def hidden(t, total):
            cols = span(t, 256)
            grad = dot(r.s_all[rows], r.w_out[cols, :], 1, 1)
            pre = r.pre_all[rows, cols]
            sigma = jax.nn.sigmoid(pre)
            r.gp_all[rows, cols] = (grad * sigma * (1.0 + pre * (1.0 - sigma))).astype(BF)
            return total + jnp.sum(pre * sigma * grad, axis=1, keepdims=True)

        total = lax.fori_loop(0, WIDTH // 256, hidden, jnp.zeros((CHUNK_ROWS, 1), F32))
        spread = jnp.where(lane128 == slot128, total, 0.0)
        r.hsend[peers] = jnp.sum(spread.reshape(PER_CHUNK, CAP, 128), axis=1, keepdims=True)

        @pl.loop(0, 2)
        def _(t):
            lo, hi = span(t, 256), span(t + 2, 256)
            first = dot(r.gp_all[rows], r.w_in[lo, :], 1, 1).reshape(PER_CHUNK, CAP, 256)
            last = dot(r.gp_all[rows], r.w_in[hi, :], 1, 1).reshape(PER_CHUNK, CAP, 256)
            bsend[peers, :, lo] = jnp.concatenate([first, last], axis=1).astype(BF)

        @pl.when(ch == 0)
        def _():
            r.brecv[0] = bsend[0]
            r.hrecv[0] = r.hsend[0]
            for j in range(1, EXP):
                give_back(j, 0, j)

        @pl.when(ch > 0)
        def _():
            for i in range(EXP):
                give_back(base + i, *hop(base + i))

        @pl.loop(EXP, PER_CHUNK)
        def _(i):
            give_back(base + i, *hop(base + i))

        @pl.when(ch < 2)
        def _():
            gather_on(0, ch + 2)

        @pl.when(ch >= 2)
        def _():
            gather_on(1, ch - 2)

        gather_wait(0, ch)
        more_rows(ch)

    @pl.loop(0, WIDTH // 256)
    def _(t):
        rows = span(t, 256)
        r.acc_in[rows] = dot(r.u_t[rows], r.gp_all[...], 1, 0)
        r.acc_out[rows] = dot(r.act_t[rows], r.s_all[...], 1, 0)

    def other_grads(ch, carry):
        gather_wait(1, ch)
        more_grads(ch)
        return carry

    gather_on(1, 2)
    kv_copies[0].wait_recv()
    kv_copies[1].wait_recv()
    seg_past = r.seg_prev[...] == row8
    augment(past, features(seg_past, listed(group_of), -FAR, 0.0))

    @pl.loop(0, BLOCKS)
    def _(b):
        softmax(b)

    lax.fori_loop(0, 2, other_grads, 0)
    gather_on(1, 3)
    lax.fori_loop(2, 3, other_grads, 0)

    wait_bytes(r.brecv.at[others], r.b_recv)
    back = r.brecv[...].reshape(PEERS * BLOCK, WIDTH // 2)
    for half in range(2):
        cols = slice(half * 512, half * 512 + 512)
        r.dres[:, cols] = (
            r.z_own[:, cols].astype(F32)
            + dot(r.pick[half * TOKENS : (half + 1) * TOKENS, :], back, 1, 0)
        ).astype(BF)
    my_rows = span(me_x, TOKENS)
    do_copies = []
    for o in range(1, EXP):
        px = lax.rem(me_x + o, EXP)
        do_copies.append(
            remote(
                r.dres.at[:, span(px, LOCAL)],
                r.do_all.at[my_rows],
                r.do_send.at[o - 1],
                r.do_recv.at[o - 1],
                {"exp": px},
            )
        )
    r.do_all[my_rows] = r.dres[:, span(me_x, LOCAL)]
    wait_bytes(r.hrecv.at[others], r.h_recv)
    sums = jnp.sum(r.hrecv[...], axis=1)
    lane_s = iota((TOKENS, 128), 1)
    for t in range(2):
        chosen = dot(named[t], sums, 1, 0, lax.Precision.HIGHEST)
        value = jnp.sum(jnp.where(lane_s == slot[t], chosen, 0.0), axis=1, keepdims=True)
        r.dgate[t : t + 1, :] = as_row(value / gates[t]).astype(BF)
    kv_copies[2].wait_recv()
    lax.fori_loop(3, 4, other_grads, 0)
    r.gin[...] = r.acc_in[...].astype(BF)
    r.gout[...] = r.acc_out[...].astype(BF)
    for c in do_copies:
        c.wait_recv()

    def backward(b, carry):
        rows = span(b, QROWS)
        window = pl.ds(pl.multiple_of(b * QROWS, QROWS), WINDOW)
        for hp in range(2):
            tile = slice(hp * 128, hp * 128 + 128)
            do_t = r.do_all[rows, tile]
            v_t = r.v_all[window, tile]
            k_t = r.k_all[window, tile]
            all_p, all_s, all_d, all_q, dq = [], [], [], [], []
            for e in range(2):
                keep = low_q if e == 0 else jnp.logical_not(low_q)
                do_e = jnp.where(keep, do_t, none)
                probs = r.probs[2 * hp + e, rows]
                weight = probs.astype(F32)
                grad = dot(do_e, v_t, 1, 1)
                delta = jnp.sum(weight * grad, axis=1, keepdims=True)
                dscore = (weight * (grad - delta)).astype(BF)
                dq.append(dot(dscore, k_t, 1, 0))
                all_p.append(probs)
                all_s.append(dscore)
                all_d.append(do_e)
                all_q.append(jnp.where(keep, r.q_aug[2 * hp + e, rows], none))
            r.dq[rows, tile] = (jnp.where(low_q, dq[0], dq[1]) * 0.125).astype(BF)
            r.acc_k[window, tile] += dot(
                jnp.concatenate(all_s, axis=0), jnp.concatenate(all_q, axis=0), 0, 0
            )
            r.acc_v[window, tile] += dot(
                jnp.concatenate(all_p, axis=0), jnp.concatenate(all_d, axis=0), 0, 0
            )
        r.over[0, rows] = r.acc_k[rows].astype(BF)
        r.over[1, rows] = r.acc_v[rows].astype(BF)
        for i in range(2):
            give_prior(b, i).start()
        return carry

    def give_prior(b, i):
        rows = span(b, QROWS)
        return pltpu.make_async_remote_copy(
            src_ref=r.over.at[i, rows],
            dst_ref=r.came.at[i, rows],
            send_sem=r.ret_send.at[b, i],
            recv_sem=r.ret_recv.at[b, i],
            device_id={"ctx": prior},
            device_id_type=MESH,
        )

    lax.fori_loop(0, BLOCKS, backward, 0)

    @pl.loop(0, BLOCKS)
    def _(b):
        rows = span(b, QROWS)
        late = pl.ds(pl.multiple_of(FRAMES + b * QROWS, QROWS), QROWS)
        for i, (out, acc) in enumerate(((r.dk, r.acc_k), (r.dv, r.acc_v))):
            give_prior(b, i).wait_recv()
            out[rows] = (acc[late] + r.came[i, rows].astype(F32)).astype(BF)
            give_prior(b, i).wait_send()

    for a in range(2):
        for ch in range(CHUNKS):
            for n in range(4):
                gather(a, ch, n).wait_send()
    for c in do_copies + kv_copies:
        c.wait_send()
    wait_bytes(r.send_s.at[others], r.s_send)
    wait_bytes(bsend.at[others], r.b_send)
    wait_bytes(r.hsend.at[others], r.h_send)


PIECES = [(name, rows) for name in ("gout", "gin") for rows in range(0, WIDTH, 256)] + [
    (name, None) for name in ("dres", "dq", "dk", "dv", "dgate")
]


def deliver_kernel(*refs):
    n = len(OUTPUTS)
    sources, targets = dict(zip(OUTPUTS, refs)), dict(zip(OUTPUTS, refs[n:]))
    buffers = dict(zip(OUTPUTS, refs[2 * n :]))
    get_sem, put_sem = refs[3 * n :]

    def view(ref, rows):
        return ref if rows is None else ref.at[pl.ds(rows, 256)]

    gets, puts = [], []
    for i, (name, rows) in enumerate(PIECES):
        source, buffer, target = (
            view(group[name], rows) for group in (sources, buffers, targets)
        )
        gets.append(pltpu.make_async_copy(source, buffer, get_sem.at[i]))
        puts.append(pltpu.make_async_copy(buffer, target, put_sem.at[i]))
    for get in gets:
        get.start()
    for get, put in zip(gets, puts):
        get.wait()
        put.start()
    for put in puts:
        put.wait()


def layer(*args):
    vmem = pl.BlockSpec(memory_space=pltpu.VMEM)
    anywhere = pl.BlockSpec(memory_space=pl.ANY)
    frames = jax.ShapeDtypeStruct((FRAMES, LOCAL), BF)
    weight = jax.ShapeDtypeStruct((WIDTH, WIDTH), BF)
    shapes = (
        frames,
        frames,
        frames,
        jax.ShapeDtypeStruct((TOKENS, WIDTH), BF),
        jax.ShapeDtypeStruct((2, TOKENS), BF),
        weight,
        weight,
    )
    results = pl.pallas_call(
        layer_kernel,
        out_shape=shapes,
        in_specs=[anywhere] * len(INPUTS),
        out_specs=(vmem,) * 7,
        scratch_shapes=list(SCRATCH.values()),
        compiler_params=pltpu.CompilerParams(
            collective_id=0, has_side_effects=True, vmem_limit_bytes=VMEM_BYTES
        ),
        name="layer",
    )(*args)
    return pl.pallas_call(
        deliver_kernel,
        out_shape=shapes,
        in_specs=[anywhere] * len(OUTPUTS),
        out_specs=(anywhere,) * len(OUTPUTS),
        scratch_shapes=[pltpu.VMEM(s.shape, s.dtype) for s in shapes]
        + [DMA((len(PIECES),)), DMA((len(PIECES),))],
        compiler_params=pltpu.CompilerParams(vmem_limit_bytes=VMEM_BYTES),
        name="deliver",
    )(*results)


def local(
    queries,
    key_rows,
    value_rows,
    segments,
    left_blocks,
    moe_input,
    out_grad,
    expert_ids,
    gate_weights,
    expert_in,
    expert_out,
):
    dq, dk, dv, d_residual, d_gates, grad_out, grad_in = layer(
        queries[0],
        key_rows[0],
        value_rows[0],
        segments,
        jnp.transpose(left_blocks, (2, 0, 1)),
        moe_input[0],
        out_grad[0],
        expert_ids[0].T,
        gate_weights[0].T,
        expert_in[0],
        expert_out[0],
    )
    return (
        dq[None],
        dk[None],
        dv[None],
        d_residual[None],
        d_gates.T[None],
        grad_in[None],
        grad_out[None],
    )


def solution(mesh):
    assert dict(mesh.shape) == {"dp": DP, "ctx": CTX, "exp": EXP}
    return jax.shard_map(
        local,
        mesh=mesh,
        in_specs=(
            P("dp", "ctx", "exp"),
            P("dp", "ctx", "exp"),
            P("dp", "ctx", "exp"),
            P("dp", "ctx"),
            P("dp", "ctx", None),
            P("dp", ("ctx", "exp"), None),
            P("dp", ("ctx", "exp"), None),
            P("dp", ("ctx", "exp"), None),
            P("dp", ("ctx", "exp"), None),
            P(("ctx", "exp"), None, None),
            P(("ctx", "exp"), None, None),
        ),
        out_specs=(
            P("dp", "ctx", "exp"),
            P("dp", "ctx", "exp"),
            P("dp", "ctx", "exp"),
            P("dp", ("ctx", "exp"), None),
            P("dp", ("ctx", "exp"), None),
            P(("ctx", "exp"), None, None),
            P(("ctx", "exp"), None, None),
        ),
        check_vma=False,
    )
```

```python
import types

import jax
import jax.numpy as jnp
from jax import lax
from jax.experimental import pallas as pl
from jax.experimental.pallas import tpu as pltpu
from jax.sharding import PartitionSpec as P

MESH = pl.DeviceIdType.MESH
BF = jnp.bfloat16
F32 = jnp.float32
I32 = jnp.int32

DP, CTX, EXP = 4, 16, 4
PEERS = CTX * EXP
HALF = CTX // 2
CAP = 8
BLOCK = 2 * CAP
TOKENS = 128
WIDTH = 1024
CHUNKS = 4
PER_CHUNK = PEERS // CHUNKS
CHUNK_ROWS = PER_CHUNK * CAP
ROWS = PEERS * CAP
OTHERS = DP - 1
OTHER_ROWS = OTHERS * CHUNK_ROWS
STEPS = PER_CHUNK // EXP
EARLY, MIDDLE = 2, 3
GROUP = 64
GROUPS = 8
FRAMES = 512
LOCAL = 256
QROWS = 128
BLOCKS = FRAMES // QROWS
WINDOW = FRAMES + QROWS
FAR = 32768.0
VMEM_BYTES = 63 * 1024 * 1024


def dot(a, b, ca, cb, precision=None):
    return lax.dot_general(
        a, b, (((ca,), (cb,)), ((), ())), preferred_element_type=F32, precision=precision
    )


def wait_bytes(ref, sem):
    pltpu.make_async_copy(ref, ref, sem).wait()


def span(index, size):
    return pl.ds(pl.multiple_of(index * size, size), size)


def hop(j):
    s = j // EXP
    return HALF + (2 * (s % 2) - 1) * (s // 2), j % EXP


def iota(shape, dim):
    return lax.broadcasted_iota(I32, shape, dim)


def column(row):
    n = row.shape[1]
    same = iota((n, n), 0) == iota((n, n), 1)
    return jnp.sum(jnp.where(same, row, jnp.zeros_like(row)), axis=1, keepdims=True)


def as_row(col):
    n = col.shape[0]
    same = iota((n, n), 0) == iota((n, n), 1)
    return jnp.sum(jnp.where(same, col, jnp.zeros_like(col)), axis=0, keepdims=True)


INPUTS = ("q", "k", "v", "seg", "lists", "x", "z", "ids", "gate", "win", "wout")
OUTPUTS = ("dq", "dk", "dv", "dres", "dgate", "gout", "gin")
DMA = pltpu.SemaphoreType.DMA
LOADS = ("ids", "gate", "x", "z", "win", "wout", "q", "seg", "lists", "k", "v")
SCRATCH = dict(
    q_own=pltpu.VMEM((FRAMES, LOCAL), BF),
    seg_own=pltpu.VMEM((1, FRAMES), I32),
    lists_own=pltpu.VMEM((3, 1, GROUPS), I32),
    x_own=pltpu.VMEM((TOKENS, WIDTH), BF),
    z_own=pltpu.VMEM((TOKENS, WIDTH), BF),
    ids_own=pltpu.VMEM((2, TOKENS), I32),
    gate_own=pltpu.VMEM((2, TOKENS), BF),
    w_in=pltpu.VMEM((WIDTH, WIDTH), BF),
    w_out=pltpu.VMEM((WIDTH, WIDTH), BF),
    pick_t=pltpu.VMEM((PEERS * BLOCK, 2 * TOKENS), BF),
    gated_t=pltpu.VMEM((PEERS * BLOCK, 2 * TOKENS), BF),
    pick=pltpu.VMEM((2 * TOKENS, PEERS * BLOCK), BF),
    xx=pltpu.VMEM((2 * TOKENS, WIDTH // 2), BF),
    zz=pltpu.VMEM((2 * TOKENS, WIDTH // 2), BF),
    send_u=pltpu.VMEM((PEERS, BLOCK, WIDTH // 2), BF),
    recv_u=pltpu.VMEM((PEERS, BLOCK, WIDTH // 2), BF),
    send_s=pltpu.VMEM((PEERS, BLOCK, WIDTH // 2), BF),
    recv_s=pltpu.VMEM((PEERS, BLOCK, WIDTH // 2), BF),
    gath=pltpu.VMEM((2, OTHERS, PEERS, BLOCK, WIDTH // 2), BF),
    more=pltpu.VMEM((OTHER_ROWS, WIDTH), BF),
    more_gp=pltpu.VMEM((OTHER_ROWS, WIDTH), BF),
    more_u_t=pltpu.VMEM((CHUNKS, WIDTH, OTHER_ROWS), BF),
    more_act_t=pltpu.VMEM((CHUNKS, WIDTH, OTHER_ROWS), BF),
    more_pre=pltpu.VMEM((CHUNKS, OTHER_ROWS, WIDTH), BF),
    acc_in=pltpu.VMEM((WIDTH, WIDTH), F32),
    acc_out=pltpu.VMEM((WIDTH, WIDTH), F32),
    u_chunk=pltpu.VMEM((CHUNK_ROWS, WIDTH), BF),
    u_t=pltpu.VMEM((WIDTH, ROWS), BF),
    act_t=pltpu.VMEM((WIDTH, ROWS), BF),
    pre_all=pltpu.VMEM((ROWS, WIDTH), F32),
    s_all=pltpu.VMEM((ROWS, WIDTH), BF),
    gp_all=pltpu.VMEM((ROWS, WIDTH), BF),
    brecv=pltpu.VMEM((PEERS, BLOCK, WIDTH // 2), BF),
    hsend=pltpu.VMEM((PEERS, 1, 128), F32),
    hrecv=pltpu.VMEM((PEERS, 1, 128), F32),
    k_all=pltpu.VMEM((2 * FRAMES, LOCAL), BF),
    v_all=pltpu.VMEM((2 * FRAMES, LOCAL), BF),
    seg_prev=pltpu.VMEM((1, FRAMES), I32),
    do_all=pltpu.VMEM((FRAMES, LOCAL), BF),
    k_aug=pltpu.VMEM((4, 2 * FRAMES, 128), BF),
    q_aug=pltpu.VMEM((4, FRAMES, 128), BF),
    probs=pltpu.VMEM((4, FRAMES, WINDOW), BF),
    acc_k=pltpu.VMEM((2 * FRAMES, LOCAL), F32),
    acc_v=pltpu.VMEM((2 * FRAMES, LOCAL), F32),
    over=pltpu.VMEM((2, FRAMES, LOCAL), BF),
    came=pltpu.VMEM((2, FRAMES, LOCAL), BF),
    load_sem=DMA((len(LOADS),)),
    u_send=DMA,
    u_recv=DMA((CTX,)),
    s_send=DMA,
    s_recv=DMA((CTX,)),
    b_send=DMA,
    b_recv=DMA,
    h_send=DMA,
    h_recv=DMA,
    ag_send=DMA((2, CHUNKS, 4)),
    ag_recv=DMA((2, CHUNKS, 4)),
    kv_send=DMA((3,)),
    kv_recv=DMA((3,)),
    do_send=DMA((EXP - 1,)),
    do_recv=DMA((EXP - 1,)),
    ret_send=DMA((BLOCKS, 2)),
    ret_recv=DMA((BLOCKS, 2)),
)


def layer_kernel(*refs):
    r = types.SimpleNamespace(**dict(zip(INPUTS + OUTPUTS + tuple(SCRATCH), refs)))
    me_d, me_c, me_x = lax.axis_index("dp"), lax.axis_index("ctx"), lax.axis_index("exp")
    right, left = lax.rem(me_d + 1, DP), lax.rem(me_d + DP - 1, DP)
    after, prior = lax.rem(me_c + 1, CTX), lax.rem(me_c + CTX - 1, CTX)

    targets = dict(
        ids=r.ids_own,
        gate=r.gate_own,
        x=r.x_own,
        z=r.z_own,
        win=r.w_in,
        wout=r.w_out,
        q=r.q_own,
        seg=r.seg_own,
        lists=r.lists_own,
        k=r.k_all.at[pl.ds(FRAMES, FRAMES)],
        v=r.v_all.at[pl.ds(FRAMES, FRAMES)],
    )
    loads = {
        name: pltpu.make_async_copy(getattr(r, name), targets[name], r.load_sem.at[i])
        for i, name in enumerate(LOADS)
    }
    def ahead(k, xo):
        return {"ctx": lax.rem(me_c + k, CTX), "exp": lax.rem(me_x + xo, EXP)}

    def behind(k, xo):
        return {"ctx": lax.rem(me_c - k + CTX, CTX), "exp": lax.rem(me_x - xo + EXP, EXP)}

    def remote(src, dst, ssem, rsem, target):
        copy = pltpu.make_async_remote_copy(
            src_ref=src,
            dst_ref=dst,
            send_sem=ssem,
            recv_sem=rsem,
            device_id=target,
            device_id_type=MESH,
        )
        copy.start()
        return copy

    barrier = pltpu.get_barrier_semaphore()
    for name in LOADS[:4]:
        loads[name].start()
    columns_of = [lax.rem(me_c + k, CTX) for k in range(CTX)]
    rows_of = [lax.rem(me_x + xo, EXP) for xo in range(EXP)]
    for other in (left, right):
        pl.semaphore_signal(barrier, inc=1, device_id={"dp": other}, device_id_type=MESH)
    for k in range(CTX):
        for xo in range(EXP):
            if k or xo:
                pl.semaphore_signal(
                    barrier,
                    inc=1,
                    device_id={"ctx": columns_of[k], "exp": rows_of[xo]},
                    device_id_type=MESH,
                )
    for name in LOADS[4:]:
        loads[name].start()

    def relative(ids):
        k = (ids // EXP - me_c + CTX) % CTX
        xo = (ids % EXP - me_x + EXP) % EXP
        s = jnp.where(k == 0, 0, jnp.where(k < HALF, CTX - 2 * k, 2 * k - CTX + 1))
        return s * EXP + xo

    loads["ids"].wait()
    expert = iota((PEERS, TOKENS), 0)
    peer_row = [relative(r.ids_own[t : t + 1, :]) for t in range(2)]
    named_t = [(peer_row[t] == expert).astype(F32) for t in range(2)]
    before = (iota((TOKENS, TOKENS), 0) < iota((TOKENS, TOKENS), 1)).astype(F32).astype(BF)
    earlier = dot((named_t[0] + named_t[1]).astype(BF), before, 1, 0)
    slot_row = [
        jnp.sum(named_t[t] * earlier, axis=0, keepdims=True).astype(I32) for t in range(2)
    ]
    place_row = [peer_row[t] * BLOCK + slot_row[t] for t in range(2)]
    loads["gate"].wait()
    gate_row = [r.gate_own[t : t + 1, :].astype(F32) for t in range(2)]
    loads["x"].wait()
    r.xx[:TOKENS] = r.x_own[:, : WIDTH // 2]
    r.xx[TOKENS:] = r.x_own[:, WIDTH // 2 :]

    @pl.loop(0, CHUNKS)
    def _(t):
        place = iota((256, TOKENS), 0) + t * 256
        for half in range(2):
            hit = [place_row[i] + half * CAP == place for i in range(2)]
            cols = slice(half * TOKENS, half * TOKENS + TOKENS)
            r.pick_t[span(t, 256), cols] = (hit[0] | hit[1]).astype(F32).astype(BF)
            r.gated_t[span(t, 256), cols] = (
                jnp.where(hit[0], gate_row[0], 0.0) + jnp.where(hit[1], gate_row[1], 0.0)
            ).astype(BF)
        rows = dot(r.pick_t[span(t, 256)], r.xx[...], 1, 0)
        r.send_u[pl.ds(t * 16, 16)] = rows.astype(BF).reshape(16, BLOCK, WIDTH // 2)

    pl.semaphore_wait(barrier, PEERS - 1 + 2)

    def send_rows(j, k, xo):
        remote(r.send_u.at[j], r.recv_u.at[j], r.u_send, r.u_recv.at[j // EXP], ahead(k, xo))

    @pl.loop(EXP, PEERS)
    def _(j):
        send_rows(j, *hop(j))

    for j in range(1, EXP):
        send_rows(j, 0, j)
    r.recv_u[0] = r.send_u[0]

    loads["z"].wait()
    r.zz[:TOKENS] = r.z_own[:, : WIDTH // 2]
    r.zz[TOKENS:] = r.z_own[:, WIDTH // 2 :]

    @pl.loop(0, CHUNKS)
    def _(t):
        rows = dot(r.gated_t[span(t, 256)], r.zz[...], 1, 0)
        r.send_s[pl.ds(t * 16, 16)] = rows.astype(BF).reshape(16, BLOCK, WIDTH // 2)

    def send_grads(j, k, xo):
        remote(r.send_s.at[j], r.recv_s.at[j], r.s_send, r.s_recv.at[j // EXP], ahead(k, xo))

    @pl.loop(EXP, PEERS)
    def _(j):
        send_grads(j, *hop(j))

    for j in range(1, EXP):
        send_grads(j, 0, j)
    r.recv_s[0] = r.send_s[0]

    past = pl.ds(0, FRAMES)
    for name in ("seg", "k", "v"):
        loads[name].wait()
    kv_copies = [
        remote(r.seg_own, r.seg_prev, r.kv_send.at[0], r.kv_recv.at[0], {"ctx": after}),
        remote(r.k_all.at[pl.ds(FRAMES, FRAMES)], r.k_all.at[past], r.kv_send.at[1], r.kv_recv.at[1], {"ctx": after}),
        remote(r.v_all.at[pl.ds(FRAMES, FRAMES)], r.v_all.at[past], r.kv_send.at[2], r.kv_recv.at[2], {"ctx": after}),
    ]

    peer = [column(peer_row[t]) for t in range(2)]
    slot = [column(slot_row[t]) for t in range(2)]
    gates = [column(gate_row[t]) for t in range(2)]
    named = [(peer[t] == iota((TOKENS, PEERS), 1)).astype(F32) for t in range(2)]
    lane_q = iota((TOKENS, PEERS * BLOCK), 1)
    for half in range(2):
        hit = [peer[t] * BLOCK + slot[t] + half * CAP == lane_q for t in range(2)]
        r.pick[pl.ds(half * TOKENS, TOKENS)] = (hit[0] | hit[1]).astype(F32).astype(BF)

    for name in ("q", "lists"):
        loads[name].wait()
    kinds = 2 * GROUPS
    lane_f, row_f = iota((kinds, 128), 1), iota((kinds, 128), 0)
    place = ((lane_f == row_f) | (lane_f == row_f + 64)).astype(F32).astype(BF)
    row8 = iota((8, FRAMES), 0)
    group_of = iota((8, FRAMES), 1) // GROUP
    moved = []
    for j in range(3):
        lists = column(r.lists_own[j])
        moved.append(jnp.where(lists >= 0, lists - (me_c - 1) * GROUPS, -1))

    def listed(groups):
        return (moved[0] == groups) | (moved[1] == groups) | (moved[2] == groups)

    def features(segment, group, miss, match):
        both = jnp.concatenate(
            [jnp.where(segment, match, miss), jnp.where(group, match, miss)], axis=0
        ).astype(BF)
        return dot(both, place, 0, 0).astype(BF)

    low = iota((FRAMES, 128), 1) < 64
    low_q = iota((QROWS, 128), 1) < 64
    none = jnp.zeros((QROWS, 128), BF)

    def augment(part, feat):
        for hp in range(2):
            k_t = r.k_all[part, hp * 128 : hp * 128 + 128]
            r.k_aug[2 * hp, part] = jnp.where(low, k_t, feat)
            r.k_aug[2 * hp + 1, part] = jnp.where(low, feat, k_t)

    seg_own = r.seg_own[...] == row8
    feat_q = features(seg_own, group_of == row8, 0.0, 1.0)
    for hp in range(2):
        q_t = (r.q_own[:, hp * 128 : hp * 128 + 128].astype(F32) * 0.125).astype(BF)
        r.q_aug[2 * hp] = jnp.where(low, q_t, feat_q)
        r.q_aug[2 * hp + 1] = jnp.where(low, feat_q, q_t)
    list_own = listed(group_of + GROUPS) | (group_of == row8)
    augment(pl.ds(FRAMES, FRAMES), features(seg_own, list_own, -FAR, 0.0))
    r.acc_k[...] = jnp.zeros_like(r.acc_k)
    r.acc_v[...] = jnp.zeros_like(r.acc_v)

    ours = (r.recv_u, r.recv_s)

    def gather(a, ch, n):
        chunk = pl.ds(ch * PER_CHUNK, PER_CHUNK)
        near = pl.ds(ch * PER_CHUNK, PER_CHUNK // 2)
        far = pl.ds(ch * PER_CHUNK + PER_CHUNK // 2, PER_CHUNK // 2)
        src, dst, other = (
            (ours[a].at[chunk], r.gath.at[a, 0, chunk], right),
            (ours[a].at[chunk], r.gath.at[a, 1, chunk], left),
            (r.gath.at[a, 0, near], r.gath.at[a, 2, near], right),
            (r.gath.at[a, 1, far], r.gath.at[a, 2, far], left),
        )[n]
        return pltpu.make_async_remote_copy(
            src_ref=src,
            dst_ref=dst,
            send_sem=r.ag_send.at[a, ch, n],
            recv_sem=r.ag_recv.at[a, ch, n],
            device_id={"dp": other},
            device_id_type=MESH,
        )

    def gather_own(a, ch):
        gather(a, ch, 0).start()
        gather(a, ch, 1).start()

    def gather_on(a, ch):
        gather(a, ch, 0).wait_recv()
        gather(a, ch, 2).start()
        gather(a, ch, 1).wait_recv()
        gather(a, ch, 3).start()

    def gather_wait(a, ch):
        gather(a, ch, 2).wait_recv()
        gather(a, ch, 3).wait_recv()

    def wait_chunk(buffer, sems, ch):
        @pl.when(ch == 0)
        def _():
            wait_bytes(buffer.at[pl.ds(1, EXP - 1)], sems.at[0])

        @pl.when(ch > 0)
        def _():
            wait_bytes(buffer.at[pl.ds(ch * PER_CHUNK, EXP)], sems.at[ch * STEPS])

        for i in range(1, STEPS):
            wait_bytes(buffer.at[pl.ds(ch * PER_CHUNK + i * EXP, EXP)], sems.at[ch * STEPS + i])

    def unpack(blocks):
        came = blocks.astype(F32)
        count = came.shape[0] * CAP
        return [
            came[:, half * CAP : half * CAP + CAP].reshape(count, WIDTH // 2) for half in range(2)
        ]

    def half_cols(half):
        return slice(half * 512, half * 512 + 512)

    def chunk_of_others(a, ch):
        blocks = r.gath[a, :, pl.ds(ch * PER_CHUNK, PER_CHUNK)]
        return blocks.reshape(OTHERS * PER_CHUNK, BLOCK, WIDTH // 2)

    def more_rows(ch):
        for half, u in enumerate(unpack(chunk_of_others(0, ch))):
            r.more[:, half_cols(half)] = u.astype(BF)
            r.more_u_t[ch, half_cols(half)] = u.T.astype(BF)

        @pl.loop(0, WIDTH // 256)
        def _(t):
            cols = span(t, 256)
            pre = dot(r.more[...], r.w_in[:, cols], 1, 0)
            r.more_pre[ch, :, cols] = pre.astype(BF)
            r.more_act_t[ch, cols] = (pre * jax.nn.sigmoid(pre)).T.astype(BF)

    def more_grads(ch):
        for half, s in enumerate(unpack(chunk_of_others(1, ch))):
            r.more[:, half_cols(half)] = s.astype(BF)

        @pl.loop(0, WIDTH // 256)
        def _(t):
            cols = span(t, 256)
            grad = dot(r.more[...], r.w_out[cols, :], 1, 1)
            pre = r.more_pre[ch, :, cols].astype(F32)
            sigma = jax.nn.sigmoid(pre)
            r.more_gp[:, cols] = (grad * sigma * (1.0 + pre * (1.0 - sigma))).astype(BF)

        @pl.loop(0, WIDTH // 256)
        def _(t):
            rows = span(t, 256)
            r.acc_in[rows] += dot(r.more_u_t[ch, rows], r.more_gp[...], 1, 0)
            r.acc_out[rows] += dot(r.more_act_t[ch, rows], r.more[...], 1, 0)

    def softmax(b):
        rows = span(b, QROWS)
        window = pl.ds(pl.multiple_of(b * QROWS, QROWS), WINDOW)
        for h in range(4):
            score = dot(r.q_aug[h, rows], r.k_aug[h, window], 1, 1)
            weight = jnp.exp(score - jnp.max(score, axis=1, keepdims=True))
            r.probs[h, rows] = (
                weight * (1.0 / jnp.sum(weight, axis=1, keepdims=True))
            ).astype(BF)

    loads["win"].wait()
    loads["wout"].wait()

    @pl.loop(0, CHUNKS)
    def _(ch):
        wait_chunk(r.recv_u, r.u_recv, ch)
        gather_own(0, ch)
        rows = span(ch, CHUNK_ROWS)
        for half, u in enumerate(unpack(r.recv_u[pl.ds(ch * PER_CHUNK, PER_CHUNK)])):
            r.u_chunk[:, half_cols(half)] = u.astype(BF)
            r.u_t[half_cols(half), rows] = u.T.astype(BF)

        @pl.loop(0, WIDTH // 256)
        def _(t):
            cols = span(t, 256)
            pre = dot(r.u_chunk[...], r.w_in[:, cols], 1, 0)
            r.pre_all[rows, cols] = pre
            r.act_t[cols, rows] = (pre * jax.nn.sigmoid(pre)).T.astype(BF)

    others = pl.ds(1, PEERS - 1)
    wait_bytes(r.send_u.at[others], r.u_send)
    bsend = r.send_u
    lane128 = iota((CHUNK_ROWS, 128), 1)
    slot128 = iota((CHUNK_ROWS, 128), 0) % CAP

    def give_back(j, k, xo):
        remote(bsend.at[j], r.brecv.at[j], r.b_send, r.b_recv, behind(k, xo))
        remote(r.hsend.at[j], r.hrecv.at[j], r.h_send, r.h_recv, behind(k, xo))

    @pl.loop(0, CHUNKS)
    def _(ch):
        base = ch * PER_CHUNK
        rows = span(ch, CHUNK_ROWS)
        peers = pl.ds(base, PER_CHUNK)
        wait_chunk(r.recv_s, r.s_recv, ch)
        gather_own(1, ch)
        for half, s in enumerate(unpack(r.recv_s[peers])):
            r.s_all[rows, half_cols(half)] = s.astype(BF)

        def hidden(t, total):
            cols = span(t, 256)
            grad = dot(r.s_all[rows], r.w_out[cols, :], 1, 1)
            pre = r.pre_all[rows, cols]
            sigma = jax.nn.sigmoid(pre)
            r.gp_all[rows, cols] = (grad * sigma * (1.0 + pre * (1.0 - sigma))).astype(BF)
            return total + jnp.sum(pre * sigma * grad, axis=1, keepdims=True)

        total = lax.fori_loop(0, WIDTH // 256, hidden, jnp.zeros((CHUNK_ROWS, 1), F32))
        spread = jnp.where(lane128 == slot128, total, 0.0)
        r.hsend[peers] = jnp.sum(spread.reshape(PER_CHUNK, CAP, 128), axis=1, keepdims=True)

        @pl.loop(0, 2)
        def _(t):
            lo, hi = span(t, 256), span(t + 2, 256)
            first = dot(r.gp_all[rows], r.w_in[lo, :], 1, 1).reshape(PER_CHUNK, CAP, 256)
            last = dot(r.gp_all[rows], r.w_in[hi, :], 1, 1).reshape(PER_CHUNK, CAP, 256)
            bsend[peers, :, lo] = jnp.concatenate([first, last], axis=1).astype(BF)

        @pl.when(ch == 0)
        def _():
            r.brecv[0] = bsend[0]
            r.hrecv[0] = r.hsend[0]
            for j in range(1, EXP):
                give_back(j, 0, j)

        @pl.when(ch > 0)
        def _():
            for i in range(EXP):
                give_back(base + i, *hop(base + i))

        @pl.loop(EXP, PER_CHUNK)
        def _(i):
            give_back(base + i, *hop(base + i))

        @pl.when(ch > 0)
        def _():
            gather_on(0, ch - 1)

    @pl.loop(0, WIDTH // 256)
    def _(t):
        rows = span(t, 256)
        r.acc_in[rows] = dot(r.u_t[rows], r.gp_all[...], 1, 0)
        r.acc_out[rows] = dot(r.act_t[rows], r.s_all[...], 1, 0)

    def other_grads(ch, carry):
        gather_wait(1, ch)
        more_grads(ch)
        return carry

    kv_copies[0].wait_recv()
    kv_copies[1].wait_recv()
    seg_past = r.seg_prev[...] == row8
    augment(past, features(seg_past, listed(group_of), -FAR, 0.0))

    @pl.loop(0, BLOCKS)
    def _(b):
        softmax(b)

    gather_on(0, CHUNKS - 1)

    @pl.loop(0, CHUNKS)
    def _(ch):
        gather_wait(0, ch)
        more_rows(ch)
        gather_on(1, ch)

    lax.fori_loop(0, EARLY, other_grads, 0)

    wait_bytes(r.brecv.at[others], r.b_recv)
    back = r.brecv[...].reshape(PEERS * BLOCK, WIDTH // 2)
    for half in range(2):
        cols = slice(half * 512, half * 512 + 512)
        r.dres[:, cols] = (
            r.z_own[:, cols].astype(F32)
            + dot(r.pick[half * TOKENS : (half + 1) * TOKENS, :], back, 1, 0)
        ).astype(BF)
    my_rows = span(me_x, TOKENS)
    do_copies = []
    for o in range(1, EXP):
        px = lax.rem(me_x + o, EXP)
        do_copies.append(
            remote(
                r.dres.at[:, span(px, LOCAL)],
                r.do_all.at[my_rows],
                r.do_send.at[o - 1],
                r.do_recv.at[o - 1],
                {"exp": px},
            )
        )
    r.do_all[my_rows] = r.dres[:, span(me_x, LOCAL)]
    wait_bytes(r.hrecv.at[others], r.h_recv)
    sums = jnp.sum(r.hrecv[...], axis=1)
    lane_s = iota((TOKENS, 128), 1)
    for t in range(2):
        chosen = dot(named[t], sums, 1, 0, lax.Precision.HIGHEST)
        value = jnp.sum(jnp.where(lane_s == slot[t], chosen, 0.0), axis=1, keepdims=True)
        r.dgate[t : t + 1, :] = as_row(value / gates[t]).astype(BF)
    kv_copies[2].wait_recv()
    lax.fori_loop(EARLY, MIDDLE, other_grads, 0)
    for c in do_copies:
        c.wait_recv()

    def backward(b, carry):
        rows = span(b, QROWS)
        window = pl.ds(pl.multiple_of(b * QROWS, QROWS), WINDOW)
        for hp in range(2):
            tile = slice(hp * 128, hp * 128 + 128)
            do_t = r.do_all[rows, tile]
            v_t = r.v_all[window, tile]
            k_t = r.k_all[window, tile]
            all_p, all_s, all_d, all_q, dq = [], [], [], [], []
            for e in range(2):
                keep = low_q if e == 0 else jnp.logical_not(low_q)
                do_e = jnp.where(keep, do_t, none)
                probs = r.probs[2 * hp + e, rows]
                weight = probs.astype(F32)
                grad = dot(do_e, v_t, 1, 1)
                delta = jnp.sum(weight * grad, axis=1, keepdims=True)
                dscore = (weight * (grad - delta)).astype(BF)
                dq.append(dot(dscore, k_t, 1, 0))
                all_p.append(probs)
                all_s.append(dscore)
                all_d.append(do_e)
                all_q.append(jnp.where(keep, r.q_aug[2 * hp + e, rows], none))
            r.dq[rows, tile] = (jnp.where(low_q, dq[0], dq[1]) * 0.125).astype(BF)
            r.acc_k[window, tile] += dot(
                jnp.concatenate(all_s, axis=0), jnp.concatenate(all_q, axis=0), 0, 0
            )
            r.acc_v[window, tile] += dot(
                jnp.concatenate(all_p, axis=0), jnp.concatenate(all_d, axis=0), 0, 0
            )
        r.over[0, rows] = r.acc_k[rows].astype(BF)
        r.over[1, rows] = r.acc_v[rows].astype(BF)
        for i in range(2):
            give_prior(b, i).start()
        return carry

    def give_prior(b, i):
        rows = span(b, QROWS)
        return pltpu.make_async_remote_copy(
            src_ref=r.over.at[i, rows],
            dst_ref=r.came.at[i, rows],
            send_sem=r.ret_send.at[b, i],
            recv_sem=r.ret_recv.at[b, i],
            device_id={"ctx": prior},
            device_id_type=MESH,
        )

    lax.fori_loop(0, BLOCKS, backward, 0)
    lax.fori_loop(MIDDLE, CHUNKS, other_grads, 0)
    r.gin[...] = r.acc_in[...].astype(BF)
    r.gout[...] = r.acc_out[...].astype(BF)

    @pl.loop(0, BLOCKS)
    def _(b):
        rows = span(b, QROWS)
        late = pl.ds(pl.multiple_of(FRAMES + b * QROWS, QROWS), QROWS)
        for i, (out, acc) in enumerate(((r.dk, r.acc_k), (r.dv, r.acc_v))):
            give_prior(b, i).wait_recv()
            out[rows] = (acc[late] + r.came[i, rows].astype(F32)).astype(BF)
            give_prior(b, i).wait_send()

    for a in range(2):
        for ch in range(CHUNKS):
            for n in range(4):
                gather(a, ch, n).wait_send()
    for c in do_copies + kv_copies:
        c.wait_send()
    wait_bytes(r.send_s.at[others], r.s_send)
    wait_bytes(bsend.at[others], r.b_send)
    wait_bytes(r.hsend.at[others], r.h_send)


PIECES = [(name, rows) for name in ("gout", "gin") for rows in range(0, WIDTH, 256)] + [
    (name, None) for name in ("dres", "dq", "dk", "dv", "dgate")
]


def deliver_kernel(*refs):
    n = len(OUTPUTS)
    sources, targets = dict(zip(OUTPUTS, refs)), dict(zip(OUTPUTS, refs[n:]))
    buffers = dict(zip(OUTPUTS, refs[2 * n :]))
    get_sem, put_sem = refs[3 * n :]

    def view(ref, rows):
        return ref if rows is None else ref.at[pl.ds(rows, 256)]

    gets, puts = [], []
    for i, (name, rows) in enumerate(PIECES):
        source, buffer, target = (
            view(group[name], rows) for group in (sources, buffers, targets)
        )
        gets.append(pltpu.make_async_copy(source, buffer, get_sem.at[i]))
        puts.append(pltpu.make_async_copy(buffer, target, put_sem.at[i]))
    for get in gets:
        get.start()
    for get, put in zip(gets, puts):
        get.wait()
        put.start()
    for put in puts:
        put.wait()


def layer(*args):
    vmem = pl.BlockSpec(memory_space=pltpu.VMEM)
    anywhere = pl.BlockSpec(memory_space=pl.ANY)
    frames = jax.ShapeDtypeStruct((FRAMES, LOCAL), BF)
    weight = jax.ShapeDtypeStruct((WIDTH, WIDTH), BF)
    shapes = (
        frames,
        frames,
        frames,
        jax.ShapeDtypeStruct((TOKENS, WIDTH), BF),
        jax.ShapeDtypeStruct((2, TOKENS), BF),
        weight,
        weight,
    )
    results = pl.pallas_call(
        layer_kernel,
        out_shape=shapes,
        in_specs=[anywhere] * len(INPUTS),
        out_specs=(vmem,) * 7,
        scratch_shapes=list(SCRATCH.values()),
        compiler_params=pltpu.CompilerParams(
            collective_id=0, has_side_effects=True, vmem_limit_bytes=VMEM_BYTES
        ),
        name="layer",
    )(*args)
    return pl.pallas_call(
        deliver_kernel,
        out_shape=shapes,
        in_specs=[anywhere] * len(OUTPUTS),
        out_specs=(anywhere,) * len(OUTPUTS),
        scratch_shapes=[pltpu.VMEM(s.shape, s.dtype) for s in shapes]
        + [DMA((len(PIECES),)), DMA((len(PIECES),))],
        compiler_params=pltpu.CompilerParams(vmem_limit_bytes=VMEM_BYTES),
        name="deliver",
    )(*results)


def local(
    queries,
    key_rows,
    value_rows,
    segments,
    left_blocks,
    moe_input,
    out_grad,
    expert_ids,
    gate_weights,
    expert_in,
    expert_out,
):
    dq, dk, dv, d_residual, d_gates, grad_out, grad_in = layer(
        queries[0],
        key_rows[0],
        value_rows[0],
        segments,
        jnp.transpose(left_blocks, (2, 0, 1)),
        moe_input[0],
        out_grad[0],
        expert_ids[0].T,
        gate_weights[0].T,
        expert_in[0],
        expert_out[0],
    )
    return (
        dq[None],
        dk[None],
        dv[None],
        d_residual[None],
        d_gates.T[None],
        grad_in[None],
        grad_out[None],
    )


def solution(mesh):
    assert dict(mesh.shape) == {"dp": DP, "ctx": CTX, "exp": EXP}
    return jax.shard_map(
        local,
        mesh=mesh,
        in_specs=(
            P("dp", "ctx", "exp"),
            P("dp", "ctx", "exp"),
            P("dp", "ctx", "exp"),
            P("dp", "ctx"),
            P("dp", "ctx", None),
            P("dp", ("ctx", "exp"), None),
            P("dp", ("ctx", "exp"), None),
            P("dp", ("ctx", "exp"), None),
            P("dp", ("ctx", "exp"), None),
            P(("ctx", "exp"), None, None),
            P(("ctx", "exp"), None, None),
        ),
        out_specs=(
            P("dp", "ctx", "exp"),
            P("dp", "ctx", "exp"),
            P("dp", "ctx", "exp"),
            P("dp", ("ctx", "exp"), None),
            P("dp", ("ctx", "exp"), None),
            P(("ctx", "exp"), None, None),
            P(("ctx", "exp"), None, None),
        ),
        check_vma=False,
    )
```

```python
import types

import jax
import jax.numpy as jnp
from jax import lax
from jax.experimental import pallas as pl
from jax.experimental.pallas import tpu as pltpu
from jax.sharding import PartitionSpec as P

MESH = pl.DeviceIdType.MESH
BF = jnp.bfloat16
F32 = jnp.float32
I32 = jnp.int32

DP, CTX, EXP = 4, 16, 4
PEERS = CTX * EXP
HALF = CTX // 2
CAP = 8
BLOCK = 2 * CAP
TOKENS = 128
WIDTH = 1024
CHUNKS = 4
PER_CHUNK = PEERS // CHUNKS
CHUNK_ROWS = PER_CHUNK * CAP
ROWS = PEERS * CAP
OTHERS = DP - 1
OTHER_ROWS = OTHERS * CHUNK_ROWS
STEPS = PER_CHUNK // EXP
EARLY, MIDDLE = 2, 3
GROUP = 64
GROUPS = 8
FRAMES = 512
LOCAL = 256
QROWS = 128
BLOCKS = FRAMES // QROWS
WINDOW = FRAMES + QROWS
FAR = 32768.0
VMEM_BYTES = 63 * 1024 * 1024


def dot(a, b, ca, cb, precision=None):
    return lax.dot_general(
        a, b, (((ca,), (cb,)), ((), ())), preferred_element_type=F32, precision=precision
    )


def wait_bytes(ref, sem):
    pltpu.make_async_copy(ref, ref, sem).wait()


def span(index, size):
    return pl.ds(pl.multiple_of(index * size, size), size)


def hop(j):
    s = j // EXP
    return HALF + (2 * (s % 2) - 1) * (s // 2), j % EXP


def iota(shape, dim):
    return lax.broadcasted_iota(I32, shape, dim)


def column(row):
    n = row.shape[1]
    same = iota((n, n), 0) == iota((n, n), 1)
    return jnp.sum(jnp.where(same, row, jnp.zeros_like(row)), axis=1, keepdims=True)


def as_row(col):
    n = col.shape[0]
    same = iota((n, n), 0) == iota((n, n), 1)
    return jnp.sum(jnp.where(same, col, jnp.zeros_like(col)), axis=0, keepdims=True)


INPUTS = ("q", "k", "v", "seg", "lists", "x", "z", "ids", "gate", "win", "wout")
OUTPUTS = ("dq", "dk", "dv", "dres", "dgate", "gout", "gin")
DMA = pltpu.SemaphoreType.DMA
LOADS = ("ids", "gate", "x", "z", "win", "wout", "q", "seg", "lists", "k", "v")
SCRATCH = dict(
    q_own=pltpu.VMEM((FRAMES, LOCAL), BF),
    seg_own=pltpu.VMEM((1, FRAMES), I32),
    lists_own=pltpu.VMEM((3, 1, GROUPS), I32),
    x_own=pltpu.VMEM((TOKENS, WIDTH), BF),
    z_own=pltpu.VMEM((TOKENS, WIDTH), BF),
    ids_own=pltpu.VMEM((2, TOKENS), I32),
    gate_own=pltpu.VMEM((2, TOKENS), BF),
    w_in=pltpu.VMEM((WIDTH, WIDTH), BF),
    w_out=pltpu.VMEM((WIDTH, WIDTH), BF),
    pick_t=pltpu.VMEM((PEERS * BLOCK, 2 * TOKENS), BF),
    gated_t=pltpu.VMEM((PEERS * BLOCK, 2 * TOKENS), BF),
    pick=pltpu.VMEM((2 * TOKENS, PEERS * BLOCK), BF),
    xx=pltpu.VMEM((2 * TOKENS, WIDTH // 2), BF),
    zz=pltpu.VMEM((2 * TOKENS, WIDTH // 2), BF),
    send_u=pltpu.VMEM((PEERS, BLOCK, WIDTH // 2), BF),
    recv_u=pltpu.VMEM((PEERS, BLOCK, WIDTH // 2), BF),
    send_s=pltpu.VMEM((PEERS, BLOCK, WIDTH // 2), BF),
    recv_s=pltpu.VMEM((PEERS, BLOCK, WIDTH // 2), BF),
    gath=pltpu.VMEM((2, OTHERS, PEERS, BLOCK, WIDTH // 2), BF),
    more=pltpu.VMEM((OTHER_ROWS, WIDTH), BF),
    more_gp=pltpu.VMEM((OTHER_ROWS, WIDTH), BF),
    more_u_t=pltpu.VMEM((CHUNKS, WIDTH, OTHER_ROWS), BF),
    more_act_t=pltpu.VMEM((CHUNKS, WIDTH, OTHER_ROWS), BF),
    more_pre=pltpu.VMEM((CHUNKS, OTHER_ROWS, WIDTH), BF),
    acc_in=pltpu.VMEM((WIDTH, WIDTH), F32),
    acc_out=pltpu.VMEM((WIDTH, WIDTH), F32),
    u_chunk=pltpu.VMEM((CHUNK_ROWS, WIDTH), BF),
    u_t=pltpu.VMEM((WIDTH, ROWS), BF),
    act_t=pltpu.VMEM((WIDTH, ROWS), BF),
    pre_all=pltpu.VMEM((ROWS, WIDTH), F32),
    s_all=pltpu.VMEM((ROWS, WIDTH), BF),
    gp_all=pltpu.VMEM((ROWS, WIDTH), BF),
    brecv=pltpu.VMEM((PEERS, BLOCK, WIDTH // 2), BF),
    hsend=pltpu.VMEM((PEERS, 1, 128), F32),
    hrecv=pltpu.VMEM((PEERS, 1, 128), F32),
    k_all=pltpu.VMEM((2 * FRAMES, LOCAL), BF),
    v_all=pltpu.VMEM((2 * FRAMES, LOCAL), BF),
    seg_prev=pltpu.VMEM((1, FRAMES), I32),
    do_all=pltpu.VMEM((FRAMES, LOCAL), BF),
    k_aug=pltpu.VMEM((4, 2 * FRAMES, 128), BF),
    q_aug=pltpu.VMEM((4, FRAMES, 128), BF),
    probs=pltpu.VMEM((4, FRAMES, WINDOW), BF),
    acc_k=pltpu.VMEM((2 * FRAMES, LOCAL), F32),
    acc_v=pltpu.VMEM((2 * FRAMES, LOCAL), F32),
    over=pltpu.VMEM((2, FRAMES, LOCAL), BF),
    came=pltpu.VMEM((2, FRAMES, LOCAL), BF),
    load_sem=DMA((len(LOADS),)),
    u_send=DMA,
    u_recv=DMA((CTX,)),
    s_send=DMA,
    s_recv=DMA((CTX,)),
    b_send=DMA,
    b_recv=DMA,
    h_send=DMA,
    h_recv=DMA,
    ag_send=DMA((2, CHUNKS, 4)),
    ag_recv=DMA((2, CHUNKS, 4)),
    kv_send=DMA((3,)),
    kv_recv=DMA((3,)),
    do_send=DMA((EXP - 1,)),
    do_recv=DMA((EXP - 1,)),
    ret_send=DMA((BLOCKS, 2)),
    ret_recv=DMA((BLOCKS, 2)),
)


def layer_kernel(*refs):
    r = types.SimpleNamespace(**dict(zip(INPUTS + OUTPUTS + tuple(SCRATCH), refs)))
    me_d, me_c, me_x = lax.axis_index("dp"), lax.axis_index("ctx"), lax.axis_index("exp")
    right, left = lax.rem(me_d + 1, DP), lax.rem(me_d + DP - 1, DP)
    after, prior = lax.rem(me_c + 1, CTX), lax.rem(me_c + CTX - 1, CTX)

    targets = dict(
        ids=r.ids_own,
        gate=r.gate_own,
        x=r.x_own,
        z=r.z_own,
        win=r.w_in,
        wout=r.w_out,
        q=r.q_own,
        seg=r.seg_own,
        lists=r.lists_own,
        k=r.k_all.at[pl.ds(FRAMES, FRAMES)],
        v=r.v_all.at[pl.ds(FRAMES, FRAMES)],
    )
    loads = {
        name: pltpu.make_async_copy(getattr(r, name), targets[name], r.load_sem.at[i])
        for i, name in enumerate(LOADS)
    }
    def ahead(k, xo):
        return {"ctx": lax.rem(me_c + k, CTX), "exp": lax.rem(me_x + xo, EXP)}

    def behind(k, xo):
        return {"ctx": lax.rem(me_c - k + CTX, CTX), "exp": lax.rem(me_x - xo + EXP, EXP)}

    def remote(src, dst, ssem, rsem, target):
        copy = pltpu.make_async_remote_copy(
            src_ref=src,
            dst_ref=dst,
            send_sem=ssem,
            recv_sem=rsem,
            device_id=target,
            device_id_type=MESH,
        )
        copy.start()
        return copy

    barrier = pltpu.get_barrier_semaphore()
    for name in LOADS[:4]:
        loads[name].start()
    columns_of = [lax.rem(me_c + k, CTX) for k in range(CTX)]
    rows_of = [lax.rem(me_x + xo, EXP) for xo in range(EXP)]
    for other in (left, right):
        pl.semaphore_signal(barrier, inc=1, device_id={"dp": other}, device_id_type=MESH)
    for k in range(CTX):
        for xo in range(EXP):
            if k or xo:
                pl.semaphore_signal(
                    barrier,
                    inc=1,
                    device_id={"ctx": columns_of[k], "exp": rows_of[xo]},
                    device_id_type=MESH,
                )
    for name in LOADS[4:]:
        loads[name].start()

    def relative(ids):
        k = (ids // EXP - me_c + CTX) % CTX
        xo = (ids % EXP - me_x + EXP) % EXP
        s = jnp.where(k == 0, 0, jnp.where(k < HALF, CTX - 2 * k, 2 * k - CTX + 1))
        return s * EXP + xo

    loads["ids"].wait()
    expert = iota((PEERS, TOKENS), 0)
    peer_row = [relative(r.ids_own[t : t + 1, :]) for t in range(2)]
    named_t = [(peer_row[t] == expert).astype(F32) for t in range(2)]
    before = (iota((TOKENS, TOKENS), 0) < iota((TOKENS, TOKENS), 1)).astype(F32).astype(BF)
    earlier = dot((named_t[0] + named_t[1]).astype(BF), before, 1, 0)
    slot_row = [
        jnp.sum(named_t[t] * earlier, axis=0, keepdims=True).astype(I32) for t in range(2)
    ]
    place_row = [peer_row[t] * BLOCK + slot_row[t] for t in range(2)]
    loads["gate"].wait()
    gate_row = [r.gate_own[t : t + 1, :].astype(F32) for t in range(2)]
    loads["x"].wait()
    r.xx[:TOKENS] = r.x_own[:, : WIDTH // 2]
    r.xx[TOKENS:] = r.x_own[:, WIDTH // 2 :]

    @pl.loop(0, CHUNKS)
    def _(t):
        place = iota((256, TOKENS), 0) + t * 256
        for half in range(2):
            hit = [place_row[i] + half * CAP == place for i in range(2)]
            cols = slice(half * TOKENS, half * TOKENS + TOKENS)
            r.pick_t[span(t, 256), cols] = (hit[0] | hit[1]).astype(F32).astype(BF)
            r.gated_t[span(t, 256), cols] = (
                jnp.where(hit[0], gate_row[0], 0.0) + jnp.where(hit[1], gate_row[1], 0.0)
            ).astype(BF)
        rows = dot(r.pick_t[span(t, 256)], r.xx[...], 1, 0)
        r.send_u[pl.ds(t * 16, 16)] = rows.astype(BF).reshape(16, BLOCK, WIDTH // 2)

    pl.semaphore_wait(barrier, PEERS - 1 + 2)

    def send_rows(j, k, xo):
        remote(r.send_u.at[j], r.recv_u.at[j], r.u_send, r.u_recv.at[j // EXP], ahead(k, xo))

    @pl.loop(EXP, PEERS)
    def _(j):
        send_rows(j, *hop(j))

    for j in range(1, EXP):
        send_rows(j, 0, j)
    r.recv_u[0] = r.send_u[0]

    loads["z"].wait()
    r.zz[:TOKENS] = r.z_own[:, : WIDTH // 2]
    r.zz[TOKENS:] = r.z_own[:, WIDTH // 2 :]

    @pl.loop(0, CHUNKS)
    def _(t):
        rows = dot(r.gated_t[span(t, 256)], r.zz[...], 1, 0)
        r.send_s[pl.ds(t * 16, 16)] = rows.astype(BF).reshape(16, BLOCK, WIDTH // 2)

    def send_grads(j, k, xo):
        remote(r.send_s.at[j], r.recv_s.at[j], r.s_send, r.s_recv.at[j // EXP], ahead(k, xo))

    @pl.loop(EXP, PEERS)
    def _(j):
        send_grads(j, *hop(j))

    for j in range(1, EXP):
        send_grads(j, 0, j)
    r.recv_s[0] = r.send_s[0]

    past = pl.ds(0, FRAMES)
    for name in ("seg", "k", "v"):
        loads[name].wait()
    kv_copies = [
        remote(r.seg_own, r.seg_prev, r.kv_send.at[0], r.kv_recv.at[0], {"ctx": after}),
        remote(r.k_all.at[pl.ds(FRAMES, FRAMES)], r.k_all.at[past], r.kv_send.at[1], r.kv_recv.at[1], {"ctx": after}),
        remote(r.v_all.at[pl.ds(FRAMES, FRAMES)], r.v_all.at[past], r.kv_send.at[2], r.kv_recv.at[2], {"ctx": after}),
    ]

    peer = [column(peer_row[t]) for t in range(2)]
    slot = [column(slot_row[t]) for t in range(2)]
    gates = [column(gate_row[t]) for t in range(2)]
    named = [(peer[t] == iota((TOKENS, PEERS), 1)).astype(F32) for t in range(2)]
    lane_q = iota((TOKENS, PEERS * BLOCK), 1)
    for half in range(2):
        hit = [peer[t] * BLOCK + slot[t] + half * CAP == lane_q for t in range(2)]
        r.pick[pl.ds(half * TOKENS, TOKENS)] = (hit[0] | hit[1]).astype(F32).astype(BF)

    for name in ("q", "lists"):
        loads[name].wait()
    kinds = 2 * GROUPS
    lane_f, row_f = iota((kinds, 128), 1), iota((kinds, 128), 0)
    place = ((lane_f == row_f) | (lane_f == row_f + 64)).astype(F32).astype(BF)
    row8 = iota((8, FRAMES), 0)
    group_of = iota((8, FRAMES), 1) // GROUP
    moved = []
    for j in range(3):
        lists = column(r.lists_own[j])
        moved.append(jnp.where(lists >= 0, lists - (me_c - 1) * GROUPS, -1))

    def listed(groups):
        return (moved[0] == groups) | (moved[1] == groups) | (moved[2] == groups)

    def features(segment, group, miss, match):
        both = jnp.concatenate(
            [jnp.where(segment, match, miss), jnp.where(group, match, miss)], axis=0
        ).astype(BF)
        return dot(both, place, 0, 0).astype(BF)

    low = iota((FRAMES, 128), 1) < 64
    low_q = iota((QROWS, 128), 1) < 64
    none = jnp.zeros((QROWS, 128), BF)

    def augment(part, feat):
        for hp in range(2):
            k_t = r.k_all[part, hp * 128 : hp * 128 + 128]
            r.k_aug[2 * hp, part] = jnp.where(low, k_t, feat)
            r.k_aug[2 * hp + 1, part] = jnp.where(low, feat, k_t)

    seg_own = r.seg_own[...] == row8
    feat_q = features(seg_own, group_of == row8, 0.0, 1.0)
    for hp in range(2):
        q_t = (r.q_own[:, hp * 128 : hp * 128 + 128].astype(F32) * 0.125).astype(BF)
        r.q_aug[2 * hp] = jnp.where(low, q_t, feat_q)
        r.q_aug[2 * hp + 1] = jnp.where(low, feat_q, q_t)
    list_own = listed(group_of + GROUPS) | (group_of == row8)
    augment(pl.ds(FRAMES, FRAMES), features(seg_own, list_own, -FAR, 0.0))
    r.acc_k[...] = jnp.zeros_like(r.acc_k)
    r.acc_v[...] = jnp.zeros_like(r.acc_v)

    ours = (r.recv_u, r.recv_s)

    def gather(a, ch, n):
        chunk = pl.ds(ch * PER_CHUNK, PER_CHUNK)
        near = pl.ds(ch * PER_CHUNK, PER_CHUNK // 2)
        far = pl.ds(ch * PER_CHUNK + PER_CHUNK // 2, PER_CHUNK // 2)
        src, dst, other = (
            (ours[a].at[chunk], r.gath.at[a, 0, chunk], right),
            (ours[a].at[chunk], r.gath.at[a, 1, chunk], left),
            (r.gath.at[a, 0, near], r.gath.at[a, 2, near], right),
            (r.gath.at[a, 1, far], r.gath.at[a, 2, far], left),
        )[n]
        return pltpu.make_async_remote_copy(
            src_ref=src,
            dst_ref=dst,
            send_sem=r.ag_send.at[a, ch, n],
            recv_sem=r.ag_recv.at[a, ch, n],
            device_id={"dp": other},
            device_id_type=MESH,
        )

    def gather_own(a, ch):
        gather(a, ch, 0).start()
        gather(a, ch, 1).start()

    def gather_on(a, ch):
        gather(a, ch, 0).wait_recv()
        gather(a, ch, 2).start()
        gather(a, ch, 1).wait_recv()
        gather(a, ch, 3).start()

    def gather_wait(a, ch):
        gather(a, ch, 2).wait_recv()
        gather(a, ch, 3).wait_recv()

    def wait_chunk(buffer, sems, ch):
        @pl.when(ch == 0)
        def _():
            wait_bytes(buffer.at[pl.ds(1, EXP - 1)], sems.at[0])

        @pl.when(ch > 0)
        def _():
            wait_bytes(buffer.at[pl.ds(ch * PER_CHUNK, EXP)], sems.at[ch * STEPS])

        for i in range(1, STEPS):
            wait_bytes(buffer.at[pl.ds(ch * PER_CHUNK + i * EXP, EXP)], sems.at[ch * STEPS + i])

    def unpack(blocks):
        came = blocks.astype(F32)
        count = came.shape[0] * CAP
        return [
            came[:, half * CAP : half * CAP + CAP].reshape(count, WIDTH // 2) for half in range(2)
        ]

    def half_cols(half):
        return slice(half * 512, half * 512 + 512)

    def chunk_of_others(a, ch):
        blocks = r.gath[a, :, pl.ds(ch * PER_CHUNK, PER_CHUNK)]
        return blocks.reshape(OTHERS * PER_CHUNK, BLOCK, WIDTH // 2)

    def more_rows(ch):
        for half, u in enumerate(unpack(chunk_of_others(0, ch))):
            r.more[:, half_cols(half)] = u.astype(BF)
            r.more_u_t[ch, half_cols(half)] = u.T.astype(BF)

        @pl.loop(0, WIDTH // 256)
        def _(t):
            cols = span(t, 256)
            pre = dot(r.more[...], r.w_in[:, cols], 1, 0)
            r.more_pre[ch, :, cols] = pre.astype(BF)
            r.more_act_t[ch, cols] = (pre * jax.nn.sigmoid(pre)).T.astype(BF)

    def more_grads(ch):
        for half, s in enumerate(unpack(chunk_of_others(1, ch))):
            r.more[:, half_cols(half)] = s.astype(BF)

        @pl.loop(0, WIDTH // 256)
        def _(t):
            cols = span(t, 256)
            grad = dot(r.more[...], r.w_out[cols, :], 1, 1)
            pre = r.more_pre[ch, :, cols].astype(F32)
            sigma = jax.nn.sigmoid(pre)
            r.more_gp[:, cols] = (grad * sigma * (1.0 + pre * (1.0 - sigma))).astype(BF)

        @pl.loop(0, WIDTH // 256)
        def _(t):
            rows = span(t, 256)
            r.acc_in[rows] += dot(r.more_u_t[ch, rows], r.more_gp[...], 1, 0)
            r.acc_out[rows] += dot(r.more_act_t[ch, rows], r.more[...], 1, 0)

    def softmax(b):
        rows = span(b, QROWS)
        window = pl.ds(pl.multiple_of(b * QROWS, QROWS), WINDOW)
        for h in range(4):
            score = dot(r.q_aug[h, rows], r.k_aug[h, window], 1, 1)
            weight = jnp.exp(score - jnp.max(score, axis=1, keepdims=True))
            r.probs[h, rows] = (
                weight * (1.0 / jnp.sum(weight, axis=1, keepdims=True))
            ).astype(BF)

    loads["win"].wait()
    loads["wout"].wait()

    @pl.loop(0, CHUNKS)
    def _(ch):
        wait_chunk(r.recv_u, r.u_recv, ch)
        gather_own(0, ch)
        rows = span(ch, CHUNK_ROWS)
        for half, u in enumerate(unpack(r.recv_u[pl.ds(ch * PER_CHUNK, PER_CHUNK)])):
            r.u_chunk[:, half_cols(half)] = u.astype(BF)
            r.u_t[half_cols(half), rows] = u.T.astype(BF)

        @pl.loop(0, WIDTH // 256)
        def _(t):
            cols = span(t, 256)
            pre = dot(r.u_chunk[...], r.w_in[:, cols], 1, 0)
            r.pre_all[rows, cols] = pre
            r.act_t[cols, rows] = (pre * jax.nn.sigmoid(pre)).T.astype(BF)

    others = pl.ds(1, PEERS - 1)
    wait_bytes(r.send_u.at[others], r.u_send)
    bsend = r.send_u
    lane128 = iota((CHUNK_ROWS, 128), 1)
    slot128 = iota((CHUNK_ROWS, 128), 0) % CAP

    def give_back(j, k, xo):
        remote(bsend.at[j], r.brecv.at[j], r.b_send, r.b_recv, behind(k, xo))
        remote(r.hsend.at[j], r.hrecv.at[j], r.h_send, r.h_recv, behind(k, xo))

    @pl.loop(0, CHUNKS)
    def _(ch):
        base = ch * PER_CHUNK
        rows = span(ch, CHUNK_ROWS)
        peers = pl.ds(base, PER_CHUNK)
        wait_chunk(r.recv_s, r.s_recv, ch)
        gather_own(1, ch)
        for half, s in enumerate(unpack(r.recv_s[peers])):
            r.s_all[rows, half_cols(half)] = s.astype(BF)

        def hidden(t, total):
            cols = span(t, 256)
            grad = dot(r.s_all[rows], r.w_out[cols, :], 1, 1)
            pre = r.pre_all[rows, cols]
            sigma = jax.nn.sigmoid(pre)
            r.gp_all[rows, cols] = (grad * sigma * (1.0 + pre * (1.0 - sigma))).astype(BF)
            return total + jnp.sum(pre * sigma * grad, axis=1, keepdims=True)

        total = lax.fori_loop(0, WIDTH // 256, hidden, jnp.zeros((CHUNK_ROWS, 1), F32))
        spread = jnp.where(lane128 == slot128, total, 0.0)
        r.hsend[peers] = jnp.sum(spread.reshape(PER_CHUNK, CAP, 128), axis=1, keepdims=True)

        @pl.loop(0, 2)
        def _(t):
            lo, hi = span(t, 256), span(t + 2, 256)
            first = dot(r.gp_all[rows], r.w_in[lo, :], 1, 1).reshape(PER_CHUNK, CAP, 256)
            last = dot(r.gp_all[rows], r.w_in[hi, :], 1, 1).reshape(PER_CHUNK, CAP, 256)
            bsend[peers, :, lo] = jnp.concatenate([first, last], axis=1).astype(BF)

        @pl.when(ch == 0)
        def _():
            r.brecv[0] = bsend[0]
            r.hrecv[0] = r.hsend[0]
            for j in range(1, EXP):
                give_back(j, 0, j)

        @pl.when(ch > 0)
        def _():
            for i in range(EXP):
                give_back(base + i, *hop(base + i))

        @pl.loop(EXP, PER_CHUNK)
        def _(i):
            give_back(base + i, *hop(base + i))

        @pl.when(ch > 0)
        def _():
            gather_on(0, ch - 1)

    @pl.loop(0, WIDTH // 256)
    def _(t):
        rows = span(t, 256)
        r.acc_in[rows] = dot(r.u_t[rows], r.gp_all[...], 1, 0)
        r.acc_out[rows] = dot(r.act_t[rows], r.s_all[...], 1, 0)

    def other_grads(ch, carry):
        gather_wait(1, ch)
        more_grads(ch)
        return carry

    kv_copies[0].wait_recv()
    kv_copies[1].wait_recv()
    seg_past = r.seg_prev[...] == row8
    augment(past, features(seg_past, listed(group_of), -FAR, 0.0))

    @pl.loop(0, BLOCKS)
    def _(b):
        softmax(b)

    gather_on(0, CHUNKS - 1)

    @pl.loop(0, CHUNKS)
    def _(ch):
        gather_on(1, ch)
        gather_wait(0, ch)
        more_rows(ch)

    lax.fori_loop(0, EARLY, other_grads, 0)

    wait_bytes(r.brecv.at[others], r.b_recv)
    back = r.brecv[...].reshape(PEERS * BLOCK, WIDTH // 2)
    for half in range(2):
        cols = slice(half * 512, half * 512 + 512)
        r.dres[:, cols] = (
            r.z_own[:, cols].astype(F32)
            + dot(r.pick[half * TOKENS : (half + 1) * TOKENS, :], back, 1, 0)
        ).astype(BF)
    my_rows = span(me_x, TOKENS)
    do_copies = []
    for o in range(1, EXP):
        px = lax.rem(me_x + o, EXP)
        do_copies.append(
            remote(
                r.dres.at[:, span(px, LOCAL)],
                r.do_all.at[my_rows],
                r.do_send.at[o - 1],
                r.do_recv.at[o - 1],
                {"exp": px},
            )
        )
    r.do_all[my_rows] = r.dres[:, span(me_x, LOCAL)]
    wait_bytes(r.hrecv.at[others], r.h_recv)
    sums = jnp.sum(r.hrecv[...], axis=1)
    lane_s = iota((TOKENS, 128), 1)
    for t in range(2):
        chosen = dot(named[t], sums, 1, 0, lax.Precision.HIGHEST)
        value = jnp.sum(jnp.where(lane_s == slot[t], chosen, 0.0), axis=1, keepdims=True)
        r.dgate[t : t + 1, :] = as_row(value / gates[t]).astype(BF)
    kv_copies[2].wait_recv()
    lax.fori_loop(EARLY, MIDDLE, other_grads, 0)
    for c in do_copies:
        c.wait_recv()

    def backward(b, carry):
        rows = span(b, QROWS)
        window = pl.ds(pl.multiple_of(b * QROWS, QROWS), WINDOW)
        for hp in range(2):
            tile = slice(hp * 128, hp * 128 + 128)
            do_t = r.do_all[rows, tile]
            v_t = r.v_all[window, tile]
            k_t = r.k_all[window, tile]
            all_p, all_s, all_d, all_q, dq = [], [], [], [], []
            for e in range(2):
                keep = low_q if e == 0 else jnp.logical_not(low_q)
                do_e = jnp.where(keep, do_t, none)
                probs = r.probs[2 * hp + e, rows]
                weight = probs.astype(F32)
                grad = dot(do_e, v_t, 1, 1)
                delta = jnp.sum(weight * grad, axis=1, keepdims=True)
                dscore = (weight * (grad - delta)).astype(BF)
                dq.append(dot(dscore, k_t, 1, 0))
                all_p.append(probs)
                all_s.append(dscore)
                all_d.append(do_e)
                all_q.append(jnp.where(keep, r.q_aug[2 * hp + e, rows], none))
            r.dq[rows, tile] = (jnp.where(low_q, dq[0], dq[1]) * 0.125).astype(BF)
            r.acc_k[window, tile] += dot(
                jnp.concatenate(all_s, axis=0), jnp.concatenate(all_q, axis=0), 0, 0
            )
            r.acc_v[window, tile] += dot(
                jnp.concatenate(all_p, axis=0), jnp.concatenate(all_d, axis=0), 0, 0
            )
        r.over[0, rows] = r.acc_k[rows].astype(BF)
        r.over[1, rows] = r.acc_v[rows].astype(BF)
        for i in range(2):
            give_prior(b, i).start()
        return carry

    def give_prior(b, i):
        rows = span(b, QROWS)
        return pltpu.make_async_remote_copy(
            src_ref=r.over.at[i, rows],
            dst_ref=r.came.at[i, rows],
            send_sem=r.ret_send.at[b, i],
            recv_sem=r.ret_recv.at[b, i],
            device_id={"ctx": prior},
            device_id_type=MESH,
        )

    lax.fori_loop(0, BLOCKS, backward, 0)
    lax.fori_loop(MIDDLE, CHUNKS, other_grads, 0)
    r.gin[...] = r.acc_in[...].astype(BF)
    r.gout[...] = r.acc_out[...].astype(BF)

    @pl.loop(0, BLOCKS)
    def _(b):
        rows = span(b, QROWS)
        late = pl.ds(pl.multiple_of(FRAMES + b * QROWS, QROWS), QROWS)
        for i, (out, acc) in enumerate(((r.dk, r.acc_k), (r.dv, r.acc_v))):
            give_prior(b, i).wait_recv()
            out[rows] = (acc[late] + r.came[i, rows].astype(F32)).astype(BF)
            give_prior(b, i).wait_send()

    for a in range(2):
        for ch in range(CHUNKS):
            for n in range(4):
                gather(a, ch, n).wait_send()
    for c in do_copies + kv_copies:
        c.wait_send()
    wait_bytes(r.send_s.at[others], r.s_send)
    wait_bytes(bsend.at[others], r.b_send)
    wait_bytes(r.hsend.at[others], r.h_send)


PIECES = [(name, rows) for name in ("gout", "gin") for rows in range(0, WIDTH, 256)] + [
    (name, None) for name in ("dres", "dq", "dk", "dv", "dgate")
]


def deliver_kernel(*refs):
    n = len(OUTPUTS)
    sources, targets = dict(zip(OUTPUTS, refs)), dict(zip(OUTPUTS, refs[n:]))
    buffers = dict(zip(OUTPUTS, refs[2 * n :]))
    get_sem, put_sem = refs[3 * n :]

    def view(ref, rows):
        return ref if rows is None else ref.at[pl.ds(rows, 256)]

    gets, puts = [], []
    for i, (name, rows) in enumerate(PIECES):
        source, buffer, target = (
            view(group[name], rows) for group in (sources, buffers, targets)
        )
        gets.append(pltpu.make_async_copy(source, buffer, get_sem.at[i]))
        puts.append(pltpu.make_async_copy(buffer, target, put_sem.at[i]))
    for get in gets:
        get.start()
    for get, put in zip(gets, puts):
        get.wait()
        put.start()
    for put in puts:
        put.wait()


def layer(*args):
    vmem = pl.BlockSpec(memory_space=pltpu.VMEM)
    anywhere = pl.BlockSpec(memory_space=pl.ANY)
    frames = jax.ShapeDtypeStruct((FRAMES, LOCAL), BF)
    weight = jax.ShapeDtypeStruct((WIDTH, WIDTH), BF)
    shapes = (
        frames,
        frames,
        frames,
        jax.ShapeDtypeStruct((TOKENS, WIDTH), BF),
        jax.ShapeDtypeStruct((2, TOKENS), BF),
        weight,
        weight,
    )
    results = pl.pallas_call(
        layer_kernel,
        out_shape=shapes,
        in_specs=[anywhere] * len(INPUTS),
        out_specs=(vmem,) * 7,
        scratch_shapes=list(SCRATCH.values()),
        compiler_params=pltpu.CompilerParams(
            collective_id=0, has_side_effects=True, vmem_limit_bytes=VMEM_BYTES
        ),
        name="layer",
    )(*args)
    return pl.pallas_call(
        deliver_kernel,
        out_shape=shapes,
        in_specs=[anywhere] * len(OUTPUTS),
        out_specs=(anywhere,) * len(OUTPUTS),
        scratch_shapes=[pltpu.VMEM(s.shape, s.dtype) for s in shapes]
        + [DMA((len(PIECES),)), DMA((len(PIECES),))],
        compiler_params=pltpu.CompilerParams(vmem_limit_bytes=VMEM_BYTES),
        name="deliver",
    )(*results)


def local(
    queries,
    key_rows,
    value_rows,
    segments,
    left_blocks,
    moe_input,
    out_grad,
    expert_ids,
    gate_weights,
    expert_in,
    expert_out,
):
    dq, dk, dv, d_residual, d_gates, grad_out, grad_in = layer(
        queries[0],
        key_rows[0],
        value_rows[0],
        segments,
        jnp.transpose(left_blocks, (2, 0, 1)),
        moe_input[0],
        out_grad[0],
        expert_ids[0].T,
        gate_weights[0].T,
        expert_in[0],
        expert_out[0],
    )
    return (
        dq[None],
        dk[None],
        dv[None],
        d_residual[None],
        d_gates.T[None],
        grad_in[None],
        grad_out[None],
    )


def solution(mesh):
    assert dict(mesh.shape) == {"dp": DP, "ctx": CTX, "exp": EXP}
    return jax.shard_map(
        local,
        mesh=mesh,
        in_specs=(
            P("dp", "ctx", "exp"),
            P("dp", "ctx", "exp"),
            P("dp", "ctx", "exp"),
            P("dp", "ctx"),
            P("dp", "ctx", None),
            P("dp", ("ctx", "exp"), None),
            P("dp", ("ctx", "exp"), None),
            P("dp", ("ctx", "exp"), None),
            P("dp", ("ctx", "exp"), None),
            P(("ctx", "exp"), None, None),
            P(("ctx", "exp"), None, None),
        ),
        out_specs=(
            P("dp", "ctx", "exp"),
            P("dp", "ctx", "exp"),
            P("dp", "ctx", "exp"),
            P("dp", ("ctx", "exp"), None),
            P("dp", ("ctx", "exp"), None),
            P(("ctx", "exp"), None, None),
            P(("ctx", "exp"), None, None),
        ),
        check_vma=False,
    )
```
